128 devices in a mesh: shot: 8 (over x_lo, y), apert: 16 (over z, x_hi, core).
Axes of the slice: x: 4 (x_hi: 2, x_lo: 2; x = x_hi * 2 + x_lo), y: 4, z: 4, core: 2. Of those that a mesh axis runs over, the one named last changes fastest.
Arguments:
- forward_prev: float32 [8, 128, 160, 256], P('shot', 'apert'), may hold values from -0.5 to 2.5
- forward_now: float32 [8, 128, 160, 256], P('shot', 'apert'), may hold values from -0.5 to 2.5
- adjoint_prev: float32 [8, 128, 160, 256], P('shot', 'apert'), may hold values from -0.5 to 2.5
- adjoint_now: float32 [8, 128, 160, 256], P('shot', 'apert'), may hold values from -0.5 to 2.5
- velocity: bfloat16 [128, 512, 256], P('apert', 'shot'), may hold values from 0.19921875 to 0.41992188
- density: bfloat16 [128, 512, 256], P('apert', 'shot'), may hold values from 1 to 2.5
- anchors: int32 [8], P('shot'), may hold values from 0 to 352
- shot_cell: int32 [8], P('shot'), may hold values from 0 to 5242879
- wavelet: float32 [8, 6], P('shot'), may hold values from -24 to 24
- records: float32 [8, 6, 128, 160], P('shot', None, 'apert'), may hold values from -6 to 6
Outputs:
- image: float32 [128, 512, 256], P('apert', 'shot')
- adjoint_state: float32 [8, 128, 160, 256], P('shot', 'apert')
The draws below stay inside these ranges and needn't reach their ends.
All inputs are finite; a program needn't handle non-finite values.
Results may differ from the reference program's by a relative error of at most 0.0004.
Values may be sent and summed in bfloat16 or wider, within the bound.
No kernel may reach another device: no remote copies, remote signals or barrier semaphores. Data moves between devices by JAX's collectives and lax.ppermute only.
A program may use at most 256 MiB of HBM per device.

```python
import math
import jax
import jax.numpy as jnp
from jax import lax

AY = 160
AZ = 256
PY_DEV = 64
STEPS = 6
SURF = 8
NGROUPS = 8
AX = 128
MY = 512
N_SHOT = 8


def wave_shape():
    return (NGROUPS, AX, AY, AZ)


def settle_field(noise, center, spread):
    return (center + spread * noise).astype(jnp.float32)


def draw_forward_prev(key, part):
    key = jax.random.fold_in(key, 11)
    return settle_field(jnp.clip(jax.random.normal(key, wave_shape(), jnp.float32), -3.0, 3.0), 1.0, 0.5)


def draw_forward_now(key, part):
    key = jax.random.fold_in(key, 12)
    return settle_field(jnp.clip(jax.random.normal(key, wave_shape(), jnp.float32), -3.0, 3.0), 1.0, 0.5)


def draw_adjoint_prev(key, part):
    key = jax.random.fold_in(key, 13)
    return settle_field(jnp.clip(jax.random.normal(key, wave_shape(), jnp.float32), -3.0, 3.0), 1.0, 0.5)


def draw_adjoint_now(key, part):
    key = jax.random.fold_in(key, 14)
    return settle_field(jnp.clip(jax.random.normal(key, wave_shape(), jnp.float32), -3.0, 3.0), 1.0, 0.5)


def place_ends(array, rng, low, high):
    longest = array.shape.index(max(array.shape))
    spots = []
    for shift in (0, 1):
        where = [jax.random.randint(jax.random.fold_in(rng, axis), (), 0, length) for axis, length in enumerate(array.shape)]
        where[longest] = (where[longest] + shift) % array.shape[longest]
        spots.append(tuple(where))
    return array.at[spots[0]].set(low).at[spots[1]].set(high)


def steps_of(own_key, dims, shards, least, top_value):
    level = 1.0
    for dim, shards_of in shards:
        draws = jax.random.uniform(jax.random.fold_in(jax.random.fold_in(own_key, 6), dim), (shards_of,), jnp.float32, least / len(shards), top_value / len(shards))
        level = level * jnp.repeat(jnp.exp(draws), dims[dim] // shards_of).reshape((-1,) + (1,) * (len(dims) - 1 - dim))
    return level


def normal_values(own_key, shape, deviation, reach, pieces=(), held_as=jnp.bfloat16):
    array = jax.random.normal(own_key, shape, jnp.float32) * deviation
    if len(pieces) > 0:
        array = steps_of(own_key, shape, pieces, -0.22, 0.18) * array
    return jnp.clip(array, min=-reach, max=reach).astype(held_as)


def setup_inputs(seed: int = 0) -> dict:
    arg_keys = jax.random.split(jax.random.key(seed), 11)
    return {
        "forward_prev": draw_forward_prev(jax.random.fold_in(arg_keys[10], 71), 0),
        "forward_now": draw_forward_now(jax.random.fold_in(arg_keys[10], 71), 0),
        "adjoint_prev": draw_adjoint_prev(jax.random.fold_in(arg_keys[10], 71), 0),
        "adjoint_now": draw_adjoint_now(jax.random.fold_in(arg_keys[10], 71), 0),
        "velocity": jnp.clip(jnp.exp(math.log(0.41992188) - 0.7456652 * jax.random.uniform(arg_keys[4], (AX, MY, AZ), jnp.float32) ** steps_of(arg_keys[4], (AX, MY, AZ), ((0, 16), (1, 8)), -0.2, 0.2)), 0.19921875, 0.41992188).astype(jnp.bfloat16),
        "density": jnp.clip(jnp.exp(math.log(2.5) - 0.916290732 * jax.random.uniform(arg_keys[5], (AX, MY, AZ), jnp.float32) ** steps_of(arg_keys[5], (AX, MY, AZ), ((0, 16), (1, 8)), -0.2, 0.2)), 1.0, 2.5).astype(jnp.bfloat16),
        "anchors": place_ends(jax.random.randint(arg_keys[6], (NGROUPS,), 0, PY_DEV * N_SHOT - AY + 1), jax.random.fold_in(arg_keys[6], 1), 0, PY_DEV * N_SHOT - AY).astype(jnp.int32),
        "shot_cell": place_ends(jax.random.randint(arg_keys[7], (NGROUPS,), 0, AX * AY * AZ), jax.random.fold_in(arg_keys[7], 1), 0, (AX * AY * AZ) - 1).astype(jnp.int32),
        "wavelet": normal_values(arg_keys[8], (NGROUPS, STEPS), 4.0, 24.0, ((0, 8),), jnp.float32),
        "records": normal_values(arg_keys[9], (NGROUPS, STEPS, AX, AY), 1.0, 6.0, ((0, 8), (2, 16)), jnp.float32),
    }


LAPLACE_WEIGHTS = (-205.0 / 72.0, 8.0 / 5.0, -1.0 / 5.0, 8.0 / 315.0, -1.0 / 560.0)
SLOPE_WEIGHTS = (4.0 / 5.0, -1.0 / 5.0, 4.0 / 105.0, -1.0 / 280.0)


def neighbours(extended, row_count):
    center = extended[4:4 + row_count]
    widths = center.shape
    padded = jnp.pad(center, ((0, 0), (4, 4), (4, 4)))
    laplacian = 3.0 * LAPLACE_WEIGHTS[0] * center
    slope_rows = jnp.zeros_like(center)
    slope_cols = jnp.zeros_like(center)
    slope_depth = jnp.zeros_like(center)
    for offset in range(1, 5):
        east_side = extended[4 + offset:4 + offset + row_count]
        west_side = extended[4 - offset:4 - offset + row_count]
        north_side = padded[:, 4 + offset:4 + offset + widths[1], 4:4 + widths[2]]
        south_side = padded[:, 4 - offset:4 - offset + widths[1], 4:4 + widths[2]]
        upper_side = padded[:, 4:4 + widths[1], 4 + offset:4 + offset + widths[2]]
        lower_side = padded[:, 4:4 + widths[1], 4 - offset:4 - offset + widths[2]]
        laplacian = laplacian + LAPLACE_WEIGHTS[offset] * (((east_side + west_side) + (north_side + south_side)) + (upper_side + lower_side))
        slope_rows = slope_rows + SLOPE_WEIGHTS[offset - 1] * (east_side - west_side)
        slope_cols = slope_cols + SLOPE_WEIGHTS[offset - 1] * (north_side - south_side)
        slope_depth = slope_depth + SLOPE_WEIGHTS[offset - 1] * (upper_side - lower_side)
    return center, laplacian, slope_rows, slope_cols, slope_depth


def advance(previous, extended, coefficient, slopes):
    center, laplacian, slope_rows, slope_cols, slope_depth = neighbours(extended, previous.shape[0])
    drift = slopes[0] * slope_rows + slopes[1] * slope_cols + slopes[2] * slope_depth
    return 2.0 * center - previous + coefficient * (laplacian - drift)


def pad_rows(field):
    return jnp.pad(field, ((4, 4), (0, 0), (0, 0)))


def reference(forward_prev, forward_now, adjoint_prev, adjoint_now, velocity, density, anchors, shot_cell, wavelet, records):
    image = jnp.zeros((AX, MY, AZ), jnp.float32)
    finals = []
    for member in range(NGROUPS):
        begin = anchors[member].astype(jnp.int32)
        window_speed = lax.dynamic_slice_in_dim(velocity, begin, AY, 1).astype(jnp.float32)
        coefficient = window_speed * window_speed
        logdens = jnp.log(lax.dynamic_slice_in_dim(density, begin, AY, 1).astype(jnp.float32))
        unused_center, unused_lap, slope_rows, slope_cols, slope_depth = neighbours(pad_rows(logdens), AX)
        slopes = jnp.stack([slope_rows, slope_cols, slope_depth])
        source_cell = shot_cell[member]
        source_row = source_cell // (AY * AZ)
        source_col = (source_cell // AZ) % AY
        source_depth = source_cell % AZ
        previous, current = forward_prev[member], forward_now[member]
        snapshots = []
        for moment in range(STEPS):
            following = advance(previous, pad_rows(current), coefficient, slopes)
            following = following.at[source_row, source_col, source_depth].add(wavelet[member, moment])
            snapshots.append(following)
            previous, current = current, following
        previous, current = adjoint_prev[member], adjoint_now[member]
        partial_value = jnp.zeros((AX, AY, AZ), jnp.float32)
        for moment in range(STEPS):
            following = advance(previous, pad_rows(current), coefficient, slopes)
            following = following.at[:, :, SURF].add(records[member, moment])
            partial_value = partial_value + following * snapshots[STEPS - 1 - moment]
            previous, current = current, following
        finals.append(current)
        placed = lax.dynamic_slice_in_dim(image, begin, AY, 1) + partial_value
        image = lax.dynamic_update_slice_in_dim(image, placed, begin, 1)
    return image, jnp.stack(finals)
```

```python
import functools

import jax
import jax.numpy as jnp
import ml_dtypes
import numpy as np
from jax import lax
from jax.experimental import pallas as pl
from jax.experimental.pallas import tpu as pltpu
from jax.sharding import PartitionSpec as P

STEPS = 6
SURF = 8
ROWS, COLS, DEPTH = 8, 160, 256
TILE = 64
LAP = (-14350.0, 8064.0, -1008.0, 128.0, -9.0)
SLOPE = (672.0, -168.0, 32.0, -3.0)
LAP_SCALE, SLOPE_SCALE = 1.0 / 5040.0, 1.0 / 840.0
F32, BF16 = jnp.float32, jnp.bfloat16
VMEM = pl.BlockSpec(memory_space=pltpu.VMEM)
SMEM = pl.BlockSpec(memory_space=pltpu.SMEM)
PARAMS = pltpu.CompilerParams(vmem_limit_bytes=56 * 1024 * 1024)


def banded(size):
    lap, slope = np.zeros((size, size)), np.zeros((size, size))
    for k in range(1, 5):
        lap += LAP[k] * (np.eye(size, k=k) + np.eye(size, k=-k))
        slope += SLOPE[k - 1] * (np.eye(size, k=k) - np.eye(size, k=-k))
    return lap, slope


def weight_tables():
    lap, slope = banded(DEPTH)
    depth_table = np.concatenate([lap.T, slope.T], axis=1).astype(ml_dtypes.bfloat16)
    lap, slope = banded(COLS)
    cols_table = np.concatenate([lap, slope], axis=0).astype(ml_dtypes.bfloat16)
    return jnp.asarray(depth_table), jnp.asarray(cols_table)


def halves(x):
    high = x.astype(BF16)
    return high, (x - high.astype(F32)).astype(BF16)


def in_plane(src, depth_w, cols_w, zz, cc):
    def body(r, carry):
        high, low = halves(src[4 + r])
        zz[r] = jnp.dot(high, depth_w[...], preferred_element_type=F32) + jnp.dot(
            low, depth_w[...], preferred_element_type=F32
        )
        cc[r] = jnp.dot(cols_w[...], high, preferred_element_type=F32) + jnp.dot(
            cols_w[...], low, preferred_element_type=F32
        )
        return carry

    lax.fori_loop(0, ROWS, body, 0)


def load_extended(ext, now, parity, core_rows, cross_rows):
    ext[4 : 4 + ROWS] = now[...]
    core_at = pl.multiple_of((1 - parity) * 12, 4)
    cross_at = pl.multiple_of(parity * 12, 4)
    ext[pl.ds(core_at, 4)] = core_rows
    ext[pl.ds(cross_at, 4)] = cross_rows


def slopes_kernel(info, vel, dens, core, cross, depth_w, cols_w, coef, s0, s1, s2, ext, zz, cc):
    parity, outer = info[0], info[1]
    pad = jnp.where(outer == 1, 1.0, 0.0).astype(F32)
    core_at = pl.multiple_of((1 - parity) * 12, 4)
    cross_at = pl.multiple_of(parity * 12, 4)
    ext[4 : 4 + ROWS] = jnp.log(dens[...].astype(F32))
    ext[pl.ds(core_at, 4)] = jnp.log(core[...].astype(F32))
    ext[pl.ds(cross_at, 4)] = jnp.log(cross[...].astype(F32) + pad)
    in_plane(ext, depth_w, cols_w, zz, cc)

    def body(i, carry):
        at = pl.ds(pl.multiple_of(i * 8, 8), 8)
        at2 = pl.ds(pl.multiple_of(COLS + i * 8, 8), 8)
        e = [ext[r, at, :] for r in range(16)]
        for r in range(ROWS):
            speed = vel[r, at, :]
            c = speed * speed
            d0 = SLOPE[0] * (e[r + 5] - e[r + 3])
            for k in range(2, 5):
                d0 += SLOPE[k - 1] * (e[r + 4 + k] - e[r + 4 - k])
            coef[r, at, :] = c * LAP_SCALE
            cs = c * (SLOPE_SCALE * SLOPE_SCALE)
            s0[r, at, :] = cs * d0
            s1[r, at, :] = cs * cc[r, at2, :]
            s2[r, at, :] = cs * zz[r, at, DEPTH:]
        return carry

    lax.fori_loop(0, COLS // 8, body, 0)


def step_kernel(mode, first, *refs):
    refs = list(refs)
    info = refs.pop(0)
    amount = refs.pop(0) if mode == "fwd" else None
    prev, now, core, cross = refs[:4]
    refs = refs[4:]
    if first:
        qs_now = None
    else:
        qr_now, qr_prev, qs_now, qs_prev = refs[:4]
        refs = refs[4:]
    plane = refs.pop(0) if mode == "bwd" else None
    coef, s0, s1, s2, depth_w, cols_w = refs[:6]
    refs = refs[6:]
    out = refs.pop(0)
    last = len(refs) == 3
    if not last:
        core_out, cross_out, qr_out, qs_out = refs[:4]
        refs = refs[4:]
    ext, zz, cc = refs
    parity = info[0]
    if first:
        seen = cross[...]
    else:
        seen = (2.0 * qr_now[...] - qr_prev[...]) + cross[...].astype(F32)
    load_extended(ext, now, parity, core[...], seen)
    if not last:
        qr_out[...] = seen
    in_plane(ext, depth_w, cols_w, zz, cc)

    def body(i, carry):
        at = pl.ds(pl.multiple_of(i * 8, 8), 8)
        at2 = pl.ds(pl.multiple_of(COLS + i * 8, 8), 8)
        e = [ext[r, at, :] for r in range(16)]
        for r in range(ROWS):
            mid = e[r + 4]
            lap = (3.0 * LAP[0]) * mid + (cc[r, at, :] + zz[r, at, :DEPTH])
            d0 = None
            for k in range(1, 5):
                hi, lo = e[r + 4 + k], e[r + 4 - k]
                lap += LAP[k] * (hi + lo)
                term = SLOPE[k - 1] * (hi - lo)
                d0 = term if d0 is None else d0 + term
            drift = s0[r, at, :] * d0 + s1[r, at, :] * cc[r, at2, :] + s2[r, at, :] * zz[r, at, DEPTH:]
            new = 2.0 * mid - prev[r, at, :] + (coef[r, at, :] * lap - drift)
            if mode == "bwd":
                out[r, at, :128] = new[:, :128] + plane[r, at, :]
                out[r, at, 128:] = new[:, 128:]
            else:
                out[r, at, :] = new
        return carry

    lax.fori_loop(0, COLS // 8, body, 0)

    if mode == "fwd":

        @pl.when(info[2] == 1)
        def _():
            row, col = info[3], info[4]
            base = pl.multiple_of((col // 8) * 8, 8)
            col_in = lax.broadcasted_iota(jnp.int32, (8, DEPTH), 0)
            depth_in = lax.broadcasted_iota(jnp.int32, (8, DEPTH), 1)
            struck = (col_in == col - base) & (depth_in == info[5])
            out[row, pl.ds(base, 8), :] += jnp.where(struck, amount[0], 0.0)

    if not last:
        core_out[...] = out[pl.ds(pl.multiple_of((1 - parity) * 4, 4), 4)]
        rows = out[pl.ds(pl.multiple_of(parity * 4, 4), 4)]
        if first:
            own = now[pl.ds(pl.multiple_of(parity * 4, 4), 4)]
            base = own
        else:
            base = 2.0 * qs_now[...] - qs_prev[...]
        sent = (rows - base).astype(BF16)
        cross_out[...] = sent
        qs_out[...] = base + sent.astype(F32)


def step(mode, info, amount, prev, now, core, cross, quant, plane, fields, tables, last):
    first = quant is None
    args = [info]
    specs = [SMEM]
    if mode == "fwd":
        args.append(amount)
        specs.append(SMEM)
    args += [prev, now, core, cross]
    if not first:
        args += list(quant)
    if mode == "bwd":
        args.append(plane)
    args += list(fields) + list(tables)
    specs += [VMEM] * (len(args) - len(specs))
    slab = jax.ShapeDtypeStruct((ROWS, COLS, DEPTH), F32)
    face = jax.ShapeDtypeStruct((4, COLS, DEPTH), F32)
    outs = [slab]
    if not last:
        outs += [face, jax.ShapeDtypeStruct((4, COLS, DEPTH), BF16), face, face]
    return pl.pallas_call(
        functools.partial(step_kernel, mode, first),
        out_shape=outs,
        in_specs=specs,
        out_specs=[VMEM] * len(outs),
        scratch_shapes=[
            pltpu.VMEM((ROWS + 8, COLS, DEPTH), F32),
            pltpu.VMEM((ROWS, COLS, 2 * DEPTH), F32),
            pltpu.VMEM((ROWS, 2 * COLS, DEPTH), F32),
        ],
        compiler_params=PARAMS,
        cost_estimate=pl.CostEstimate(flops=1_500_000_000, bytes_accessed=12_000_000, transcendentals=0),
        name="step_" + mode,
    )(*args)


def window_kernel(info, t0, t1, t2, t3, vel_out, dens_out, core_out, cross_out, wide, shifted):
    parity, offset = info[0], info[1]
    want = lax.broadcasted_iota(jnp.int32, (COLS, TILE), 0) + offset
    within = lax.broadcasted_iota(jnp.int32, (COLS, TILE), 1)
    pick = jnp.concatenate(
        [jnp.where(within + info[2 + s] * TILE == want, 1.0, 0.0) for s in range(4)], axis=1
    ).astype(BF16)
    for which in range(2):
        for s, tile in enumerate((t0, t1, t2, t3)):
            wide[:, s * TILE : (s + 1) * TILE, :] = tile[which]
        target = vel_out if which == 0 else shifted
        for r in range(ROWS):
            target[r] = jnp.dot(pick, wide[r], preferred_element_type=F32)
    dens_out[...] = shifted[...].astype(BF16)
    core_out[...] = shifted[pl.ds(pl.multiple_of((1 - parity) * 4, 4), 4)].astype(BF16)
    cross_out[...] = shifted[pl.ds(pl.multiple_of(parity * 4, 4), 4)].astype(BF16)


def blocks_kernel(info, part, a5, s0, a0, s5, b0, b1, b2, b3):
    within = lax.broadcasted_iota(jnp.int32, (TILE, COLS), 0)
    column = lax.broadcasted_iota(jnp.int32, (TILE, COLS), 1) + info[0]
    pick = jnp.concatenate(
        [jnp.where(within + info[1 + s] * TILE == column, 1.0, 0.0) for s in range(4)], axis=0
    ).astype(BF16)
    for r in range(ROWS):
        total = part[r] + a5[r] * s0[r] + a0[r] * s5[r]
        high, low = halves(total)
        placed = jnp.dot(pick, high, preferred_element_type=F32) + jnp.dot(
            pick, low, preferred_element_type=F32
        )
        for s, block in enumerate((b0, b1, b2, b3)):
            block[r] = placed[s * TILE : (s + 1) * TILE]


def shards(
    forward_prev,
    forward_now,
    adjoint_prev,
    adjoint_now,
    velocity,
    density,
    anchors,
    shot_cell,
    wavelet,
    records,
):
    tables = weight_tables()
    place = lax.axis_index("apert")
    shot = lax.axis_index("shot")
    count = lax.axis_size("apert")
    groups = lax.axis_size("shot")
    half = groups // 2
    parity = place & 1
    core_pairs = [(i, i ^ 1) for i in range(count)]
    cross_pairs = [(i, i + 1) for i in range(1, count - 1, 2)] + [(i + 1, i) for i in range(1, count - 1, 2)]
    side_pairs = [(i, (i + half) % groups) for i in range(groups)]

    def ring_pairs(shift):
        return [(i, (i // half) * half + (i % half + shift) % half) for i in range(groups)]

    def faces(field):
        return (
            lax.dynamic_slice_in_dim(field, (1 - parity) * 4, 4, 0),
            lax.dynamic_slice_in_dim(field, parity * 4, 4, 0),
        )

    def swap(core, cross):
        return lax.ppermute(core, "apert", core_pairs), lax.ppermute(cross, "apert", cross_pairs)

    starts = lax.all_gather(anchors[0], "shot")
    both = jnp.stack([velocity, density])
    other = lax.ppermute(both, "shot", side_pairs)
    upper = shot // half
    ring = shot % half

    def tile_of(group):
        first = starts[group] // TILE
        return (first + (ring - first) % half) // half

    tiles = []
    for shift in range(half):
        group = upper * half + (ring + shift) % half
        piece = jnp.where(tile_of(group) == upper, both, other)
        tiles.append(piece if shift == 0 else lax.ppermute(piece, "shot", ring_pairs(shift)))
    begin = anchors[0]
    first_tile = begin // TILE
    offset = begin - first_tile * TILE

    fwd_prev, fwd_now, bwd_prev, bwd_now = forward_prev[0], forward_now[0], adjoint_prev[0], adjoint_now[0]
    fwd_core, fwd_cross = swap(*faces(fwd_now))
    bwd_core, bwd_cross = swap(*faces(bwd_now))

    slots = [(ring - shift - first_tile) % half for shift in range(half)]
    info = jnp.stack([parity, offset] + slots).astype(jnp.int32)
    slab = jax.ShapeDtypeStruct((ROWS, COLS, DEPTH), F32)
    thin = jax.ShapeDtypeStruct((4, COLS, DEPTH), BF16)
    vel, dens, dens_core, dens_cross = pl.pallas_call(
        window_kernel,
        out_shape=[slab, jax.ShapeDtypeStruct((ROWS, COLS, DEPTH), BF16), thin, thin],
        in_specs=[SMEM] + [VMEM] * 4,
        out_specs=[VMEM] * 4,
        scratch_shapes=[pltpu.VMEM((ROWS, 4 * TILE, DEPTH), BF16), pltpu.VMEM((ROWS, COLS, DEPTH), F32)],
        compiler_params=PARAMS,
        name="window",
    )(info, *tiles)
    dens_core, dens_cross = swap(dens_core, dens_cross)
    outer = ((place == 0) | (place == count - 1)).astype(jnp.int32)
    info = jnp.stack([parity, outer]).astype(jnp.int32)
    fields = pl.pallas_call(
        slopes_kernel,
        out_shape=[slab] * 4,
        in_specs=[SMEM] + [VMEM] * 6,
        out_specs=[VMEM] * 4,
        scratch_shapes=[
            pltpu.VMEM((ROWS + 8, COLS, DEPTH), F32),
            pltpu.VMEM((ROWS, COLS, 2 * DEPTH), F32),
            pltpu.VMEM((ROWS, 2 * COLS, DEPTH), F32),
        ],
        compiler_params=PARAMS,
        name="slopes",
    )(info, vel, dens, dens_core, dens_cross, *tables)

    cell = shot_cell[0]
    row = cell // (COLS * DEPTH) - place * ROWS
    here = ((row >= 0) & (row < ROWS)).astype(jnp.int32)
    info = jnp.stack(
        [parity, outer, here, jnp.clip(row, 0, ROWS - 1), cell // DEPTH % COLS, cell % DEPTH]
    ).astype(jnp.int32)
    lane = lax.broadcasted_iota(jnp.int32, (1, 1, 1, 128), 3)
    planes = jnp.where(lane == SURF, records[0][..., None], 0.0)

    fwd_quant = bwd_quant = None
    snapshots, states = [], []
    part = None
    for moment in range(STEPS):
        last = moment == STEPS - 1
        if moment > 0:
            fwd_core, fwd_cross = swap(fwd_core, fwd_cross)
        new, *sent = step(
            "fwd", info, wavelet[0, moment : moment + 1], fwd_prev, fwd_now, fwd_core, fwd_cross,
            fwd_quant, None, fields, tables, last,
        )
        if not last:
            own = faces(fwd_now)[1] if moment == 0 else fwd_quant[2]
            fwd_core, fwd_cross, seen, shown = sent
            fwd_quant = (seen, seen if moment == 0 else fwd_quant[0], shown, own)
        snapshots.append(new)
        fwd_prev, fwd_now = fwd_now, new

        if moment > 0:
            bwd_core, bwd_cross = swap(bwd_core, bwd_cross)
        new, *sent = step(
            "bwd", info, None, bwd_prev, bwd_now, bwd_core, bwd_cross,
            bwd_quant, planes[moment], fields, tables, last,
        )
        if not last:
            own = faces(bwd_now)[1] if moment == 0 else bwd_quant[2]
            bwd_core, bwd_cross, seen, shown = sent
            bwd_quant = (seen, seen if moment == 0 else bwd_quant[0], shown, own)
        states.append(new)
        bwd_prev, bwd_now = bwd_now, new
    part = sum(states[t] * snapshots[STEPS - 1 - t] for t in range(1, STEPS - 1))

    slots = [(ring + shift - first_tile) % half for shift in range(half)]
    info = jnp.stack([offset] + slots).astype(jnp.int32)
    block = jax.ShapeDtypeStruct((ROWS, TILE, DEPTH), F32)
    blocks = pl.pallas_call(
        blocks_kernel,
        out_shape=[block] * 4,
        in_specs=[SMEM] + [VMEM] * 5,
        out_specs=[VMEM] * 4,
        compiler_params=PARAMS,
        name="blocks",
    )(info, part, states[STEPS - 1], snapshots[0], states[0], snapshots[STEPS - 1])
    keep = give = jnp.zeros((ROWS, TILE, DEPTH), F32)
    for shift in range(half):
        arrived = blocks[0] if shift == 0 else lax.ppermute(blocks[shift], "shot", ring_pairs(shift))
        mine = tile_of(upper * half + (ring - shift) % half) == upper
        keep = keep + jnp.where(mine, arrived, 0.0)
        give = give + jnp.where(mine, 0.0, arrived)
    image = keep + lax.ppermute(give, "shot", side_pairs)
    return image, states[STEPS - 1][None]


def solution(mesh):
    placed = (
        P("shot", "apert", None, None),
        P("shot", "apert", None, None),
        P("shot", "apert", None, None),
        P("shot", "apert", None, None),
        P("apert", "shot", None),
        P("apert", "shot", None),
        P("shot"),
        P("shot"),
        P("shot", None),
        P("shot", None, "apert", None),
    )
    return jax.shard_map(
        shards,
        mesh=mesh,
        in_specs=placed,
        out_specs=(P("apert", "shot", None), P("shot", "apert", None, None)),
        check_vma=False,
    )
```

```python
import functools

import jax
import jax.numpy as jnp
import ml_dtypes
import numpy as np
from jax import lax
from jax.experimental import pallas as pl
from jax.experimental.pallas import tpu as pltpu
from jax.sharding import PartitionSpec as P

STEPS = 6
SURF = 8
ROWS, COLS, DEPTH = 8, 160, 256
TILE = 64
LAP = (-14350.0, 8064.0, -1008.0, 128.0, -9.0)
SLOPE = (672.0, -168.0, 32.0, -3.0)
LAP_SCALE, SLOPE_SCALE = 1.0 / 5040.0, 1.0 / 840.0
F32, BF16 = jnp.float32, jnp.bfloat16
VMEM = pl.BlockSpec(memory_space=pltpu.VMEM)
SMEM = pl.BlockSpec(memory_space=pltpu.SMEM)
PARAMS = pltpu.CompilerParams(vmem_limit_bytes=16 * 1024 * 1024)


def banded(size):
    lap, slope = np.zeros((size, size)), np.zeros((size, size))
    for k in range(1, 5):
        lap += LAP[k] * (np.eye(size, k=k) + np.eye(size, k=-k))
        slope += SLOPE[k - 1] * (np.eye(size, k=k) - np.eye(size, k=-k))
    return lap, slope


def weight_tables():
    lap, slope = banded(DEPTH)
    depth_table = np.concatenate([lap.T, slope.T], axis=1).astype(ml_dtypes.bfloat16)
    lap, slope = banded(COLS)
    cols_table = np.concatenate([lap, slope], axis=0).astype(ml_dtypes.bfloat16)
    return jnp.asarray(depth_table), jnp.asarray(cols_table)


def halves(x):
    high = x.astype(BF16)
    return high, (x - high.astype(F32)).astype(BF16)


def in_plane(src, depth_w, cols_w, zz, cc):
    def body(r, carry):
        high, low = halves(src[4 + r])
        zz[r] = jnp.dot(high, depth_w[...], preferred_element_type=F32) + jnp.dot(
            low, depth_w[...], preferred_element_type=F32
        )
        cc[r] = jnp.dot(cols_w[...], high, preferred_element_type=F32) + jnp.dot(
            cols_w[...], low, preferred_element_type=F32
        )
        return carry

    lax.fori_loop(0, ROWS, body, 0)


def load_extended(ext, now, parity, core_rows, cross_rows):
    ext[4 : 4 + ROWS] = now[...]
    core_at = pl.multiple_of((1 - parity) * 12, 4)
    cross_at = pl.multiple_of(parity * 12, 4)
    ext[pl.ds(core_at, 4)] = core_rows
    ext[pl.ds(cross_at, 4)] = cross_rows


def call(body, args, outs, scratch=(), name=None):
    specs, given = [], []
    for arg in args:
        if arg.ndim == 1:
            specs.append(SMEM)
            given.append(arg)
        else:
            specs.append(VMEM)
            given.append(pltpu.with_memory_space_constraint(arg, pltpu.VMEM))
    return pl.pallas_call(
        body,
        out_shape=[pltpu.VMEM(shape, dtype) for shape, dtype in outs],
        in_specs=specs,
        out_specs=[VMEM] * len(outs),
        scratch_shapes=list(scratch),
        compiler_params=PARAMS,
        name=name,
    )(*given)


SLAB, FACE = (ROWS, COLS, DEPTH), (4, COLS, DEPTH)


def ring_of(ids):
    return ids[1] & 3, ids[1] >> 2


def serves_upper(start, ids):
    ring, upper = ring_of(ids)
    first = start >> 6
    return ((first + ((ring - first) & 3)) >> 2) == upper


def select_kernel(ids, begin, s1, s2, s3, vel, dens, other_vel, other_dens, *outs):
    for out, start in zip(outs, (begin, s3, s2, s1)):
        mine = serves_upper(start[0], ids)

        @pl.when(mine)
        def _():
            out[0] = vel[...]
            out[1] = dens[...]

        @pl.when(jnp.logical_not(mine))
        def _():
            out[0] = other_vel[...]
            out[1] = other_dens[...]


def window_pick(ids, begin):
    ring, _ = ring_of(ids)
    first, offset = begin[0] >> 6, begin[0] & 63
    want = lax.broadcasted_iota(jnp.int32, (COLS, TILE), 0) + offset
    within = lax.broadcasted_iota(jnp.int32, (COLS, TILE), 1)
    picks = [jnp.where(within + ((ring - s - first) & 3) * TILE == want, 1.0, 0.0) for s in range(4)]
    return jnp.concatenate(picks, axis=1).astype(BF16)


def window_dens_kernel(ids, begin, t0, t1, t2, t3, dens_out, core_out, cross_out, wide):
    parity = ids[0] & 1
    pick = window_pick(ids, begin)
    for s, tile in enumerate((t0, t1, t2, t3)):
        wide[:, s * TILE : (s + 1) * TILE, :] = tile[1]
    for r in range(ROWS):
        dens_out[r] = jnp.dot(pick, wide[r], preferred_element_type=F32)
    core_out[...] = dens_out[pl.ds(pl.multiple_of((1 - parity) * 4, 4), 4)].astype(BF16)
    cross_out[...] = dens_out[pl.ds(pl.multiple_of(parity * 4, 4), 4)].astype(BF16)


def coef_kernel(ids, begin, t0, t1, t2, t3, dens, depth_w, cols_w, coef, s1, s2, logs, wide):
    pick = window_pick(ids, begin)
    for s, tile in enumerate((t0, t1, t2, t3)):
        wide[:, s * TILE : (s + 1) * TILE, :] = tile[0]
    for r in range(ROWS):
        speed = jnp.dot(pick, wide[r], preferred_element_type=F32)
        c = speed * speed
        coef[r] = c * LAP_SCALE
        log = jnp.log(dens[r])
        logs[r] = log
        high, low = halves(log)
        cs = c * (SLOPE_SCALE * SLOPE_SCALE)
        s1[r] = cs * (
            jnp.dot(cols_w[COLS:], high, preferred_element_type=F32)
            + jnp.dot(cols_w[COLS:], low, preferred_element_type=F32)
        )
        s2[r] = cs * (
            jnp.dot(high, depth_w[:, DEPTH:], preferred_element_type=F32)
            + jnp.dot(low, depth_w[:, DEPTH:], preferred_element_type=F32)
        )


def row_slope_kernel(ids, logs, core, cross, coef, s0, ext):
    parity, place = ids[0] & 1, ids[0]
    pad = jnp.where((place == 0) | (place == 15), 1.0, 0.0).astype(F32)
    load_extended(ext, logs, parity, jnp.log(core[...].astype(F32)), jnp.log(cross[...].astype(F32) + pad))

    def body(i, carry):
        at = pl.ds(pl.multiple_of(i * 8, 8), 8)
        e = [ext[r, at, :] for r in range(16)]
        for r in range(ROWS):
            d0 = SLOPE[0] * (e[r + 5] - e[r + 3])
            for k in range(2, 5):
                d0 += SLOPE[k - 1] * (e[r + 4 + k] - e[r + 4 - k])
            s0[r, at, :] = (coef[r, at, :] * (SLOPE_SCALE * SLOPE_SCALE / LAP_SCALE)) * d0
        return carry

    lax.fori_loop(0, COLS // 8, body, 0)


def step_kernel(mode, first, moment, *refs):
    refs = list(refs)
    ids = refs.pop(0)
    cell, amount = (refs.pop(0), refs.pop(0)) if mode == "fwd" else (None, None)
    prev, now, core, cross = refs[:4]
    refs = refs[4:]
    if first:
        qs_now = None
    else:
        qr_now, qr_prev, qs_now, qs_prev = refs[:4]
        refs = refs[4:]
    plane = refs.pop(0) if mode == "bwd" else None
    coef, s0, s1, s2, depth_w, cols_w = refs[:6]
    refs = refs[6:]
    out = refs.pop(0)
    last = len(refs) == 3
    if not last:
        core_out, cross_out, qr_out, qs_out = refs[:4]
        refs = refs[4:]
    ext, zz, cc = refs
    parity = ids[0] & 1
    if first:
        seen = cross[...]
    else:
        seen = (2.0 * qr_now[...] - qr_prev[...]) + cross[...].astype(F32)
    load_extended(ext, now, parity, core[...], seen)
    if not last:
        qr_out[...] = seen
    in_plane(ext, depth_w, cols_w, zz, cc)

    def body(i, carry):
        at = pl.ds(pl.multiple_of(i * 8, 8), 8)
        at2 = pl.ds(pl.multiple_of(COLS + i * 8, 8), 8)
        e = [ext[r, at, :] for r in range(16)]
        for r in range(ROWS):
            mid = e[r + 4]
            lap = (3.0 * LAP[0]) * mid + (cc[r, at, :] + zz[r, at, :DEPTH])
            d0 = None
            for k in range(1, 5):
                hi, lo = e[r + 4 + k], e[r + 4 - k]
                lap += LAP[k] * (hi + lo)
                term = SLOPE[k - 1] * (hi - lo)
                d0 = term if d0 is None else d0 + term
            drift = s0[r, at, :] * d0 + s1[r, at, :] * cc[r, at2, :] + s2[r, at, :] * zz[r, at, DEPTH:]
            new = 2.0 * mid - prev[r, at, :] + (coef[r, at, :] * lap - drift)
            if mode == "bwd":
                out[r, at, :128] = new[:, :128] + plane[moment, r, at, :]
                out[r, at, 128:] = new[:, 128:]
            else:
                out[r, at, :] = new
        return carry

    lax.fori_loop(0, COLS // 8, body, 0)

    if mode == "fwd":

        line = cell[0] >> 8
        row = lax.div(line, COLS) - ids[0] * ROWS

        @pl.when((row >= 0) & (row < ROWS))
        def _():
            col = lax.rem(line, COLS)
            base = pl.multiple_of(col & ~7, 8)
            col_in = lax.broadcasted_iota(jnp.int32, (8, DEPTH), 0)
            depth_in = lax.broadcasted_iota(jnp.int32, (8, DEPTH), 1)
            struck = (col_in == (col & 7)) & (depth_in == (cell[0] & 255))
            out[row, pl.ds(base, 8), :] += jnp.where(struck, amount[moment], 0.0)

    if not last:
        core_out[...] = out[pl.ds(pl.multiple_of((1 - parity) * 4, 4), 4)]
        rows = out[pl.ds(pl.multiple_of(parity * 4, 4), 4)]
        if first:
            own = now[pl.ds(pl.multiple_of(parity * 4, 4), 4)]
            base = own
        else:
            base = 2.0 * qs_now[...] - qs_prev[...]
        sent = (rows - base).astype(BF16)
        cross_out[...] = sent
        qs_out[...] = base + sent.astype(F32)


def step(mode, moment, ids, source, prev, now, core, cross, quant, planes, fields, tables):
    first, last = moment == 0, moment == STEPS - 1
    args = [ids]
    if mode == "fwd":
        args += list(source)
    args += [prev, now, core, cross]
    if not first:
        args += list(quant)
    if mode == "bwd":
        args.append(planes)
    args += list(fields) + list(tables)
    outs = [(SLAB, F32)]
    if not last:
        outs += [(FACE, F32), (FACE, BF16), (FACE, F32), (FACE, F32)]
    scratch = [
        pltpu.VMEM((ROWS + 8, COLS, DEPTH), F32),
        pltpu.VMEM((ROWS, COLS, 2 * DEPTH), F32),
        pltpu.VMEM((ROWS, 2 * COLS, DEPTH), F32),
    ]
    return call(functools.partial(step_kernel, mode, first, moment), args, outs, scratch, "step_" + mode)


def blocks_kernel(ids, begin, part, a5, s0, a0, s5, b0, b1, b2, b3):
    ring, _ = ring_of(ids)
    first, offset = begin[0] >> 6, begin[0] & 63
    within = lax.broadcasted_iota(jnp.int32, (TILE, COLS), 0)
    column = lax.broadcasted_iota(jnp.int32, (TILE, COLS), 1) + offset
    picks = [jnp.where(within + ((ring + s - first) & 3) * TILE == column, 1.0, 0.0) for s in range(4)]
    pick = jnp.concatenate(picks, axis=0).astype(BF16)
    for r in range(ROWS):
        total = part[r] + a5[r] * s0[r] + a0[r] * s5[r]
        high, low = halves(total)
        placed = jnp.dot(pick, high, preferred_element_type=F32) + jnp.dot(
            pick, low, preferred_element_type=F32
        )
        for s, block in enumerate((b0, b1, b2, b3)):
            block[r] = placed[s * TILE : (s + 1) * TILE]


def combine_kernel(ids, begin, s1, s2, s3, b0, b1, b2, b3, keep, give):
    flags = [jnp.where(serves_upper(start[0], ids), 1.0, 0.0).astype(F32) for start in (begin, s1, s2, s3)]
    for r in range(ROWS):
        kept = flags[0] * b0[r]
        total = b0[r]
        for flag, block in zip(flags[1:], (b1, b2, b3)):
            kept += flag * block[r]
            total += block[r]
        keep[r] = kept
        gave = (1.0 - flags[0]) * b0[r]
        for flag, block in zip(flags[1:], (b1, b2, b3)):
            gave += (1.0 - flag) * block[r]
        give[r] = gave


def shards(
    forward_prev,
    forward_now,
    adjoint_prev,
    adjoint_now,
    velocity,
    density,
    anchors,
    shot_cell,
    wavelet,
    records,
):
    tables = weight_tables()
    place = lax.axis_index("apert")
    shot = lax.axis_index("shot")
    count = lax.axis_size("apert")
    groups = lax.axis_size("shot")
    half = groups // 2
    parity = place & 1
    ids = jnp.stack([place, shot]).astype(jnp.int32)
    core_pairs = [(i, i ^ 1) for i in range(count)]
    cross_pairs = [(i, i + 1) for i in range(1, count - 1, 2)] + [(i + 1, i) for i in range(1, count - 1, 2)]
    side_pairs = [(i, (i + half) % groups) for i in range(groups)]

    def ring_pairs(shift):
        return [(i, (i // half) * half + (i % half + shift) % half) for i in range(groups)]

    def faces(field):
        return (
            lax.dynamic_slice_in_dim(field, (1 - parity) * 4, 4, 0),
            lax.dynamic_slice_in_dim(field, parity * 4, 4, 0),
        )

    def swap(core, cross):
        return lax.ppermute(core, "apert", core_pairs), lax.ppermute(cross, "apert", cross_pairs)

    starts = [lax.ppermute(anchors, "shot", ring_pairs(k)) for k in range(1, half)]
    other_vel = lax.ppermute(velocity, "shot", side_pairs)
    other_dens = lax.ppermute(density, "shot", side_pairs)
    tile2 = ((2, ROWS, TILE, DEPTH), BF16)
    tiles = call(
        select_kernel, [ids, anchors, *starts, velocity, density, other_vel, other_dens], [tile2] * half, name="select"
    )
    tiles = [tiles[0]] + [lax.ppermute(tiles[k], "shot", ring_pairs(k)) for k in range(1, half)]

    fwd_prev, fwd_now, bwd_prev, bwd_now = forward_prev[0], forward_now[0], adjoint_prev[0], adjoint_now[0]
    fwd_faces, bwd_faces = faces(fwd_now), faces(bwd_now)
    fwd_core, fwd_cross = swap(*fwd_faces)
    bwd_core, bwd_cross = swap(*bwd_faces)

    wide = [pltpu.VMEM((ROWS, 4 * TILE, DEPTH), BF16)]
    dens, dens_core, dens_cross = call(
        window_dens_kernel, [ids, anchors, *tiles], [(SLAB, F32), (FACE, BF16), (FACE, BF16)], wide, "window_dens"
    )
    dens_core, dens_cross = swap(dens_core, dens_cross)
    coef, slope1, slope2, logs = call(
        coef_kernel, [ids, anchors, *tiles, dens, *tables], [(SLAB, F32)] * 4, wide, "coef"
    )
    (slope0,) = call(
        row_slope_kernel,
        [ids, logs, dens_core, dens_cross, coef],
        [(SLAB, F32)],
        [pltpu.VMEM((ROWS + 8, COLS, DEPTH), F32)],
        "row_slope",
    )
    fields = (coef, slope0, slope1, slope2)
    lane = lax.broadcasted_iota(jnp.int32, (1, 1, 1, 128), 3)
    planes = jnp.where(lane == SURF, records[0][..., None], 0.0)
    source = (shot_cell, wavelet[0])

    fwd_quant = bwd_quant = None
    snapshots, states = [], []
    for moment in range(STEPS):
        last = moment == STEPS - 1
        if moment > 0:
            fwd_core, fwd_cross = swap(fwd_core, fwd_cross)
        new, *sent = step(
            "fwd", moment, ids, source, fwd_prev, fwd_now, fwd_core, fwd_cross, fwd_quant, None, fields, tables
        )
        if not last:
            own = fwd_faces[1] if moment == 0 else fwd_quant[2]
            fwd_core, fwd_cross, seen, shown = sent
            fwd_quant = (seen, seen if moment == 0 else fwd_quant[0], shown, own)
        snapshots.append(new)
        fwd_prev, fwd_now = fwd_now, new

        if moment > 0:
            bwd_core, bwd_cross = swap(bwd_core, bwd_cross)
        new, *sent = step(
            "bwd", moment, ids, source, bwd_prev, bwd_now, bwd_core, bwd_cross, bwd_quant, planes, fields, tables
        )
        if not last:
            own = bwd_faces[1] if moment == 0 else bwd_quant[2]
            bwd_core, bwd_cross, seen, shown = sent
            bwd_quant = (seen, seen if moment == 0 else bwd_quant[0], shown, own)
        states.append(new)
        bwd_prev, bwd_now = bwd_now, new
    part = sum(states[t] * snapshots[STEPS - 1 - t] for t in range(1, STEPS - 1))

    block = ((ROWS, TILE, DEPTH), F32)
    blocks = call(
        blocks_kernel,
        [ids, anchors, part, states[STEPS - 1], snapshots[0], states[0], snapshots[STEPS - 1]],
        [block] * half,
        name="blocks",
    )
    arrived = [blocks[0]] + [lax.ppermute(blocks[k], "shot", ring_pairs(k)) for k in range(1, half)]
    keep, give = call(combine_kernel, [ids, anchors, *starts, *arrived], [block] * 2, name="combine")
    image = keep + lax.ppermute(give, "shot", side_pairs)
    return image, states[STEPS - 1][None]


def solution(mesh):
    placed = (
        P("shot", "apert", None, None),
        P("shot", "apert", None, None),
        P("shot", "apert", None, None),
        P("shot", "apert", None, None),
        P("apert", "shot", None),
        P("apert", "shot", None),
        P("shot"),
        P("shot"),
        P("shot", None),
        P("shot", None, "apert", None),
    )
    return jax.shard_map(
        shards,
        mesh=mesh,
        in_specs=placed,
        out_specs=(P("apert", "shot", None), P("shot", "apert", None, None)),
        check_vma=False,
    )
```

```python
import functools

import jax
import jax.numpy as jnp
import ml_dtypes
import numpy as np
from jax import lax
from jax.experimental import pallas as pl
from jax.experimental.pallas import tpu as pltpu
from jax.sharding import PartitionSpec as P

STEPS = 6
SURF = 8
ROWS, COLS, DEPTH = 8, 160, 256
TILE = 64
LAP = (-14350.0, 8064.0, -1008.0, 128.0, -9.0)
SLOPE = (672.0, -168.0, 32.0, -3.0)
LAP_SCALE, SLOPE_SCALE = 1.0 / 5040.0, 1.0 / 840.0
F32, BF16 = jnp.float32, jnp.bfloat16
VMEM = pl.BlockSpec(memory_space=pltpu.VMEM)
SMEM = pl.BlockSpec(memory_space=pltpu.SMEM)
PARAMS = pltpu.CompilerParams(vmem_limit_bytes=16 * 1024 * 1024)


def banded(size):
    lap, slope = np.zeros((size, size)), np.zeros((size, size))
    for k in range(1, 5):
        lap += LAP[k] * (np.eye(size, k=k) + np.eye(size, k=-k))
        slope += SLOPE[k - 1] * (np.eye(size, k=k) - np.eye(size, k=-k))
    return lap, slope


def weight_tables():
    lap, slope = banded(DEPTH)
    depth_table = np.concatenate([lap.T, slope.T], axis=1).astype(ml_dtypes.bfloat16)
    lap, slope = banded(COLS)
    cols_table = np.concatenate([lap, slope], axis=0).astype(ml_dtypes.bfloat16)
    return jnp.asarray(depth_table), jnp.asarray(cols_table)


def halves(x):
    high = x.astype(BF16)
    return high, (x - high.astype(F32)).astype(BF16)


def in_plane(src, depth_w, cols_w, zz, cc):
    def body(r, carry):
        high, low = halves(src[4 + r])
        zz[r] = jnp.dot(high, depth_w[...], preferred_element_type=F32) + jnp.dot(
            low, depth_w[...], preferred_element_type=F32
        )
        cc[r] = jnp.dot(cols_w[...], high, preferred_element_type=F32) + jnp.dot(
            cols_w[...], low, preferred_element_type=F32
        )
        return carry

    lax.fori_loop(0, ROWS, body, 0)


def load_extended(ext, now, parity, core_rows, cross_rows):
    ext[4 : 4 + ROWS] = now[...]
    core_at = pl.multiple_of((1 - parity) * 12, 4)
    cross_at = pl.multiple_of(parity * 12, 4)
    ext[pl.ds(core_at, 4)] = core_rows
    ext[pl.ds(cross_at, 4)] = cross_rows


def call(body, args, outs, scratch=(), name=None, flops=20_000_000_000):
    specs, given = [], []
    for arg in args:
        if arg.ndim == 1:
            specs.append(SMEM)
            given.append(arg)
        else:
            specs.append(VMEM)
            given.append(pltpu.with_memory_space_constraint(arg, pltpu.VMEM))
    return pl.pallas_call(
        body,
        out_shape=[pltpu.VMEM(shape, dtype) for shape, dtype in outs],
        in_specs=specs,
        out_specs=[VMEM] * len(outs),
        scratch_shapes=list(scratch),
        compiler_params=PARAMS,
        cost_estimate=pl.CostEstimate(flops=flops, bytes_accessed=100_000, transcendentals=0),
        name=name,
    )(*given)


SLAB, FACE = (ROWS, COLS, DEPTH), (4, COLS, DEPTH)


def ring_of(ids):
    return ids[1] & 3, ids[1] >> 2


def serves_upper(start, ids):
    ring, upper = ring_of(ids)
    first = start >> 6
    return ((first + ((ring - first) & 3)) >> 2) == upper


def faces_kernel(ids, fwd, bwd, vel, dens, core, cross, own_fwd, own_bwd, vel_out, dens_out):
    parity = ids[0] & 1
    for f, (field, own) in enumerate(((fwd, own_fwd), (bwd, own_bwd))):
        core[f] = field[pl.ds(pl.multiple_of((1 - parity) * 4, 4), 4)]
        own[...] = field[pl.ds(pl.multiple_of(parity * 4, 4), 4)]
        high = own[...].astype(BF16)
        cross[f, :4] = high
        near = parity * 3
        low = (own[near] - own[near].astype(BF16).astype(F32)).astype(BF16)
        cross[f, 4] = low
        own[...] = high.astype(F32)
        own[near] += low.astype(F32)
    vel_out[...] = vel[...]
    dens_out[...] = dens[...]


def select_kernel(ids, vel, dens, other_vel, other_dens, *outs):
    for out, start in zip(outs, (ids[2], ids[6], ids[5], ids[4])):
        mine = serves_upper(start, ids)

        @pl.when(mine)
        def _():
            out[0] = vel[...]
            out[1] = dens[...]

        @pl.when(jnp.logical_not(mine))
        def _():
            out[0] = other_vel[...]
            out[1] = other_dens[...]


def window_pick(ids):
    ring, _ = ring_of(ids)
    first, offset = ids[2] >> 6, ids[2] & 63
    want = lax.broadcasted_iota(jnp.int32, (COLS, TILE), 0) + offset
    within = lax.broadcasted_iota(jnp.int32, (COLS, TILE), 1)
    picks = [jnp.where(within + ((ring - s - first) & 3) * TILE == want, 1.0, 0.0) for s in range(4)]
    return jnp.concatenate(picks, axis=1).astype(BF16)


def window_dens_kernel(ids, t0, t1, t2, t3, dens_out, core_out, cross_out, wide):
    parity = ids[0] & 1
    pick = window_pick(ids)
    for s, tile in enumerate((t0, t1, t2, t3)):
        wide[:, s * TILE : (s + 1) * TILE, :] = tile[1]
    for r in range(ROWS):
        dens_out[r] = jnp.dot(pick, wide[r], preferred_element_type=F32)
    core_out[...] = dens_out[pl.ds(pl.multiple_of((1 - parity) * 4, 4), 4)].astype(BF16)
    cross_out[...] = dens_out[pl.ds(pl.multiple_of(parity * 4, 4), 4)].astype(BF16)


def coef_kernel(ids, t0, t1, t2, t3, dens, depth_w, cols_w, coef, s1, s2, logs, wide):
    pick = window_pick(ids)
    for s, tile in enumerate((t0, t1, t2, t3)):
        wide[:, s * TILE : (s + 1) * TILE, :] = tile[0]
    for r in range(ROWS):
        speed = jnp.dot(pick, wide[r], preferred_element_type=F32)
        c = speed * speed
        coef[r] = c * LAP_SCALE
        log = jnp.log(dens[r])
        logs[r] = log
        high, low = halves(log)
        cs = c * (SLOPE_SCALE * SLOPE_SCALE)
        s1[r] = cs * (
            jnp.dot(cols_w[COLS:], high, preferred_element_type=F32)
            + jnp.dot(cols_w[COLS:], low, preferred_element_type=F32)
        )
        s2[r] = cs * (
            jnp.dot(high, depth_w[:, DEPTH:], preferred_element_type=F32)
            + jnp.dot(low, depth_w[:, DEPTH:], preferred_element_type=F32)
        )


def row_slope_kernel(ids, logs, core, cross, coef, s0, ext):
    parity, place = ids[0] & 1, ids[0]
    pad = jnp.where((place == 0) | (place == 15), 1.0, 0.0).astype(F32)
    load_extended(ext, logs, parity, jnp.log(core[...].astype(F32)), jnp.log(cross[...].astype(F32) + pad))

    def body(i, carry):
        at = pl.ds(pl.multiple_of(i * 8, 8), 8)
        e = [ext[r, at, :] for r in range(16)]
        for r in range(ROWS):
            d0 = SLOPE[0] * (e[r + 5] - e[r + 3])
            for k in range(2, 5):
                d0 += SLOPE[k - 1] * (e[r + 4 + k] - e[r + 4 - k])
            s0[r, at, :] = (coef[r, at, :] * (SLOPE_SCALE * SLOPE_SCALE / LAP_SCALE)) * d0
        return carry

    lax.fori_loop(0, COLS // 8, body, 0)


def step_kernel(mode, first, moment, *refs):
    refs = list(refs)
    ids = refs.pop(0)
    amount = refs.pop(0) if mode == "fwd" else None
    prev, now, core, cross = refs[:4]
    refs = refs[4:]
    which = 0 if mode == "fwd" else 1
    if first:
        own = refs.pop(0)
    else:
        qr_now, qr_prev, qs_now, qs_prev = refs[:4]
        refs = refs[4:]
    plane = refs.pop(0) if mode == "bwd" else None
    coef, s0, s1, s2, depth_w, cols_w = refs[:6]
    refs = refs[6:]
    out = refs.pop(0)
    last = len(refs) == 3
    if not last:
        core_out, cross_out, qr_out, qs_out = refs[:4]
        refs = refs[4:]
    ext, zz, cc = refs
    parity = ids[0] & 1
    if first:
        load_extended(ext, now, parity, core[which], cross[which, :4].astype(F32))
        ext[12 * parity + 3 - 3 * parity] += cross[which, 4].astype(F32)
    else:
        seen = (2.0 * qr_now[...] - qr_prev[...]) + cross[...].astype(F32)
        load_extended(ext, now, parity, core[...], seen)
    if not last:
        qr_out[...] = ext[pl.ds(pl.multiple_of(parity * 12, 4), 4)]
    in_plane(ext, depth_w, cols_w, zz, cc)

    def body(i, carry):
        at = pl.ds(pl.multiple_of(i * 8, 8), 8)
        at2 = pl.ds(pl.multiple_of(COLS + i * 8, 8), 8)
        e = [ext[r, at, :] for r in range(16)]
        for r in range(ROWS):
            mid = e[r + 4]
            lap = (3.0 * LAP[0]) * mid + (cc[r, at, :] + zz[r, at, :DEPTH])
            d0 = None
            for k in range(1, 5):
                hi, lo = e[r + 4 + k], e[r + 4 - k]
                lap += LAP[k] * (hi + lo)
                term = SLOPE[k - 1] * (hi - lo)
                d0 = term if d0 is None else d0 + term
            drift = s0[r, at, :] * d0 + s1[r, at, :] * cc[r, at2, :] + s2[r, at, :] * zz[r, at, DEPTH:]
            new = 2.0 * mid - prev[r, at, :] + (coef[r, at, :] * lap - drift)
            if mode == "bwd":
                out[r, at, :128] = new[:, :128] + plane[moment, r, at, :]
                out[r, at, 128:] = new[:, 128:]
            else:
                out[r, at, :] = new
        return carry

    lax.fori_loop(0, COLS // 8, body, 0)

    if mode == "fwd":

        line = ids[3] >> 8
        row = lax.div(line, COLS) - ids[0] * ROWS

        @pl.when((row >= 0) & (row < ROWS))
        def _():
            col = lax.rem(line, COLS)
            base = pl.multiple_of(col & ~7, 8)
            col_in = lax.broadcasted_iota(jnp.int32, (8, DEPTH), 0)
            depth_in = lax.broadcasted_iota(jnp.int32, (8, DEPTH), 1)
            struck = (col_in == (col & 7)) & (depth_in == (ids[3] & 255))
            out[row, pl.ds(base, 8), :] += jnp.where(struck, amount[moment], 0.0)

    if not last:
        core_out[...] = out[pl.ds(pl.multiple_of((1 - parity) * 4, 4), 4)]
        rows = out[pl.ds(pl.multiple_of(parity * 4, 4), 4)]
        if first:
            base = own[...]
        else:
            base = 2.0 * qs_now[...] - qs_prev[...]
        sent = (rows - base).astype(BF16)
        cross_out[...] = sent
        qs_out[...] = base + sent.astype(F32)


def step(mode, moment, ids, source, prev, now, core, cross, quant, planes, fields, tables):
    first, last = moment == 0, moment == STEPS - 1
    args = [ids]
    if mode == "fwd":
        args.append(source)
    args += [prev, now, core, cross] + list(quant)
    if mode == "bwd":
        args.append(planes)
    args += list(fields) + list(tables)
    outs = [(SLAB, F32)]
    if not last:
        outs += [(FACE, F32), (FACE, BF16), (FACE, F32), (FACE, F32)]
    scratch = [
        pltpu.VMEM((ROWS + 8, COLS, DEPTH), F32),
        pltpu.VMEM((ROWS, COLS, 2 * DEPTH), F32),
        pltpu.VMEM((ROWS, 2 * COLS, DEPTH), F32),
    ]
    return call(functools.partial(step_kernel, mode, first, moment), args, outs, scratch, "step_" + mode)


def blocks_kernel(ids, part, a5, s0, a0, s5, b0, b1, b2, b3):
    ring, _ = ring_of(ids)
    first, offset = ids[2] >> 6, ids[2] & 63
    within = lax.broadcasted_iota(jnp.int32, (TILE, COLS), 0)
    column = lax.broadcasted_iota(jnp.int32, (TILE, COLS), 1) + offset
    picks = [jnp.where(within + ((ring + s - first) & 3) * TILE == column, 1.0, 0.0) for s in range(4)]
    pick = jnp.concatenate(picks, axis=0).astype(BF16)
    for r in range(ROWS):
        total = part[r] + a5[r] * s0[r] + a0[r] * s5[r]
        high, low = halves(total)
        placed = jnp.dot(pick, high, preferred_element_type=F32) + jnp.dot(
            pick, low, preferred_element_type=F32
        )
        for s, block in enumerate((b0, b1, b2, b3)):
            block[r] = placed[s * TILE : (s + 1) * TILE]


def combine_kernel(ids, b0, b1, b2, b3, keep, give):
    flags = [jnp.where(serves_upper(ids[i], ids), 1.0, 0.0).astype(F32) for i in (2, 4, 5, 6)]
    for r in range(ROWS):
        kept = flags[0] * b0[r]
        total = b0[r]
        for flag, block in zip(flags[1:], (b1, b2, b3)):
            kept += flag * block[r]
            total += block[r]
        keep[r] = kept
        gave = (1.0 - flags[0]) * b0[r]
        for flag, block in zip(flags[1:], (b1, b2, b3)):
            gave += (1.0 - flag) * block[r]
        give[r] = gave


def shards(
    forward_prev,
    forward_now,
    adjoint_prev,
    adjoint_now,
    velocity,
    density,
    anchors,
    shot_cell,
    wavelet,
    records,
):
    tables = weight_tables()
    place = lax.axis_index("apert")
    shot = lax.axis_index("shot")
    count = lax.axis_size("apert")
    groups = lax.axis_size("shot")
    half = groups // 2
    ids = jnp.stack([place, shot]).astype(jnp.int32)
    core_pairs = [(i, i ^ 1) for i in range(count)]
    cross_pairs = [(i, i + 1) for i in range(1, count - 1, 2)] + [(i + 1, i) for i in range(1, count - 1, 2)]
    side_pairs = [(i, (i + half) % groups) for i in range(groups)]

    def ring_pairs(shift):
        return [(i, (i // half) * half + (i % half + shift) % half) for i in range(groups)]

    def swap(core, cross):
        return lax.ppermute(core, "apert", core_pairs), lax.ppermute(cross, "apert", cross_pairs)

    both_ways = [
        (i * count + j, ((i // half) * half + (i % half + (1 if j % 2 == 0 else -1)) % half) * count + j)
        for i in range(groups)
        for j in range(count)
    ]

    def ring_send(pieces):
        halfway = lax.ppermute(pieces[2], ("shot", "apert"), both_ways)
        near = lax.ppermute(pieces[1], "shot", ring_pairs(1)), lax.ppermute(pieces[3], "shot", ring_pairs(3))
        return [pieces[0], near[0], lax.ppermute(halfway, ("shot", "apert"), both_ways), near[1]]

    starts = [lax.ppermute(anchors, "shot", ring_pairs(k)) for k in range(1, half)]
    other_vel = lax.ppermute(velocity, "shot", side_pairs)
    other_dens = lax.ppermute(density, "shot", side_pairs)
    fwd_prev, fwd_now, bwd_prev, bwd_now = forward_prev[0], forward_now[0], adjoint_prev[0], adjoint_now[0]
    pair = ((2,) + FACE, F32)
    tile = ((ROWS, TILE, DEPTH), BF16)
    core_faces, cross_faces, own_fwd, own_bwd, vel, dens = call(
        faces_kernel,
        [ids, fwd_now, bwd_now, velocity, density],
        [pair, ((2, 5, COLS, DEPTH), BF16), (FACE, F32), (FACE, F32), tile, tile],
        name="faces",
    )
    nums = jnp.concatenate([ids, anchors, shot_cell, *starts])
    tile2 = ((2, ROWS, TILE, DEPTH), BF16)
    tiles = call(select_kernel, [nums, vel, dens, other_vel, other_dens], [tile2] * half, name="select")
    tiles = ring_send(tiles)
    first_core, first_cross = swap(core_faces, cross_faces)

    wide = [pltpu.VMEM((ROWS, 4 * TILE, DEPTH), BF16)]
    dens, dens_core, dens_cross = call(
        window_dens_kernel, [nums, *tiles], [(SLAB, F32), (FACE, BF16), (FACE, BF16)], wide, "window_dens"
    )
    dens_core, dens_cross = swap(dens_core, dens_cross)
    coef, slope1, slope2, logs = call(
        coef_kernel, [nums, *tiles, dens, *tables], [(SLAB, F32)] * 4, wide, "coef"
    )
    (slope0,) = call(
        row_slope_kernel,
        [ids, logs, dens_core, dens_cross, coef],
        [(SLAB, F32)],
        [pltpu.VMEM((ROWS + 8, COLS, DEPTH), F32)],
        "row_slope",
    )
    fields = (coef, slope0, slope1, slope2)
    lane = lax.broadcasted_iota(jnp.int32, (1, 1, 1, 128), 3)
    planes = jnp.where(lane == SURF, records[0][..., None], 0.0)
    source = wavelet[0]

    fwd_core = bwd_core = first_core
    fwd_cross = bwd_cross = first_cross
    fwd_quant, bwd_quant = (own_fwd,), (own_bwd,)
    snapshots, states = [], []
    for moment in range(STEPS):
        last = moment == STEPS - 1
        if moment > 0:
            fwd_core, fwd_cross = swap(fwd_core, fwd_cross)
        new, *sent = step(
            "fwd", moment, nums, source, fwd_prev, fwd_now, fwd_core, fwd_cross, fwd_quant, None, fields, tables
        )
        if not last:
            own = own_fwd if moment == 0 else fwd_quant[2]
            fwd_core, fwd_cross, seen, shown = sent
            fwd_quant = (seen, seen if moment == 0 else fwd_quant[0], shown, own)
        snapshots.append(new)
        fwd_prev, fwd_now = fwd_now, new

        if moment > 0:
            bwd_core, bwd_cross = swap(bwd_core, bwd_cross)
        new, *sent = step(
            "bwd", moment, nums, source, bwd_prev, bwd_now, bwd_core, bwd_cross, bwd_quant, planes, fields, tables
        )
        if not last:
            own = own_bwd if moment == 0 else bwd_quant[2]
            bwd_core, bwd_cross, seen, shown = sent
            bwd_quant = (seen, seen if moment == 0 else bwd_quant[0], shown, own)
        states.append(new)
        bwd_prev, bwd_now = bwd_now, new
    part = sum(states[t] * snapshots[STEPS - 1 - t] for t in range(1, STEPS - 1))

    block = ((ROWS, TILE, DEPTH), F32)
    blocks = call(
        blocks_kernel,
        [nums, part, states[STEPS - 1], snapshots[0], states[0], snapshots[STEPS - 1]],
        [block] * half,
        name="blocks",
    )
    arrived = ring_send(blocks)
    keep, give = call(combine_kernel, [nums, *arrived], [block] * 2, name="combine")
    image = keep + lax.ppermute(give, "shot", side_pairs)
    return image, states[STEPS - 1][None]


def solution(mesh):
    placed = (
        P("shot", "apert", None, None),
        P("shot", "apert", None, None),
        P("shot", "apert", None, None),
        P("shot", "apert", None, None),
        P("apert", "shot", None),
        P("apert", "shot", None),
        P("shot"),
        P("shot"),
        P("shot", None),
        P("shot", None, "apert", None),
    )
    return jax.shard_map(
        shards,
        mesh=mesh,
        in_specs=placed,
        out_specs=(P("apert", "shot", None), P("shot", "apert", None, None)),
        check_vma=False,
    )
```

```python
import functools

import jax
import jax.numpy as jnp
import ml_dtypes
import numpy as np
from jax import lax
from jax.experimental import pallas as pl
from jax.experimental.pallas import tpu as pltpu
from jax.sharding import PartitionSpec as P

STEPS = 6
SURF = 8
ROWS, COLS, DEPTH = 8, 160, 256
TILE = 64
LAP = (-14350.0, 8064.0, -1008.0, 128.0, -9.0)
SLOPE = (672.0, -168.0, 32.0, -3.0)
LAP_SCALE, SLOPE_SCALE = 1.0 / 5040.0, 1.0 / 840.0
F32, BF16 = jnp.float32, jnp.bfloat16
VMEM = pl.BlockSpec(memory_space=pltpu.VMEM)
SMEM = pl.BlockSpec(memory_space=pltpu.SMEM)
PARAMS = pltpu.CompilerParams(vmem_limit_bytes=16 * 1024 * 1024)


def banded(size):
    lap, slope = np.zeros((size, size)), np.zeros((size, size))
    for k in range(1, 5):
        lap += LAP[k] * (np.eye(size, k=k) + np.eye(size, k=-k))
        slope += SLOPE[k - 1] * (np.eye(size, k=k) - np.eye(size, k=-k))
    return lap, slope


def weight_tables():
    lap, slope = banded(DEPTH)
    depth_table = np.concatenate([lap.T, slope.T], axis=1).astype(ml_dtypes.bfloat16)
    lap, slope = banded(COLS)
    cols_table = np.concatenate([lap, slope], axis=0).astype(ml_dtypes.bfloat16)
    return jnp.asarray(depth_table), jnp.asarray(cols_table)


def halves(x):
    high = x.astype(BF16)
    return high, (x - high.astype(F32)).astype(BF16)


def load_halo(halo, parity, core_rows, cross_rows):
    halo[pl.ds(pl.multiple_of((1 - parity) * 4, 4), 4)] = core_rows
    halo[pl.ds(pl.multiple_of(parity * 4, 4), 4)] = cross_rows


def extended_rows(halo, mid, first, count, at):
    rows = {}
    for r in range(first - 4, first + count + 4):
        if r < 0:
            rows[r] = halo[r + 4, at, :]
        elif r < ROWS:
            rows[r] = mid[r, at, :]
        else:
            rows[r] = halo[r - ROWS + 4, at, :]
    return rows


def row_slope_of(rows, r):
    total = None
    for k in range(1, 5):
        term = SLOPE[k - 1] * (rows[r + k] - rows[r - k])
        total = term if total is None else total + term
    return total


def call(body, args, outs, scratch=(), name=None, flops=20_000_000_000):
    specs, given = [], []
    for arg in args:
        if arg.ndim == 1:
            specs.append(SMEM)
            given.append(arg)
        else:
            specs.append(VMEM)
            given.append(pltpu.with_memory_space_constraint(arg, pltpu.VMEM))
    return pl.pallas_call(
        body,
        out_shape=[pltpu.VMEM(shape, dtype) for shape, dtype in outs],
        in_specs=specs,
        out_specs=[VMEM] * len(outs),
        scratch_shapes=list(scratch),
        compiler_params=PARAMS,
        cost_estimate=pl.CostEstimate(flops=flops, bytes_accessed=100_000, transcendentals=0),
        name=name,
    )(*given)


SLAB, FACE = (ROWS, COLS, DEPTH), (4, COLS, DEPTH)


def ring_of(ids):
    return ids[1] & 3, ids[1] >> 2


def serves_upper(start, ids):
    ring, upper = ring_of(ids)
    first = start >> 6
    return ((first + ((ring - first) & 3)) >> 2) == upper


def faces_kernel(ids, fwd, bwd, vel, dens, core, cross, own_fwd, own_bwd, vel_out, dens_out):
    parity = ids[0] & 1
    for f, (field, own) in enumerate(((fwd, own_fwd), (bwd, own_bwd))):
        core[f] = field[pl.ds(pl.multiple_of((1 - parity) * 4, 4), 4)]
        own[...] = field[pl.ds(pl.multiple_of(parity * 4, 4), 4)]
        high = own[...].astype(BF16)
        cross[f, :4] = high
        near = parity * 3
        low = (own[near] - own[near].astype(BF16).astype(F32)).astype(BF16)
        cross[f, 4] = low
        own[...] = high.astype(F32)
        own[near] += low.astype(F32)
    vel_out[...] = vel[...]
    dens_out[...] = dens[...]


def select_kernel(ids, own, other, *outs):
    for out, start in zip(outs, (ids[2], ids[6], ids[5], ids[4])):
        mine = serves_upper(start, ids)

        @pl.when(mine)
        def _():
            out[...] = own[...]

        @pl.when(jnp.logical_not(mine))
        def _():
            out[...] = other[...]


def window_pick(ids):
    ring, _ = ring_of(ids)
    first, offset = ids[2] >> 6, ids[2] & 63
    want = lax.broadcasted_iota(jnp.int32, (COLS, TILE), 0) + offset
    within = lax.broadcasted_iota(jnp.int32, (COLS, TILE), 1)
    picks = [jnp.where(within + ((ring - s - first) & 3) * TILE == want, 1.0, 0.0) for s in range(4)]
    return jnp.concatenate(picks, axis=1).astype(BF16)


def window_dens_kernel(ids, t0, t1, t2, t3, dens_out, core_out, cross_out, wide):
    parity = ids[0] & 1
    pick = window_pick(ids)
    for s, tile in enumerate((t0, t1, t2, t3)):
        wide[:, s * TILE : (s + 1) * TILE, :] = tile[...]
    for r in range(ROWS):
        dens_out[r] = jnp.dot(pick, wide[r], preferred_element_type=F32)
    core_out[...] = dens_out[pl.ds(pl.multiple_of((1 - parity) * 4, 4), 4)].astype(BF16)
    cross_out[...] = dens_out[pl.ds(pl.multiple_of(parity * 4, 4), 4)].astype(BF16)


def coef_kernel(ids, t0, t1, t2, t3, dens, depth_w, cols_w, coef, s1, s2, logs, wide):
    pick = window_pick(ids)
    for s, tile in enumerate((t0, t1, t2, t3)):
        wide[:, s * TILE : (s + 1) * TILE, :] = tile[...]
    for r in range(ROWS):
        speed = jnp.dot(pick, wide[r], preferred_element_type=F32)
        c = speed * speed
        coef[r] = c * LAP_SCALE
        log = jnp.log(dens[r])
        logs[r] = log
        high, low = halves(log)
        cs = c * (SLOPE_SCALE * SLOPE_SCALE)
        s1[r] = cs * (
            jnp.dot(cols_w[COLS:], high, preferred_element_type=F32)
            + jnp.dot(cols_w[COLS:], low, preferred_element_type=F32)
        )
        s2[r] = cs * (
            jnp.dot(high, depth_w[:, DEPTH:], preferred_element_type=F32)
            + jnp.dot(low, depth_w[:, DEPTH:], preferred_element_type=F32)
        )


def row_slope_kernel(ids, logs, core, cross, coef, s0, halo):
    parity, place = ids[0] & 1, ids[0]
    pad = jnp.where((place == 0) | (place == 15), 1.0, 0.0).astype(F32)
    load_halo(halo, parity, jnp.log(core[...].astype(F32)), jnp.log(cross[...].astype(F32) + pad))

    def body(i, carry):
        at = pl.ds(pl.multiple_of(i * 8, 8), 8)
        rows = extended_rows(halo, logs, 0, ROWS, at)
        for r in range(ROWS):
            s0[r, at, :] = (coef[r, at, :] * (SLOPE_SCALE * SLOPE_SCALE / LAP_SCALE)) * row_slope_of(rows, r)
        return carry

    lax.fori_loop(0, COLS // 8, body, 0)


def step_kernel(mode, first, moment, *refs):
    refs = list(refs)
    ids = refs.pop(0)
    amount = refs.pop(0) if mode == "fwd" else None
    prev, now, core, cross = refs[:4]
    refs = refs[4:]
    which = 0 if mode == "fwd" else 1
    if first:
        own = refs.pop(0)
    else:
        qr_now, qr_prev, qs_now, qs_prev = refs[:4]
        refs = refs[4:]
    plane = refs.pop(0) if mode == "bwd" else None
    coef, s0, s1, s2, depth_w, cols_w = refs[:6]
    refs = refs[6:]
    out = refs.pop(0)
    last = len(refs) == 3
    if not last:
        core_out, cross_out, qr_out, qs_out = refs[:4]
        refs = refs[4:]
    halo, zz, cc = refs
    parity = ids[0] & 1
    if first:
        load_halo(halo, parity, core[which], cross[which, :4].astype(F32))
        halo[3 + parity] += cross[which, 4].astype(F32)
    else:
        seen = (2.0 * qr_now[...] - qr_prev[...]) + cross[...].astype(F32)
        load_halo(halo, parity, core[...], seen)
    if not last:
        qr_out[...] = halo[pl.ds(pl.multiple_of(parity * 4, 4), 4)]

    def products(r):
        high, low = halves(now[r])
        zz[r] = jnp.dot(high, depth_w[...], preferred_element_type=F32) + jnp.dot(
            low, depth_w[...], preferred_element_type=F32
        )
        cc[r] = jnp.dot(cols_w[...], high, preferred_element_type=F32) + jnp.dot(
            cols_w[...], low, preferred_element_type=F32
        )

    def update(first_row, i):
        at = pl.ds(i * 8, 8)
        at2 = pl.ds(COLS + i * 8, 8)
        rows = extended_rows(halo, now, first_row, 2, at)
        for r in (first_row, first_row + 1):
            lap = (3.0 * LAP[0]) * rows[r] + (cc[r, at, :] + zz[r, at, :DEPTH])
            for k in range(1, 5):
                lap += LAP[k] * (rows[r + k] + rows[r - k])
            drift = (
                s0[r, at, :] * row_slope_of(rows, r)
                + s1[r, at, :] * cc[r, at2, :]
                + s2[r, at, :] * zz[r, at, DEPTH:]
            )
            new = 2.0 * rows[r] - prev[r, at, :] + (coef[r, at, :] * lap - drift)
            if mode == "bwd":
                out[r, at, :128] = new[:, :128] + plane[moment, r, at, :]
                out[r, at, 128:] = new[:, 128:]
            else:
                out[r, at, :] = new

    for r in range(0, ROWS + 2, 2):
        if r < ROWS:
            products(r)
            products(r + 1)
        if r > 0:
            for i in range(COLS // 8):
                update(r - 2, i)

    if mode == "fwd":

        line = ids[3] >> 8
        row = lax.div(line, COLS) - ids[0] * ROWS

        @pl.when((row >= 0) & (row < ROWS))
        def _():
            col = lax.rem(line, COLS)
            base = pl.multiple_of(col & ~7, 8)
            col_in = lax.broadcasted_iota(jnp.int32, (8, DEPTH), 0)
            depth_in = lax.broadcasted_iota(jnp.int32, (8, DEPTH), 1)
            struck = (col_in == (col & 7)) & (depth_in == (ids[3] & 255))
            out[row, pl.ds(base, 8), :] += jnp.where(struck, amount[moment], 0.0)

    if not last:
        core_out[...] = out[pl.ds(pl.multiple_of((1 - parity) * 4, 4), 4)]
        rows = out[pl.ds(pl.multiple_of(parity * 4, 4), 4)]
        if first:
            base = own[...]
        else:
            base = 2.0 * qs_now[...] - qs_prev[...]
        sent = (rows - base).astype(BF16)
        cross_out[...] = sent
        qs_out[...] = base + sent.astype(F32)


def step(mode, moment, ids, source, prev, now, core, cross, quant, planes, fields, tables):
    first, last = moment == 0, moment == STEPS - 1
    args = [ids]
    if mode == "fwd":
        args.append(source)
    args += [prev, now, core, cross] + list(quant)
    if mode == "bwd":
        args.append(planes)
    args += list(fields) + list(tables)
    outs = [(SLAB, F32)]
    if not last:
        outs += [(FACE, F32), (FACE, BF16), (FACE, F32), (FACE, F32)]
    scratch = [
        pltpu.VMEM((8, COLS, DEPTH), F32),
        pltpu.VMEM((ROWS, COLS, 2 * DEPTH), F32),
        pltpu.VMEM((ROWS, 2 * COLS, DEPTH), F32),
    ]
    return call(functools.partial(step_kernel, mode, first, moment), args, outs, scratch, "step_" + mode)


def blocks_kernel(ids, part, a5, s0, a0, s5, *blocks):
    ring, _ = ring_of(ids)
    first, offset = ids[2] >> 6, ids[2] & 63
    within = lax.broadcasted_iota(jnp.int32, (TILE, COLS), 0)
    column = lax.broadcasted_iota(jnp.int32, (TILE, COLS), 1) + offset
    picks = [jnp.where(within + ((ring + s - first) & 3) * TILE == column, 1.0, 0.0) for s in range(4)]
    pick = jnp.concatenate(picks, axis=0).astype(BF16)
    for r in range(ROWS):
        total = part[r] + a5[r] * s0[r] + a0[r] * s5[r]
        high, low = halves(total)
        placed = jnp.dot(pick, high, preferred_element_type=F32) + jnp.dot(
            pick, low, preferred_element_type=F32
        )
        for s in range(4):
            blocks[r // 4 * 4 + s][r % 4] = placed[s * TILE : (s + 1) * TILE]


def combine_kernel(ids, b0, b1, b2, b3, keep, give):
    flags = [jnp.where(serves_upper(ids[i], ids), 1.0, 0.0).astype(F32) for i in (2, 4, 5, 6)]
    for r in range(ROWS // 2):
        kept = flags[0] * b0[r]
        total = b0[r]
        for flag, block in zip(flags[1:], (b1, b2, b3)):
            kept += flag * block[r]
            total += block[r]
        keep[r] = kept
        gave = (1.0 - flags[0]) * b0[r]
        for flag, block in zip(flags[1:], (b1, b2, b3)):
            gave += (1.0 - flag) * block[r]
        give[r] = gave


def shards(
    forward_prev,
    forward_now,
    adjoint_prev,
    adjoint_now,
    velocity,
    density,
    anchors,
    shot_cell,
    wavelet,
    records,
):
    tables = weight_tables()
    place = lax.axis_index("apert")
    shot = lax.axis_index("shot")
    count = lax.axis_size("apert")
    groups = lax.axis_size("shot")
    half = groups // 2
    ids = jnp.stack([place, shot]).astype(jnp.int32)
    core_pairs = [(i, i ^ 1) for i in range(count)]
    cross_pairs = [(i, i + 1) for i in range(1, count - 1, 2)] + [(i + 1, i) for i in range(1, count - 1, 2)]
    side_pairs = [(i, (i + half) % groups) for i in range(groups)]

    def ring_pairs(shift):
        return [(i, (i // half) * half + (i % half + shift) % half) for i in range(groups)]

    def swap(core, cross):
        return lax.ppermute(core, "apert", core_pairs), lax.ppermute(cross, "apert", cross_pairs)

    both_ways = [
        (i * count + j, ((i // half) * half + (i % half + (1 if j % 2 == 0 else -1)) % half) * count + j)
        for i in range(groups)
        for j in range(count)
    ]

    def ring_send(pieces):
        halfway = lax.ppermute(pieces[2], ("shot", "apert"), both_ways)
        near = lax.ppermute(pieces[1], "shot", ring_pairs(1)), lax.ppermute(pieces[3], "shot", ring_pairs(3))
        return [pieces[0], near[0], lax.ppermute(halfway, ("shot", "apert"), both_ways), near[1]]

    starts = [lax.ppermute(anchors, "shot", ring_pairs(k)) for k in range(1, half)]
    other_dens = lax.ppermute(density, "shot", side_pairs)
    other_vel = lax.ppermute(velocity, "shot", side_pairs)
    fwd_prev, fwd_now, bwd_prev, bwd_now = forward_prev[0], forward_now[0], adjoint_prev[0], adjoint_now[0]
    pair = ((2,) + FACE, F32)
    tile = ((ROWS, TILE, DEPTH), BF16)
    core_faces, cross_faces, own_fwd, own_bwd, vel, dens = call(
        faces_kernel,
        [ids, fwd_now, bwd_now, velocity, density],
        [pair, ((2, 5, COLS, DEPTH), BF16), (FACE, F32), (FACE, F32), tile, tile],
        name="faces",
    )
    nums = jnp.concatenate([ids, anchors, shot_cell, *starts])
    dens_tiles = ring_send(call(select_kernel, [nums, dens, other_dens], [tile] * half, name="select_dens"))
    vel_tiles = ring_send(call(select_kernel, [nums, vel, other_vel], [tile] * half, name="select_vel"))
    first_core, first_cross = swap(core_faces, cross_faces)

    wide = [pltpu.VMEM((ROWS, 4 * TILE, DEPTH), BF16)]
    dens, dens_core, dens_cross = call(
        window_dens_kernel, [nums, *dens_tiles], [(SLAB, F32), (FACE, BF16), (FACE, BF16)], wide, "window_dens"
    )
    dens_core, dens_cross = swap(dens_core, dens_cross)
    coef, slope1, slope2, logs = call(
        coef_kernel, [nums, *vel_tiles, dens, *tables], [(SLAB, F32)] * 4, wide, "coef"
    )
    (slope0,) = call(
        row_slope_kernel,
        [ids, logs, dens_core, dens_cross, coef],
        [(SLAB, F32)],
        [pltpu.VMEM((8, COLS, DEPTH), F32)],
        "row_slope",
    )
    fields = (coef, slope0, slope1, slope2)
    lane = lax.broadcasted_iota(jnp.int32, (1, 1, 1, 128), 3)
    planes = jnp.where(lane == SURF, records[0][..., None], 0.0)
    source = wavelet[0]

    fwd_core = bwd_core = first_core
    fwd_cross = bwd_cross = first_cross
    fwd_quant, bwd_quant = (own_fwd,), (own_bwd,)
    snapshots, states = [], []
    for moment in range(STEPS):
        last = moment == STEPS - 1
        if moment > 0:
            fwd_core, fwd_cross = swap(fwd_core, fwd_cross)
        new, *sent = step(
            "fwd", moment, nums, source, fwd_prev, fwd_now, fwd_core, fwd_cross, fwd_quant, None, fields, tables
        )
        if not last:
            own = own_fwd if moment == 0 else fwd_quant[2]
            fwd_core, fwd_cross, seen, shown = sent
            fwd_quant = (seen, seen if moment == 0 else fwd_quant[0], shown, own)
        snapshots.append(new)
        fwd_prev, fwd_now = fwd_now, new

        if moment > 0:
            bwd_core, bwd_cross = swap(bwd_core, bwd_cross)
        new, *sent = step(
            "bwd", moment, nums, source, bwd_prev, bwd_now, bwd_core, bwd_cross, bwd_quant, planes, fields, tables
        )
        if not last:
            own = own_bwd if moment == 0 else bwd_quant[2]
            bwd_core, bwd_cross, seen, shown = sent
            bwd_quant = (seen, seen if moment == 0 else bwd_quant[0], shown, own)
        states.append(new)
        bwd_prev, bwd_now = bwd_now, new
    part = sum(states[t] * snapshots[STEPS - 1 - t] for t in range(1, STEPS - 1))

    block = ((ROWS // 2, TILE, DEPTH), F32)
    blocks = call(
        blocks_kernel,
        [nums, part, states[STEPS - 1], snapshots[0], states[0], snapshots[STEPS - 1]],
        [block] * (2 * half),
        name="blocks",
    )
    arrived = [ring_send(blocks[:half]), ring_send(blocks[half:])]
    rows = []
    for each in arrived:
        keep, give = call(combine_kernel, [nums, *each], [block] * 2, name="combine")
        rows.append(keep + lax.ppermute(give, "shot", side_pairs))
    image = jnp.concatenate(rows, axis=0)
    return image, states[STEPS - 1][None]


def solution(mesh):
    placed = (
        P("shot", "apert", None, None),
        P("shot", "apert", None, None),
        P("shot", "apert", None, None),
        P("shot", "apert", None, None),
        P("apert", "shot", None),
        P("apert", "shot", None),
        P("shot"),
        P("shot"),
        P("shot", None),
        P("shot", None, "apert", None),
    )
    return jax.shard_map(
        shards,
        mesh=mesh,
        in_specs=placed,
        out_specs=(P("apert", "shot", None), P("shot", "apert", None, None)),
        check_vma=False,
    )
```

```python
import functools

import jax
import jax.numpy as jnp
import ml_dtypes
import numpy as np
from jax import lax
from jax.experimental import pallas as pl
from jax.experimental.pallas import tpu as pltpu
from jax.sharding import PartitionSpec as P

STEPS = 6
SURF = 8
ROWS, COLS, DEPTH = 8, 160, 256
TILE = 64
LAP = (-14350.0, 8064.0, -1008.0, 128.0, -9.0)
SLOPE = (672.0, -168.0, 32.0, -3.0)
LAP_SCALE, SLOPE_SCALE = 1.0 / 5040.0, 1.0 / 840.0
F32, BF16 = jnp.float32, jnp.bfloat16
VMEM = pl.BlockSpec(memory_space=pltpu.VMEM)
SMEM = pl.BlockSpec(memory_space=pltpu.SMEM)
PARAMS = pltpu.CompilerParams(vmem_limit_bytes=16 * 1024 * 1024)


def banded(size):
    lap, slope = np.zeros((size, size)), np.zeros((size, size))
    for k in range(1, 5):
        lap += LAP[k] * (np.eye(size, k=k) + np.eye(size, k=-k))
        slope += SLOPE[k - 1] * (np.eye(size, k=k) - np.eye(size, k=-k))
    return lap, slope


def weight_tables():
    lap, slope = banded(DEPTH)
    depth_table = np.concatenate([lap.T, slope.T], axis=1).astype(ml_dtypes.bfloat16)
    lap, slope = banded(COLS)
    cols_table = np.concatenate([lap, slope], axis=0).astype(ml_dtypes.bfloat16)
    return jnp.asarray(depth_table), jnp.asarray(cols_table)


def halves(x):
    high = x.astype(BF16)
    return high, (x - high.astype(F32)).astype(BF16)


def load_halo(halo, parity, core_rows, cross_rows):
    halo[pl.ds(pl.multiple_of((1 - parity) * 4, 4), 4)] = core_rows
    halo[pl.ds(pl.multiple_of(parity * 4, 4), 4)] = cross_rows


def extended_rows(halo, mid, first, count, at):
    rows = {}
    for r in range(first - 4, first + count + 4):
        if r < 0:
            rows[r] = halo[r + 4, at, :]
        elif r < ROWS:
            rows[r] = mid[r, at, :]
        else:
            rows[r] = halo[r - ROWS + 4, at, :]
    return rows


def row_slope_of(rows, r):
    total = None
    for k in range(1, 5):
        term = SLOPE[k - 1] * (rows[r + k] - rows[r - k])
        total = term if total is None else total + term
    return total


def call(body, args, outs, scratch=(), name=None, flops=10_000_000):
    specs, given = [], []
    for arg in args:
        if arg.ndim == 1:
            specs.append(SMEM)
            given.append(arg)
        else:
            specs.append(VMEM)
            given.append(pltpu.with_memory_space_constraint(arg, pltpu.VMEM))
    return pl.pallas_call(
        body,
        out_shape=[
            jax.ShapeDtypeStruct(shape, dtype) if len(shape) == 1 else pltpu.VMEM(shape, dtype)
            for shape, dtype in outs
        ],
        in_specs=specs,
        out_specs=[SMEM if len(shape) == 1 else VMEM for shape, _ in outs],
        scratch_shapes=list(scratch),
        compiler_params=PARAMS,
        cost_estimate=pl.CostEstimate(flops=flops, bytes_accessed=100_000, transcendentals=0),
        name=name,
    )(*given)


SLAB, FACE = (ROWS, COLS, DEPTH), (4, COLS, DEPTH)


def ring_of(ids):
    return ids[1] & 3, ids[1] >> 2


def serves_upper(start, ids):
    ring, upper = ring_of(ids)
    first = start >> 6
    return ((first + ((ring - first) & 3)) >> 2) == upper


def faces_kernel(ids, fwd, bwd, cross, own_fwd, own_bwd):
    parity = ids[0] & 1
    for f, (field, own) in enumerate(((fwd, own_fwd), (bwd, own_bwd))):
        own[...] = field[pl.ds(pl.multiple_of(parity * 4, 4), 4)]
        high = own[...].astype(BF16)
        cross[f, :4] = high
        near = parity * 3
        low = (own[near] - own[near].astype(BF16).astype(F32)).astype(BF16)
        cross[f, 4] = low
        own[...] = high.astype(F32)
        own[near] += low.astype(F32)


def select_kernel(base, s1, s2, s3, dens, vel, other_dens, other_vel, dens_out, vel_out, nums):
    numbers = [base[i] for i in range(4)] + [s1[0], s2[0], s3[0]]
    for i in range(7):
        nums[i] = numbers[i]
    ring, _ = ring_of(numbers)
    for i, start in enumerate((numbers[2], numbers[4], numbers[5], numbers[6])):
        mine = serves_upper(start, numbers)
        target = (ring - i) & 3

        @pl.when(mine)
        def _():
            dens_out[target] = dens[...]
            vel_out[target] = vel[...]

        @pl.when(jnp.logical_not(mine))
        def _():
            dens_out[target] = other_dens[...]
            vel_out[target] = other_vel[...]


def window_pick(ids):
    first, offset = ids[2] >> 6, ids[2] & 63
    want = lax.broadcasted_iota(jnp.int32, (COLS, TILE), 0) + offset
    within = lax.broadcasted_iota(jnp.int32, (COLS, TILE), 1)
    picks = [jnp.where(within + ((s - first) & 3) * TILE == want, 1.0, 0.0) for s in range(4)]
    return jnp.concatenate(picks, axis=1).astype(BF16)


def window_dens_kernel(ids, tiles, fwd, bwd, dens_out, core_out, cross_out, wide):
    parity = ids[0] & 1
    pick = window_pick(ids)
    for s in range(4):
        wide[:, s * TILE : (s + 1) * TILE, :] = tiles[s]
    for r in range(ROWS):
        dens_out[r] = jnp.dot(pick, wide[r], preferred_element_type=F32)
    for i, field in enumerate((fwd, bwd, dens_out)):
        core_out[i] = field[pl.ds(pl.multiple_of((1 - parity) * 4, 4), 4)]
    cross_out[...] = dens_out[pl.ds(pl.multiple_of(parity * 4, 4), 4)].astype(BF16)


def coef_kernel(ids, tiles, dens, depth_w, cols_w, coef, s1, s2, logs, wide):
    pick = window_pick(ids)
    for s in range(4):
        wide[:, s * TILE : (s + 1) * TILE, :] = tiles[s]
    for r in range(ROWS):
        speed = jnp.dot(pick, wide[r], preferred_element_type=F32)
        c = speed * speed
        coef[r] = c * LAP_SCALE
        log = jnp.log(dens[r])
        logs[r] = log
        high, low = halves(log)
        cs = c * (SLOPE_SCALE * SLOPE_SCALE)
        s1[r] = cs * (
            jnp.dot(cols_w[COLS:], high, preferred_element_type=F32)
            + jnp.dot(cols_w[COLS:], low, preferred_element_type=F32)
        )
        s2[r] = cs * (
            jnp.dot(high, depth_w[:, DEPTH:], preferred_element_type=F32)
            + jnp.dot(low, depth_w[:, DEPTH:], preferred_element_type=F32)
        )


def row_slope_kernel(ids, logs, core, cross, coef, s0, halo):
    parity, place = ids[0] & 1, ids[0]
    pad = jnp.where((place == 0) | (place == 15), 1.0, 0.0).astype(F32)
    load_halo(halo, parity, jnp.log(core[2]), jnp.log(cross[...].astype(F32) + pad))

    def body(i, carry):
        at = pl.ds(pl.multiple_of(i * 8, 8), 8)
        rows = extended_rows(halo, logs, 0, ROWS, at)
        for r in range(ROWS):
            s0[r, at, :] = (coef[r, at, :] * (SLOPE_SCALE * SLOPE_SCALE / LAP_SCALE)) * row_slope_of(rows, r)
        return carry

    lax.fori_loop(0, COLS // 8, body, 0)


def step_kernel(mode, first, moment, *refs):
    refs = list(refs)
    ids = refs.pop(0)
    amount = refs.pop(0) if mode == "fwd" else None
    prev, now, core, cross = refs[:4]
    refs = refs[4:]
    which = 0 if mode == "fwd" else 1
    if first:
        own = refs.pop(0)
    else:
        qr_now, qr_prev, qs_now, qs_prev = refs[:4]
        refs = refs[4:]
    plane = refs.pop(0) if mode == "bwd" else None
    coef, s0, s1, s2, depth_w, cols_w = refs[:6]
    refs = refs[6:]
    out = refs.pop(0)
    last = len(refs) == 3
    if not last:
        core_out, cross_out, qr_out, qs_out = refs[:4]
        refs = refs[4:]
    halo, zz, cc = refs
    parity = ids[0] & 1
    if first:
        load_halo(halo, parity, core[which], cross[which, :4].astype(F32))
        halo[3 + parity] += cross[which, 4].astype(F32)
    else:
        seen = (2.0 * qr_now[...] - qr_prev[...]) + cross[...].astype(F32)
        load_halo(halo, parity, core[...], seen)
    if not last:
        qr_out[...] = halo[pl.ds(pl.multiple_of(parity * 4, 4), 4)]

    def products(r):
        high, low = halves(now[r])
        zz[r] = jnp.dot(high, depth_w[...], preferred_element_type=F32) + jnp.dot(
            low, depth_w[...], preferred_element_type=F32
        )
        cc[r] = jnp.dot(cols_w[...], high, preferred_element_type=F32) + jnp.dot(
            cols_w[...], low, preferred_element_type=F32
        )

    def update(first_row, i):
        at = pl.ds(i * 8, 8)
        at2 = pl.ds(COLS + i * 8, 8)
        rows = extended_rows(halo, now, first_row, 2, at)
        for r in (first_row, first_row + 1):
            lap = (3.0 * LAP[0]) * rows[r] + (cc[r, at, :] + zz[r, at, :DEPTH])
            for k in range(1, 5):
                lap += LAP[k] * (rows[r + k] + rows[r - k])
            drift = (
                s0[r, at, :] * row_slope_of(rows, r)
                + s1[r, at, :] * cc[r, at2, :]
                + s2[r, at, :] * zz[r, at, DEPTH:]
            )
            new = 2.0 * rows[r] - prev[r, at, :] + (coef[r, at, :] * lap - drift)
            if mode == "bwd":
                out[r, at, :128] = new[:, :128] + plane[moment, r, at, :]
                out[r, at, 128:] = new[:, 128:]
            else:
                out[r, at, :] = new

    for r in range(0, ROWS + 2, 2):
        if r < ROWS:
            products(r)
            products(r + 1)
        if r > 0:
            for i in range(COLS // 8):
                update(r - 2, i)

    if mode == "fwd":

        line = ids[3] >> 8
        row = lax.div(line, COLS) - ids[0] * ROWS

        @pl.when((row >= 0) & (row < ROWS))
        def _():
            col = lax.rem(line, COLS)
            base = pl.multiple_of(col & ~7, 8)
            col_in = lax.broadcasted_iota(jnp.int32, (8, DEPTH), 0)
            depth_in = lax.broadcasted_iota(jnp.int32, (8, DEPTH), 1)
            struck = (col_in == (col & 7)) & (depth_in == (ids[3] & 255))
            out[row, pl.ds(base, 8), :] += jnp.where(struck, amount[moment], 0.0)

    if not last:
        core_out[...] = out[pl.ds(pl.multiple_of((1 - parity) * 4, 4), 4)]
        rows = out[pl.ds(pl.multiple_of(parity * 4, 4), 4)]
        if first:
            base = own[...]
        else:
            base = 2.0 * qs_now[...] - qs_prev[...]
        sent = (rows - base).astype(BF16)
        cross_out[...] = sent
        qs_out[...] = base + sent.astype(F32)


def step(mode, moment, ids, source, prev, now, core, cross, quant, planes, fields, tables):
    first, last = moment == 0, moment == STEPS - 1
    args = [ids]
    if mode == "fwd":
        args.append(source)
    args += [prev, now, core, cross] + list(quant)
    if mode == "bwd":
        args.append(planes)
    args += list(fields) + list(tables)
    outs = [(SLAB, F32)]
    if not last:
        outs += [(FACE, F32), (FACE, BF16), (FACE, F32), (FACE, F32)]
    scratch = [
        pltpu.VMEM((8, COLS, DEPTH), F32),
        pltpu.VMEM((ROWS, COLS, 2 * DEPTH), F32),
        pltpu.VMEM((ROWS, 2 * COLS, DEPTH), F32),
    ]
    return call(functools.partial(step_kernel, mode, first, moment), args, outs, scratch, "step_" + mode, 20_000_000_000)


def blocks_kernel(ids, part, a5, s0, a0, s5, *blocks):
    first, offset = ids[2] >> 6, ids[2] & 63
    within = lax.broadcasted_iota(jnp.int32, (TILE, COLS), 0)
    column = lax.broadcasted_iota(jnp.int32, (TILE, COLS), 1) + offset
    picks = [jnp.where(within + ((s - first) & 3) * TILE == column, 1.0, 0.0) for s in range(4)]
    pick = jnp.concatenate(picks, axis=0).astype(BF16)
    for r in range(ROWS):
        total = part[r] + a5[r] * s0[r] + a0[r] * s5[r]
        high, low = halves(total)
        placed = jnp.dot(pick, high, preferred_element_type=F32) + jnp.dot(
            pick, low, preferred_element_type=F32
        )
        for s in range(4):
            blocks[r // 4][s, r % 4] = placed[s * TILE : (s + 1) * TILE]


def combine_kernel(ids, blocks, keep, give):
    ring, _ = ring_of(ids)
    starts = (ids[2], ids[4], ids[5], ids[6])
    places = [(ring - i) & 3 for i in range(4)]
    flags = [jnp.where(serves_upper(start, ids), 1.0, 0.0).astype(F32) for start in starts]
    for r in range(ROWS // 2):
        kept = gave = None
        for place, flag in zip(places, flags):
            block = blocks[place, r]
            mine = flag * block
            kept = mine if kept is None else kept + mine
            gave = block - mine if gave is None else gave + (block - mine)
        keep[r] = kept
        give[r] = gave


def shards(
    forward_prev,
    forward_now,
    adjoint_prev,
    adjoint_now,
    velocity,
    density,
    anchors,
    shot_cell,
    wavelet,
    records,
):
    tables = weight_tables()
    place = lax.axis_index("apert")
    shot = lax.axis_index("shot")
    count = lax.axis_size("apert")
    groups = lax.axis_size("shot")
    half = groups // 2
    ids = jnp.stack([place, shot]).astype(jnp.int32)
    core_pairs = [(i, i ^ 1) for i in range(count)]
    cross_pairs = [(i, i + 1) for i in range(1, count - 1, 2)] + [(i + 1, i) for i in range(1, count - 1, 2)]
    side_pairs = [(i, (i + half) % groups) for i in range(groups)]

    def ring_pairs(shift):
        return [(i, (i // half) * half + (i % half + shift) % half) for i in range(groups)]

    def swap(core, cross):
        return lax.ppermute(core, "apert", core_pairs), lax.ppermute(cross, "apert", cross_pairs)

    rings = [list(range(i, i + half)) for i in range(0, groups, half)]

    def ring_send(pieces):
        return lax.all_to_all(pieces, "shot", split_axis=0, concat_axis=0, axis_index_groups=rings, tiled=True)

    starts = [lax.ppermute(anchors, "shot", ring_pairs(k)) for k in range(1, half)]
    other_dens = lax.ppermute(density, "shot", side_pairs)
    other_vel = lax.ppermute(velocity, "shot", side_pairs)
    base = jnp.concatenate([ids, anchors, shot_cell])
    tiles = ((half, ROWS, TILE, DEPTH), BF16)
    dens_tiles, vel_tiles, nums = call(
        select_kernel,
        [base, *starts, density, velocity, other_dens, other_vel],
        [tiles, tiles, ((7,), jnp.int32)],
        name="select",
    )
    fwd_prev, fwd_now, bwd_prev, bwd_now = forward_prev[0], forward_now[0], adjoint_prev[0], adjoint_now[0]
    first_cross, own_fwd, own_bwd = call(
        faces_kernel,
        [nums, fwd_now, bwd_now],
        [((2, 5, COLS, DEPTH), BF16), (FACE, F32), (FACE, F32)],
        name="faces",
    )
    first_cross, dens_tiles = lax.optimization_barrier((first_cross, dens_tiles))
    first_cross = lax.ppermute(first_cross, "apert", cross_pairs)
    dens_tiles, vel_tiles = ring_send(dens_tiles), ring_send(vel_tiles)
    lane = lax.broadcasted_iota(jnp.int32, (1, 1, 1, 128), 3)
    planes = jnp.where(lane == SURF, records[0][..., None], 0.0)
    dens_tiles, first_cross, planes = lax.optimization_barrier((dens_tiles, first_cross, planes))

    wide = [pltpu.VMEM((ROWS, 4 * TILE, DEPTH), BF16)]
    dens, first_core, dens_cross = call(
        window_dens_kernel,
        [nums, dens_tiles, fwd_now, bwd_now],
        [(SLAB, F32), ((3,) + FACE, F32), (FACE, BF16)],
        wide,
        "window_dens",
    )
    first_core, dens_cross = swap(first_core, dens_cross)
    coef, slope1, slope2, logs = call(
        coef_kernel, [nums, vel_tiles, dens, *tables], [(SLAB, F32)] * 4, wide, "coef"
    )
    (slope0,) = call(
        row_slope_kernel,
        [nums, logs, first_core, dens_cross, coef],
        [(SLAB, F32)],
        [pltpu.VMEM((8, COLS, DEPTH), F32)],
        "row_slope",
    )
    fields = (coef, slope0, slope1, slope2)
    source = wavelet[0]

    fwd_core = bwd_core = first_core
    fwd_cross = bwd_cross = first_cross
    fwd_quant, bwd_quant = (own_fwd,), (own_bwd,)
    snapshots, states = [], []
    for moment in range(STEPS):
        last = moment == STEPS - 1
        if moment > 0:
            fwd_core, fwd_cross = swap(fwd_core, fwd_cross)
        new, *sent = step(
            "fwd", moment, nums, source, fwd_prev, fwd_now, fwd_core, fwd_cross, fwd_quant, None, fields, tables
        )
        if not last:
            own = own_fwd if moment == 0 else fwd_quant[2]
            fwd_core, fwd_cross, seen, shown = sent
            fwd_quant = (seen, seen if moment == 0 else fwd_quant[0], shown, own)
        snapshots.append(new)
        fwd_prev, fwd_now = fwd_now, new

        if moment > 0:
            bwd_core, bwd_cross = swap(bwd_core, bwd_cross)
        new, *sent = step(
            "bwd", moment, nums, source, bwd_prev, bwd_now, bwd_core, bwd_cross, bwd_quant, planes, fields, tables
        )
        if not last:
            own = own_bwd if moment == 0 else bwd_quant[2]
            bwd_core, bwd_cross, seen, shown = sent
            bwd_quant = (seen, seen if moment == 0 else bwd_quant[0], shown, own)
        states.append(new)
        bwd_prev, bwd_now = bwd_now, new
    part = sum(states[t] * snapshots[STEPS - 1 - t] for t in range(1, STEPS - 1))

    block = (ROWS // 2, TILE, DEPTH)
    blocks = call(
        blocks_kernel,
        [nums, part, states[STEPS - 1], snapshots[0], states[0], snapshots[STEPS - 1]],
        [((half,) + block, F32)] * 2,
        name="blocks",
    )
    rows = []
    for each in blocks:
        keep, give = call(combine_kernel, [nums, ring_send(each)], [(block, F32)] * 2, name="combine")
        rows.append(keep + lax.ppermute(give, "shot", side_pairs))
    image = jnp.concatenate(rows, axis=0)
    return image, states[STEPS - 1][None]


def solution(mesh):
    placed = (
        P("shot", "apert", None, None),
        P("shot", "apert", None, None),
        P("shot", "apert", None, None),
        P("shot", "apert", None, None),
        P("apert", "shot", None),
        P("apert", "shot", None),
        P("shot"),
        P("shot"),
        P("shot", None),
        P("shot", None, "apert", None),
    )
    return jax.shard_map(
        shards,
        mesh=mesh,
        in_specs=placed,
        out_specs=(P("apert", "shot", None), P("shot", "apert", None, None)),
        check_vma=False,
    )
```

```python
import functools

import jax
import jax.numpy as jnp
import ml_dtypes
import numpy as np
from jax import lax
from jax.experimental import pallas as pl
from jax.experimental.pallas import tpu as pltpu
from jax.sharding import PartitionSpec as P

STEPS = 6
SURF = 8
ROWS, COLS, DEPTH = 8, 160, 256
TILE = 64
LAP = (-14350.0, 8064.0, -1008.0, 128.0, -9.0)
SLOPE = (672.0, -168.0, 32.0, -3.0)
LAP_SCALE, SLOPE_SCALE = 1.0 / 5040.0, 1.0 / 840.0
F32, BF16 = jnp.float32, jnp.bfloat16
VMEM = pl.BlockSpec(memory_space=pltpu.VMEM)
SMEM = pl.BlockSpec(memory_space=pltpu.SMEM)
PARAMS = pltpu.CompilerParams(vmem_limit_bytes=16 * 1024 * 1024)


def banded(size):
    lap, slope = np.zeros((size, size)), np.zeros((size, size))
    for k in range(1, 5):
        lap += LAP[k] * (np.eye(size, k=k) + np.eye(size, k=-k))
        slope += SLOPE[k - 1] * (np.eye(size, k=k) - np.eye(size, k=-k))
    return lap, slope


def weight_tables():
    lap, slope = banded(DEPTH)
    depth_table = np.concatenate([lap.T, slope.T], axis=1).astype(ml_dtypes.bfloat16)
    lap, slope = banded(COLS)
    cols_table = np.concatenate([lap, slope], axis=0).astype(ml_dtypes.bfloat16)
    return jnp.asarray(depth_table), jnp.asarray(cols_table)


def halves(x):
    high = x.astype(BF16)
    return high, (x - high.astype(F32)).astype(BF16)


def load_halo(halo, parity, core_rows, cross_rows):
    halo[pl.ds(pl.multiple_of((1 - parity) * 4, 4), 4)] = core_rows
    halo[pl.ds(pl.multiple_of(parity * 4, 4), 4)] = cross_rows


def extended_rows(halo, mid, first, count, at):
    rows = {}
    for r in range(first - 4, first + count + 4):
        if r < 0:
            rows[r] = halo[r + 4, at, :]
        elif r < ROWS:
            rows[r] = mid[r, at, :]
        else:
            rows[r] = halo[r - ROWS + 4, at, :]
    return rows


def row_slope_of(rows, r):
    total = None
    for k in range(1, 5):
        term = SLOPE[k - 1] * (rows[r + k] - rows[r - k])
        total = term if total is None else total + term
    return total


def call(body, args, outs, scratch=(), name=None, flops=10_000_000):
    specs, given = [], []
    for arg in args:
        if arg.ndim == 1:
            specs.append(SMEM)
            given.append(arg)
        else:
            specs.append(VMEM)
            given.append(pltpu.with_memory_space_constraint(arg, pltpu.VMEM))
    return pl.pallas_call(
        body,
        out_shape=[
            jax.ShapeDtypeStruct(shape, dtype) if len(shape) == 1 else pltpu.VMEM(shape, dtype)
            for shape, dtype in outs
        ],
        in_specs=specs,
        out_specs=[SMEM if len(shape) == 1 else VMEM for shape, _ in outs],
        scratch_shapes=list(scratch),
        compiler_params=PARAMS,
        cost_estimate=pl.CostEstimate(flops=flops, bytes_accessed=100_000, transcendentals=0),
        name=name,
    )(*given)


SLAB, FACE = (ROWS, COLS, DEPTH), (4, COLS, DEPTH)


def ring_of(ids):
    return ids[1] & 3, ids[1] >> 2


def serves_upper(start, ids):
    ring, upper = ring_of(ids)
    first = start >> 6
    return ((first + ((ring - first) & 3)) >> 2) == upper


def faces_kernel(ids, fwd, bwd, cross, own_fwd, own_bwd):
    parity = ids[0] & 1
    for f, (field, own) in enumerate(((fwd, own_fwd), (bwd, own_bwd))):
        own[...] = field[pl.ds(pl.multiple_of(parity * 4, 4), 4)]
        high = own[...].astype(BF16)
        cross[f, :4] = high
        near = parity * 3
        low = (own[near] - own[near].astype(BF16).astype(F32)).astype(BF16)
        cross[f, 4] = low
        own[...] = high.astype(F32)
        own[near] += low.astype(F32)


def select_kernel(base, s1, s2, s3, dens, vel, other_dens, other_vel, *outs):
    *outs, nums = outs
    numbers = [base[i] for i in range(4)] + [s1[0], s2[0], s3[0]]
    for i in range(7):
        nums[i] = numbers[i]
    for i, start in enumerate((numbers[2], numbers[6], numbers[5], numbers[4])):
        mine = serves_upper(start, numbers)

        @pl.when(mine)
        def _():
            outs[i][...] = dens[...]
            outs[4 + i][...] = vel[...]

        @pl.when(jnp.logical_not(mine))
        def _():
            outs[i][...] = other_dens[...]
            outs[4 + i][...] = other_vel[...]


def window_pick(ids):
    ring, _ = ring_of(ids)
    first, offset = ids[2] >> 6, ids[2] & 63
    want = lax.broadcasted_iota(jnp.int32, (COLS, TILE), 0) + offset
    within = lax.broadcasted_iota(jnp.int32, (COLS, TILE), 1)
    picks = [jnp.where(within + ((ring - s - first) & 3) * TILE == want, 1.0, 0.0) for s in range(4)]
    return jnp.concatenate(picks, axis=1).astype(BF16)


def window_dens_kernel(ids, t0, t1, t2, t3, fwd, bwd, dens_out, core_out, cross_out, wide):
    parity = ids[0] & 1
    pick = window_pick(ids)
    for s, tile in enumerate((t0, t1, t2, t3)):
        wide[:, s * TILE : (s + 1) * TILE, :] = tile[...]
    for r in range(ROWS):
        dens_out[r] = jnp.dot(pick, wide[r], preferred_element_type=F32)
    for i, field in enumerate((fwd, bwd, dens_out)):
        core_out[i] = field[pl.ds(pl.multiple_of((1 - parity) * 4, 4), 4)]
    cross_out[...] = dens_out[pl.ds(pl.multiple_of(parity * 4, 4), 4)].astype(BF16)


def coef_kernel(ids, t0, t1, t2, t3, dens, depth_w, cols_w, coef, s1, s2, logs, wide):
    pick = window_pick(ids)
    for s, tile in enumerate((t0, t1, t2, t3)):
        wide[:, s * TILE : (s + 1) * TILE, :] = tile[...]
    for r in range(ROWS):
        speed = jnp.dot(pick, wide[r], preferred_element_type=F32)
        c = speed * speed
        coef[r] = c * LAP_SCALE
        log = jnp.log(dens[r])
        logs[r] = log
        high, low = halves(log)
        cs = c * (SLOPE_SCALE * SLOPE_SCALE)
        s1[r] = cs * (
            jnp.dot(cols_w[COLS:], high, preferred_element_type=F32)
            + jnp.dot(cols_w[COLS:], low, preferred_element_type=F32)
        )
        s2[r] = cs * (
            jnp.dot(high, depth_w[:, DEPTH:], preferred_element_type=F32)
            + jnp.dot(low, depth_w[:, DEPTH:], preferred_element_type=F32)
        )


def row_slope_kernel(ids, logs, core, cross, coef, s0, halo):
    parity, place = ids[0] & 1, ids[0]
    pad = jnp.where((place == 0) | (place == 15), 1.0, 0.0).astype(F32)
    load_halo(halo, parity, jnp.log(core[2]), jnp.log(cross[...].astype(F32) + pad))

    def body(i, carry):
        at = pl.ds(pl.multiple_of(i * 8, 8), 8)
        rows = extended_rows(halo, logs, 0, ROWS, at)
        for r in range(ROWS):
            s0[r, at, :] = (coef[r, at, :] * (SLOPE_SCALE * SLOPE_SCALE / LAP_SCALE)) * row_slope_of(rows, r)
        return carry

    lax.fori_loop(0, COLS // 8, body, 0)


def step_kernel(mode, first, moment, *refs):
    refs = list(refs)
    ids = refs.pop(0)
    amount = refs.pop(0) if mode == "fwd" else None
    prev, now, core, cross = refs[:4]
    refs = refs[4:]
    which = 0 if mode == "fwd" else 1
    if first:
        own = refs.pop(0)
    else:
        qr_now, qr_prev, qs_now, qs_prev = refs[:4]
        refs = refs[4:]
    plane = refs.pop(0) if mode == "bwd" else None
    coef, s0, s1, s2, depth_w, cols_w = refs[:6]
    refs = refs[6:]
    out = refs.pop(0)
    last = len(refs) == 3
    if not last:
        core_out, cross_out, qr_out, qs_out = refs[:4]
        refs = refs[4:]
    halo, zz, cc = refs
    parity = ids[0] & 1
    if first:
        load_halo(halo, parity, core[which], cross[which, :4].astype(F32))
        halo[3 + parity] += cross[which, 4].astype(F32)
    else:
        seen = (2.0 * qr_now[...] - qr_prev[...]) + cross[...].astype(F32)
        load_halo(halo, parity, core[...], seen)
    if not last:
        qr_out[...] = halo[pl.ds(pl.multiple_of(parity * 4, 4), 4)]

    def products(r):
        high, low = halves(now[r])
        zz[r] = jnp.dot(high, depth_w[...], preferred_element_type=F32) + jnp.dot(
            low, depth_w[...], preferred_element_type=F32
        )
        cc[r] = jnp.dot(cols_w[...], high, preferred_element_type=F32) + jnp.dot(
            cols_w[...], low, preferred_element_type=F32
        )

    def update(first_row, i):
        at = pl.ds(i * 8, 8)
        at2 = pl.ds(COLS + i * 8, 8)
        rows = extended_rows(halo, now, first_row, 2, at)
        for r in (first_row, first_row + 1):
            lap = (3.0 * LAP[0]) * rows[r] + (cc[r, at, :] + zz[r, at, :DEPTH])
            for k in range(1, 5):
                lap += LAP[k] * (rows[r + k] + rows[r - k])
            drift = (
                s0[r, at, :] * row_slope_of(rows, r)
                + s1[r, at, :] * cc[r, at2, :]
                + s2[r, at, :] * zz[r, at, DEPTH:]
            )
            new = 2.0 * rows[r] - prev[r, at, :] + (coef[r, at, :] * lap - drift)
            if mode == "bwd":
                out[r, at, :128] = new[:, :128] + plane[moment, r, at, :]
                out[r, at, 128:] = new[:, 128:]
            else:
                out[r, at, :] = new

    for r in range(0, ROWS + 2, 2):
        if r < ROWS:
            products(r)
            products(r + 1)
        if r > 0:
            for i in range(COLS // 8):
                update(r - 2, i)

    if mode == "fwd":

        line = ids[3] >> 8
        row = lax.div(line, COLS) - ids[0] * ROWS

        @pl.when((row >= 0) & (row < ROWS))
        def _():
            col = lax.rem(line, COLS)
            base = pl.multiple_of(col & ~7, 8)
            col_in = lax.broadcasted_iota(jnp.int32, (8, DEPTH), 0)
            depth_in = lax.broadcasted_iota(jnp.int32, (8, DEPTH), 1)
            struck = (col_in == (col & 7)) & (depth_in == (ids[3] & 255))
            out[row, pl.ds(base, 8), :] += jnp.where(struck, amount[moment], 0.0)

    if not last:
        core_out[...] = out[pl.ds(pl.multiple_of((1 - parity) * 4, 4), 4)]
        rows = out[pl.ds(pl.multiple_of(parity * 4, 4), 4)]
        if first:
            base = own[...]
        else:
            base = 2.0 * qs_now[...] - qs_prev[...]
        sent = (rows - base).astype(BF16)
        cross_out[...] = sent
        qs_out[...] = base + sent.astype(F32)


def step(mode, moment, ids, source, prev, now, core, cross, quant, planes, fields, tables):
    first, last = moment == 0, moment == STEPS - 1
    args = [ids]
    if mode == "fwd":
        args.append(source)
    args += [prev, now, core, cross] + list(quant)
    if mode == "bwd":
        args.append(planes)
    args += list(fields) + list(tables)
    outs = [(SLAB, F32)]
    if not last:
        outs += [(FACE, F32), (FACE, BF16), (FACE, F32), (FACE, F32)]
    scratch = [
        pltpu.VMEM((8, COLS, DEPTH), F32),
        pltpu.VMEM((ROWS, COLS, 2 * DEPTH), F32),
        pltpu.VMEM((ROWS, 2 * COLS, DEPTH), F32),
    ]
    return call(functools.partial(step_kernel, mode, first, moment), args, outs, scratch, "step_" + mode, 20_000_000_000)


def blocks_kernel(ids, part, a5, s0, a0, s5, *blocks):
    ring, _ = ring_of(ids)
    first, offset = ids[2] >> 6, ids[2] & 63
    within = lax.broadcasted_iota(jnp.int32, (TILE, COLS), 0)
    column = lax.broadcasted_iota(jnp.int32, (TILE, COLS), 1) + offset
    picks = [jnp.where(within + ((ring + s - first) & 3) * TILE == column, 1.0, 0.0) for s in range(4)]
    pick = jnp.concatenate(picks, axis=0).astype(BF16)
    for r in range(ROWS):
        total = part[r] + a5[r] * s0[r] + a0[r] * s5[r]
        high, low = halves(total)
        placed = jnp.dot(pick, high, preferred_element_type=F32) + jnp.dot(
            pick, low, preferred_element_type=F32
        )
        for s in range(4):
            blocks[r // 4 * 4 + s][r % 4] = placed[s * TILE : (s + 1) * TILE]


def combine_kernel(ids, b0, b1, b2, b3, keep, give):
    flags = [jnp.where(serves_upper(ids[i], ids), 1.0, 0.0).astype(F32) for i in (2, 4, 5, 6)]
    for r in range(ROWS // 2):
        kept = flags[0] * b0[r]
        total = b0[r]
        for flag, block in zip(flags[1:], (b1, b2, b3)):
            kept += flag * block[r]
            total += block[r]
        keep[r] = kept
        gave = (1.0 - flags[0]) * b0[r]
        for flag, block in zip(flags[1:], (b1, b2, b3)):
            gave += (1.0 - flag) * block[r]
        give[r] = gave


def shards(
    forward_prev,
    forward_now,
    adjoint_prev,
    adjoint_now,
    velocity,
    density,
    anchors,
    shot_cell,
    wavelet,
    records,
):
    tables = weight_tables()
    place = lax.axis_index("apert")
    shot = lax.axis_index("shot")
    count = lax.axis_size("apert")
    groups = lax.axis_size("shot")
    half = groups // 2
    ids = jnp.stack([place, shot]).astype(jnp.int32)
    core_pairs = [(i, i ^ 1) for i in range(count)]
    cross_pairs = [(i, i + 1) for i in range(1, count - 1, 2)] + [(i + 1, i) for i in range(1, count - 1, 2)]
    side_pairs = [(i, (i + half) % groups) for i in range(groups)]

    def ring_pairs(shift):
        return [(i, (i // half) * half + (i % half + shift) % half) for i in range(groups)]

    def swap(core, cross):
        return lax.ppermute(core, "apert", core_pairs), lax.ppermute(cross, "apert", cross_pairs)

    both_ways = [
        (i * count + j, ((i // half) * half + (i % half + (1 if j % 2 == 0 else -1)) % half) * count + j)
        for i in range(groups)
        for j in range(count)
    ]

    def ring_send(pieces):
        halfway = lax.ppermute(pieces[2], ("shot", "apert"), both_ways)
        near = lax.ppermute(pieces[1], "shot", ring_pairs(1)), lax.ppermute(pieces[3], "shot", ring_pairs(3))
        return [pieces[0], near[0], lax.ppermute(halfway, ("shot", "apert"), both_ways), near[1]]

    starts = [lax.ppermute(anchors, "shot", ring_pairs(k)) for k in range(1, half)]
    other_dens = lax.ppermute(density, "shot", side_pairs)
    other_vel = lax.ppermute(velocity, "shot", side_pairs)
    base = jnp.concatenate([ids, anchors, shot_cell])
    tile = ((ROWS, TILE, DEPTH), BF16)
    *picked, nums = call(
        select_kernel,
        [base, *starts, density, velocity, other_dens, other_vel],
        [tile] * (2 * half) + [((7,), jnp.int32)],
        name="select",
    )
    fwd_prev, fwd_now, bwd_prev, bwd_now = forward_prev[0], forward_now[0], adjoint_prev[0], adjoint_now[0]
    first_cross, own_fwd, own_bwd = call(
        faces_kernel,
        [nums, fwd_now, bwd_now],
        [((2, 5, COLS, DEPTH), BF16), (FACE, F32), (FACE, F32)],
        name="faces",
    )
    first_cross, *picked = lax.optimization_barrier((first_cross, *picked))
    first_cross = lax.ppermute(first_cross, "apert", cross_pairs)
    dens_tiles = ring_send(picked[:half])
    later = lax.optimization_barrier((dens_tiles[1], dens_tiles[3], *picked[half:]))
    dens_tiles[1], dens_tiles[3] = later[:2]
    vel_tiles = ring_send(later[2:])
    lane = lax.broadcasted_iota(jnp.int32, (1, 1, 1, 128), 3)
    planes = jnp.where(lane == SURF, records[0][..., None], 0.0)
    first_cross, planes, *dens_tiles = lax.optimization_barrier((first_cross, planes, *dens_tiles))

    wide = [pltpu.VMEM((ROWS, 4 * TILE, DEPTH), BF16)]
    dens, first_core, dens_cross = call(
        window_dens_kernel,
        [nums, *dens_tiles, fwd_now, bwd_now],
        [(SLAB, F32), ((3,) + FACE, F32), (FACE, BF16)],
        wide,
        "window_dens",
        20_000_000_000,
    )
    first_core, dens_cross = swap(first_core, dens_cross)
    coef, slope1, slope2, logs = call(
        coef_kernel, [nums, *vel_tiles, dens, *tables], [(SLAB, F32)] * 4, wide, "coef", 20_000_000_000
    )
    (slope0,) = call(
        row_slope_kernel,
        [nums, logs, first_core, dens_cross, coef],
        [(SLAB, F32)],
        [pltpu.VMEM((8, COLS, DEPTH), F32)],
        "row_slope",
    )
    fields = (coef, slope0, slope1, slope2)
    source = wavelet[0]

    fwd_core = bwd_core = first_core
    fwd_cross = bwd_cross = first_cross
    fwd_quant, bwd_quant = (own_fwd,), (own_bwd,)
    snapshots, states = [], []
    for moment in range(STEPS):
        last = moment == STEPS - 1
        if moment > 0:
            fwd_core, fwd_cross = swap(fwd_core, fwd_cross)
        new, *sent = step(
            "fwd", moment, nums, source, fwd_prev, fwd_now, fwd_core, fwd_cross, fwd_quant, None, fields, tables
        )
        if not last:
            own = own_fwd if moment == 0 else fwd_quant[2]
            fwd_core, fwd_cross, seen, shown = sent
            fwd_quant = (seen, seen if moment == 0 else fwd_quant[0], shown, own)
        snapshots.append(new)
        fwd_prev, fwd_now = fwd_now, new

        if moment > 0:
            bwd_core, bwd_cross = swap(bwd_core, bwd_cross)
        new, *sent = step(
            "bwd", moment, nums, source, bwd_prev, bwd_now, bwd_core, bwd_cross, bwd_quant, planes, fields, tables
        )
        if not last:
            own = own_bwd if moment == 0 else bwd_quant[2]
            bwd_core, bwd_cross, seen, shown = sent
            bwd_quant = (seen, seen if moment == 0 else bwd_quant[0], shown, own)
        states.append(new)
        bwd_prev, bwd_now = bwd_now, new
    part = sum(states[t] * snapshots[STEPS - 1 - t] for t in range(1, STEPS - 1))

    block = ((ROWS // 2, TILE, DEPTH), F32)
    blocks = call(
        blocks_kernel,
        [nums, part, states[STEPS - 1], snapshots[0], states[0], snapshots[STEPS - 1]],
        [block] * (2 * half),
        name="blocks",
    )
    arrived = [ring_send(blocks[:half]), ring_send(blocks[half:])]
    rows = []
    for each in arrived:
        keep, give = call(combine_kernel, [nums, *each], [block] * 2, name="combine")
        rows.append(keep + lax.ppermute(give, "shot", side_pairs))
    image = jnp.concatenate(rows, axis=0)
    return image, states[STEPS - 1][None]


def solution(mesh):
    placed = (
        P("shot", "apert", None, None),
        P("shot", "apert", None, None),
        P("shot", "apert", None, None),
        P("shot", "apert", None, None),
        P("apert", "shot", None),
        P("apert", "shot", None),
        P("shot"),
        P("shot"),
        P("shot", None),
        P("shot", None, "apert", None),
    )
    return jax.shard_map(
        shards,
        mesh=mesh,
        in_specs=placed,
        out_specs=(P("apert", "shot", None), P("shot", "apert", None, None)),
        check_vma=False,
    )
```

```python
import functools

import jax
import jax.numpy as jnp
import ml_dtypes
import numpy as np
from jax import lax
from jax.experimental import pallas as pl
from jax.experimental.pallas import tpu as pltpu
from jax.sharding import PartitionSpec as P

STEPS = 6
SURF = 8
ROWS, COLS, DEPTH = 8, 160, 256
TILE = 64
LAP = (-14350.0, 8064.0, -1008.0, 128.0, -9.0)
SLOPE = (672.0, -168.0, 32.0, -3.0)
LAP_SCALE, SLOPE_SCALE = 1.0 / 5040.0, 1.0 / 840.0
F32, BF16 = jnp.float32, jnp.bfloat16
VMEM = pl.BlockSpec(memory_space=pltpu.VMEM)
SMEM = pl.BlockSpec(memory_space=pltpu.SMEM)
PARAMS = pltpu.CompilerParams(vmem_limit_bytes=16 * 1024 * 1024)


def banded(size):
    lap, slope = np.zeros((size, size)), np.zeros((size, size))
    for k in range(1, 5):
        lap += LAP[k] * (np.eye(size, k=k) + np.eye(size, k=-k))
        slope += SLOPE[k - 1] * (np.eye(size, k=k) - np.eye(size, k=-k))
    return lap, slope


def weight_tables():
    lap, slope = banded(DEPTH)
    depth_table = np.concatenate([lap.T, slope.T], axis=1).astype(ml_dtypes.bfloat16)
    lap, slope = banded(COLS)
    cols_table = np.concatenate([lap, slope], axis=0).astype(ml_dtypes.bfloat16)
    return jnp.asarray(depth_table), jnp.asarray(cols_table)


def halves(x):
    high = x.astype(BF16)
    return high, (x - high.astype(F32)).astype(BF16)


def load_halo(halo, parity, core_rows, cross_rows):
    halo[pl.ds(pl.multiple_of((1 - parity) * 4, 4), 4)] = core_rows
    halo[pl.ds(pl.multiple_of(parity * 4, 4), 4)] = cross_rows


def extended_rows(halo, mid, first, count, at):
    rows = {}
    for r in range(first - 4, first + count + 4):
        if r < 0:
            rows[r] = halo[r + 4, at, :]
        elif r < ROWS:
            rows[r] = mid[r, at, :]
        else:
            rows[r] = halo[r - ROWS + 4, at, :]
    return rows


def row_slope_of(rows, r):
    total = None
    for k in range(1, 5):
        term = SLOPE[k - 1] * (rows[r + k] - rows[r - k])
        total = term if total is None else total + term
    return total


def call(body, args, outs, scratch=(), name=None, flops=10_000_000):
    specs, given = [], []
    for arg in args:
        if arg.ndim == 1:
            specs.append(SMEM)
            given.append(arg)
        else:
            specs.append(VMEM)
            given.append(pltpu.with_memory_space_constraint(arg, pltpu.VMEM))
    return pl.pallas_call(
        body,
        out_shape=[
            jax.ShapeDtypeStruct(shape, dtype) if len(shape) == 1 else pltpu.VMEM(shape, dtype)
            for shape, dtype in outs
        ],
        in_specs=specs,
        out_specs=[SMEM if len(shape) == 1 else VMEM for shape, _ in outs],
        scratch_shapes=list(scratch),
        compiler_params=PARAMS,
        cost_estimate=pl.CostEstimate(flops=flops, bytes_accessed=100_000, transcendentals=0),
        name=name,
    )(*given)


SLAB, FACE = (ROWS, COLS, DEPTH), (4, COLS, DEPTH)


def ring_of(ids):
    return ids[1] & 3, ids[1] >> 2


def serves_upper(start, ids):
    ring, upper = ring_of(ids)
    first = start >> 6
    return ((first + ((ring - first) & 3)) >> 2) == upper


def faces_kernel(ids, fwd, bwd, dens, vel, cross, own_fwd, own_bwd, dens_out, vel_out):
    parity = ids[0] & 1
    for f, (field, own) in enumerate(((fwd, own_fwd), (bwd, own_bwd))):
        own[...] = field[pl.ds(pl.multiple_of(parity * 4, 4), 4)]
        high = own[...].astype(BF16)
        cross[f, :4] = high
        near = parity * 3
        low = (own[near] - own[near].astype(BF16).astype(F32)).astype(BF16)
        cross[f, 4] = low
        own[...] = high.astype(F32)
        own[near] += low.astype(F32)
    dens_out[...] = dens[...]
    vel_out[...] = vel[...]


def select_kernel(base, s1, s2, s3, dens, vel, other_dens, other_vel, *outs):
    *outs, nums = outs
    numbers = [base[i] for i in range(4)] + [s1[0], s2[0], s3[0]]
    for i in range(7):
        nums[i] = numbers[i]
    for i, start in enumerate((numbers[2], numbers[6], numbers[5], numbers[4])):
        mine = serves_upper(start, numbers)

        @pl.when(mine)
        def _():
            outs[i][...] = dens[...]
            outs[4 + i][...] = vel[...]

        @pl.when(jnp.logical_not(mine))
        def _():
            outs[i][...] = other_dens[...]
            outs[4 + i][...] = other_vel[...]


def window_pick(ids):
    ring, _ = ring_of(ids)
    first, offset = ids[2] >> 6, ids[2] & 63
    want = lax.broadcasted_iota(jnp.int32, (COLS, TILE), 0) + offset
    within = lax.broadcasted_iota(jnp.int32, (COLS, TILE), 1)
    picks = [jnp.where(within + ((ring - s - first) & 3) * TILE == want, 1.0, 0.0) for s in range(4)]
    return jnp.concatenate(picks, axis=1).astype(BF16)


def window_dens_kernel(ids, t0, t1, t2, t3, fwd, bwd, dens_out, core_out, cross_out, wide):
    parity = ids[0] & 1
    pick = window_pick(ids)
    for s, tile in enumerate((t0, t1, t2, t3)):
        wide[:, s * TILE : (s + 1) * TILE, :] = tile[...]
    for r in range(ROWS):
        dens_out[r] = jnp.dot(pick, wide[r], preferred_element_type=F32)
    for i, field in enumerate((fwd, bwd, dens_out)):
        core_out[i] = field[pl.ds(pl.multiple_of((1 - parity) * 4, 4), 4)]
    cross_out[...] = dens_out[pl.ds(pl.multiple_of(parity * 4, 4), 4)].astype(BF16)


def coef_kernel(ids, t0, t1, t2, t3, dens, depth_w, cols_w, coef, s1, s2, logs, wide):
    pick = window_pick(ids)
    for s, tile in enumerate((t0, t1, t2, t3)):
        wide[:, s * TILE : (s + 1) * TILE, :] = tile[...]
    for r in range(ROWS):
        speed = jnp.dot(pick, wide[r], preferred_element_type=F32)
        c = speed * speed
        coef[r] = c * LAP_SCALE
        log = jnp.log(dens[r])
        logs[r] = log
        high, low = halves(log)
        cs = c * (SLOPE_SCALE * SLOPE_SCALE)
        s1[r] = cs * (
            jnp.dot(cols_w[COLS:], high, preferred_element_type=F32)
            + jnp.dot(cols_w[COLS:], low, preferred_element_type=F32)
        )
        s2[r] = cs * (
            jnp.dot(high, depth_w[:, DEPTH:], preferred_element_type=F32)
            + jnp.dot(low, depth_w[:, DEPTH:], preferred_element_type=F32)
        )


def row_slope_kernel(ids, logs, core, cross, coef, s0, halo):
    parity, place = ids[0] & 1, ids[0]
    pad = jnp.where((place == 0) | (place == 15), 1.0, 0.0).astype(F32)
    load_halo(halo, parity, jnp.log(core[2]), jnp.log(cross[...].astype(F32) + pad))

    def body(i, carry):
        at = pl.ds(pl.multiple_of(i * 8, 8), 8)
        rows = extended_rows(halo, logs, 0, ROWS, at)
        for r in range(ROWS):
            s0[r, at, :] = (coef[r, at, :] * (SLOPE_SCALE * SLOPE_SCALE / LAP_SCALE)) * row_slope_of(rows, r)
        return carry

    lax.fori_loop(0, COLS // 8, body, 0)


def step_kernel(mode, first, moment, *refs):
    refs = list(refs)
    ids = refs.pop(0)
    amount = refs.pop(0) if mode == "fwd" else None
    prev, now, core, cross = refs[:4]
    refs = refs[4:]
    which = 0 if mode == "fwd" else 1
    if first:
        own = refs.pop(0)
    else:
        qr_now, qr_prev, qs_now, qs_prev = refs[:4]
        refs = refs[4:]
    plane = refs.pop(0) if mode == "bwd" else None
    coef, s0, s1, s2, depth_w, cols_w = refs[:6]
    refs = refs[6:]
    out = refs.pop(0)
    last = len(refs) == 3
    if not last:
        core_out, cross_out, qr_out, qs_out = refs[:4]
        refs = refs[4:]
    halo, zz, cc = refs
    parity = ids[0] & 1
    if first:
        load_halo(halo, parity, core[which], cross[which, :4].astype(F32))
        halo[3 + parity] += cross[which, 4].astype(F32)
    else:
        seen = (2.0 * qr_now[...] - qr_prev[...]) + cross[...].astype(F32)
        load_halo(halo, parity, core[...], seen)
    if not last:
        qr_out[...] = halo[pl.ds(pl.multiple_of(parity * 4, 4), 4)]

    def products(r):
        high, low = halves(now[r])
        zz[r] = jnp.dot(high, depth_w[...], preferred_element_type=F32) + jnp.dot(
            low, depth_w[...], preferred_element_type=F32
        )
        cc[r] = jnp.dot(cols_w[...], high, preferred_element_type=F32) + jnp.dot(
            cols_w[...], low, preferred_element_type=F32
        )

    def update(first_row, i):
        at = pl.ds(i * 8, 8)
        at2 = pl.ds(COLS + i * 8, 8)
        rows = extended_rows(halo, now, first_row, 2, at)
        for r in (first_row, first_row + 1):
            lap = (3.0 * LAP[0]) * rows[r] + (cc[r, at, :] + zz[r, at, :DEPTH])
            for k in range(1, 5):
                lap += LAP[k] * (rows[r + k] + rows[r - k])
            drift = (
                s0[r, at, :] * row_slope_of(rows, r)
                + s1[r, at, :] * cc[r, at2, :]
                + s2[r, at, :] * zz[r, at, DEPTH:]
            )
            new = 2.0 * rows[r] - prev[r, at, :] + (coef[r, at, :] * lap - drift)
            if mode == "bwd":
                out[r, at, :128] = new[:, :128] + plane[moment, r, at, :]
                out[r, at, 128:] = new[:, 128:]
            else:
                out[r, at, :] = new

    for r in range(0, ROWS + 2, 2):
        if r < ROWS:
            products(r)
            products(r + 1)
        if r > 0:
            for i in range(COLS // 8):
                update(r - 2, i)

    if mode == "fwd":

        line = ids[3] >> 8
        row = lax.div(line, COLS) - ids[0] * ROWS

        @pl.when((row >= 0) & (row < ROWS))
        def _():
            col = lax.rem(line, COLS)
            base = pl.multiple_of(col & ~7, 8)
            col_in = lax.broadcasted_iota(jnp.int32, (8, DEPTH), 0)
            depth_in = lax.broadcasted_iota(jnp.int32, (8, DEPTH), 1)
            struck = (col_in == (col & 7)) & (depth_in == (ids[3] & 255))
            out[row, pl.ds(base, 8), :] += jnp.where(struck, amount[moment], 0.0)

    if not last:
        core_out[...] = out[pl.ds(pl.multiple_of((1 - parity) * 4, 4), 4)]
        rows = out[pl.ds(pl.multiple_of(parity * 4, 4), 4)]
        if first:
            base = own[...]
        else:
            base = 2.0 * qs_now[...] - qs_prev[...]
        sent = (rows - base).astype(BF16)
        cross_out[...] = sent
        qs_out[...] = base + sent.astype(F32)


def step(mode, moment, ids, source, prev, now, core, cross, quant, planes, fields, tables):
    first, last = moment == 0, moment == STEPS - 1
    args = [ids]
    if mode == "fwd":
        args.append(source)
    args += [prev, now, core, cross] + list(quant)
    if mode == "bwd":
        args.append(planes)
    args += list(fields) + list(tables)
    outs = [(SLAB, F32)]
    if not last:
        outs += [(FACE, F32), (FACE, BF16), (FACE, F32), (FACE, F32)]
    scratch = [
        pltpu.VMEM((8, COLS, DEPTH), F32),
        pltpu.VMEM((ROWS, COLS, 2 * DEPTH), F32),
        pltpu.VMEM((ROWS, 2 * COLS, DEPTH), F32),
    ]
    return call(functools.partial(step_kernel, mode, first, moment), args, outs, scratch, "step_" + mode, 20_000_000_000)


def blocks_kernel(ids, part, a5, s0, a0, s5, *blocks):
    ring, _ = ring_of(ids)
    first, offset = ids[2] >> 6, ids[2] & 63
    within = lax.broadcasted_iota(jnp.int32, (TILE, COLS), 0)
    column = lax.broadcasted_iota(jnp.int32, (TILE, COLS), 1) + offset
    picks = [jnp.where(within + ((ring + s - first) & 3) * TILE == column, 1.0, 0.0) for s in range(4)]
    pick = jnp.concatenate(picks, axis=0).astype(BF16)
    for r in range(ROWS):
        total = part[r] + a5[r] * s0[r] + a0[r] * s5[r]
        high, low = halves(total)
        placed = jnp.dot(pick, high, preferred_element_type=F32) + jnp.dot(
            pick, low, preferred_element_type=F32
        )
        for s in range(4):
            blocks[r // 4 * 4 + s][r % 4] = placed[s * TILE : (s + 1) * TILE]


def combine_kernel(ids, b0, b1, b2, b3, keep, give):
    flags = [jnp.where(serves_upper(ids[i], ids), 1.0, 0.0).astype(F32) for i in (2, 4, 5, 6)]
    for r in range(ROWS // 2):
        kept = flags[0] * b0[r]
        total = b0[r]
        for flag, block in zip(flags[1:], (b1, b2, b3)):
            kept += flag * block[r]
            total += block[r]
        keep[r] = kept
        gave = (1.0 - flags[0]) * b0[r]
        for flag, block in zip(flags[1:], (b1, b2, b3)):
            gave += (1.0 - flag) * block[r]
        give[r] = gave


def shards(
    forward_prev,
    forward_now,
    adjoint_prev,
    adjoint_now,
    velocity,
    density,
    anchors,
    shot_cell,
    wavelet,
    records,
):
    tables = weight_tables()
    place = lax.axis_index("apert")
    shot = lax.axis_index("shot")
    count = lax.axis_size("apert")
    groups = lax.axis_size("shot")
    half = groups // 2
    ids = jnp.stack([place, shot]).astype(jnp.int32)
    core_pairs = [(i, i ^ 1) for i in range(count)]
    cross_pairs = [(i, i + 1) for i in range(1, count - 1, 2)] + [(i + 1, i) for i in range(1, count - 1, 2)]
    side_pairs = [(i, (i + half) % groups) for i in range(groups)]

    def ring_pairs(shift):
        return [(i, (i // half) * half + (i % half + shift) % half) for i in range(groups)]

    def swap(core, cross):
        return lax.ppermute(core, "apert", core_pairs), lax.ppermute(cross, "apert", cross_pairs)

    both_ways = [
        (i * count + j, ((i // half) * half + (i % half + (1 if j % 2 == 0 else -1)) % half) * count + j)
        for i in range(groups)
        for j in range(count)
    ]

    def ring_send(pieces):
        halfway = lax.ppermute(pieces[2], ("shot", "apert"), both_ways)
        near = lax.ppermute(pieces[1], "shot", ring_pairs(1)), lax.ppermute(pieces[3], "shot", ring_pairs(3))
        return [pieces[0], near[0], lax.ppermute(halfway, ("shot", "apert"), both_ways), near[1]]

    def ring_direct(pieces):
        return [pieces[0]] + [lax.ppermute(pieces[k], "shot", ring_pairs(k)) for k in (1, 2, 3)]

    starts = [lax.ppermute(anchors, "shot", ring_pairs(k)) for k in range(1, half)]
    other_dens = lax.ppermute(density, "shot", side_pairs)
    other_vel = lax.ppermute(velocity, "shot", side_pairs)
    base = jnp.concatenate([ids, anchors, shot_cell])
    tile = ((ROWS, TILE, DEPTH), BF16)
    fwd_prev, fwd_now, bwd_prev, bwd_now = forward_prev[0], forward_now[0], adjoint_prev[0], adjoint_now[0]
    first_cross, own_fwd, own_bwd, dens, vel = call(
        faces_kernel,
        [base, fwd_now, bwd_now, density, velocity],
        [((2, 5, COLS, DEPTH), BF16), (FACE, F32), (FACE, F32), tile, tile],
        name="faces",
    )
    *picked, nums = call(
        select_kernel,
        [base, *starts, dens, vel, other_dens, other_vel],
        [tile] * (2 * half) + [((7,), jnp.int32)],
        name="select",
    )
    first_cross, *picked = lax.optimization_barrier((first_cross, *picked))
    first_cross = lax.ppermute(first_cross, "apert", cross_pairs)
    dens_tiles = ring_direct(picked[:half])
    later = lax.optimization_barrier((dens_tiles[1], dens_tiles[3], *picked[half:]))
    dens_tiles[1], dens_tiles[3] = later[:2]
    vel_tiles = ring_direct(later[2:])
    lane = lax.broadcasted_iota(jnp.int32, (1, 1, 1, 128), 3)
    planes = jnp.where(lane == SURF, records[0][..., None], 0.0)
    first_cross, planes, *dens_tiles = lax.optimization_barrier((first_cross, planes, *dens_tiles))

    wide = [pltpu.VMEM((ROWS, 4 * TILE, DEPTH), BF16)]
    dens, first_core, dens_cross = call(
        window_dens_kernel,
        [nums, *dens_tiles, fwd_now, bwd_now],
        [(SLAB, F32), ((3,) + FACE, F32), (FACE, BF16)],
        wide,
        "window_dens",
        20_000_000_000,
    )
    first_core, dens_cross = swap(first_core, dens_cross)
    coef, slope1, slope2, logs = call(
        coef_kernel, [nums, *vel_tiles, dens, *tables], [(SLAB, F32)] * 4, wide, "coef", 20_000_000_000
    )
    (slope0,) = call(
        row_slope_kernel,
        [nums, logs, first_core, dens_cross, coef],
        [(SLAB, F32)],
        [pltpu.VMEM((8, COLS, DEPTH), F32)],
        "row_slope",
    )
    fields = (coef, slope0, slope1, slope2)
    source = wavelet[0]

    fwd_core = bwd_core = first_core
    fwd_cross = bwd_cross = first_cross
    fwd_quant, bwd_quant = (own_fwd,), (own_bwd,)
    snapshots, states = [], []
    for moment in range(STEPS):
        last = moment == STEPS - 1
        if moment > 0:
            fwd_core, fwd_cross = swap(fwd_core, fwd_cross)
        new, *sent = step(
            "fwd", moment, nums, source, fwd_prev, fwd_now, fwd_core, fwd_cross, fwd_quant, None, fields, tables
        )
        if not last:
            own = own_fwd if moment == 0 else fwd_quant[2]
            fwd_core, fwd_cross, seen, shown = sent
            fwd_quant = (seen, seen if moment == 0 else fwd_quant[0], shown, own)
        snapshots.append(new)
        fwd_prev, fwd_now = fwd_now, new

        if moment > 0:
            bwd_core, bwd_cross = swap(bwd_core, bwd_cross)
        new, *sent = step(
            "bwd", moment, nums, source, bwd_prev, bwd_now, bwd_core, bwd_cross, bwd_quant, planes, fields, tables
        )
        if not last:
            own = own_bwd if moment == 0 else bwd_quant[2]
            bwd_core, bwd_cross, seen, shown = sent
            bwd_quant = (seen, seen if moment == 0 else bwd_quant[0], shown, own)
        states.append(new)
        bwd_prev, bwd_now = bwd_now, new
    part = sum(states[t] * snapshots[STEPS - 1 - t] for t in range(1, STEPS - 1))

    block = ((ROWS // 2, TILE, DEPTH), F32)
    blocks = call(
        blocks_kernel,
        [nums, part, states[STEPS - 1], snapshots[0], states[0], snapshots[STEPS - 1]],
        [block] * (2 * half),
        name="blocks",
    )
    arrived = [ring_send(blocks[:half]), ring_send(blocks[half:])]
    rows = []
    for each in arrived:
        keep, give = call(combine_kernel, [nums, *each], [block] * 2, name="combine")
        rows.append(keep + lax.ppermute(give, "shot", side_pairs))
    image = jnp.concatenate(rows, axis=0)
    return image, states[STEPS - 1][None]


def solution(mesh):
    placed = (
        P("shot", "apert", None, None),
        P("shot", "apert", None, None),
        P("shot", "apert", None, None),
        P("shot", "apert", None, None),
        P("apert", "shot", None),
        P("apert", "shot", None),
        P("shot"),
        P("shot"),
        P("shot", None),
        P("shot", None, "apert", None),
    )
    return jax.shard_map(
        shards,
        mesh=mesh,
        in_specs=placed,
        out_specs=(P("apert", "shot", None), P("shot", "apert", None, None)),
        check_vma=False,
    )
```

```python
import functools

import jax
import jax.numpy as jnp
import ml_dtypes
import numpy as np
from jax import lax
from jax.experimental import pallas as pl
from jax.experimental.pallas import tpu as pltpu
from jax.sharding import PartitionSpec as P

STEPS = 6
SURF = 8
ROWS, COLS, DEPTH = 8, 160, 256
TILE = 64
SPLIT = 6
LAP = (-14350.0, 8064.0, -1008.0, 128.0, -9.0)
SLOPE = (672.0, -168.0, 32.0, -3.0)
LAP_SCALE, SLOPE_SCALE = 1.0 / 5040.0, 1.0 / 840.0
F32, BF16 = jnp.float32, jnp.bfloat16
VMEM = pl.BlockSpec(memory_space=pltpu.VMEM)
SMEM = pl.BlockSpec(memory_space=pltpu.SMEM)
PARAMS = pltpu.CompilerParams(vmem_limit_bytes=16 * 1024 * 1024)


def banded(size):
    lap, slope = np.zeros((size, size)), np.zeros((size, size))
    for k in range(1, 5):
        lap += LAP[k] * (np.eye(size, k=k) + np.eye(size, k=-k))
        slope += SLOPE[k - 1] * (np.eye(size, k=k) - np.eye(size, k=-k))
    return lap, slope


def weight_tables():
    lap, slope = banded(DEPTH)
    depth_table = np.concatenate([lap.T, slope.T], axis=1).astype(ml_dtypes.bfloat16)
    lap, slope = banded(COLS)
    cols_table = np.concatenate([lap, slope], axis=0).astype(ml_dtypes.bfloat16)
    return jnp.asarray(depth_table), jnp.asarray(cols_table)


def halves(x):
    high = x.astype(BF16)
    return high, (x - high.astype(F32)).astype(BF16)


def load_halo(halo, parity, core_rows, cross_rows):
    halo[pl.ds(pl.multiple_of((1 - parity) * 4, 4), 4)] = core_rows
    halo[pl.ds(pl.multiple_of(parity * 4, 4), 4)] = cross_rows


def extended_rows(halo, mid, first, count, at):
    rows = {}
    for r in range(first - 4, first + count + 4):
        if r < 0:
            rows[r] = halo[r + 4, at, :]
        elif r < ROWS:
            rows[r] = mid[r, at, :]
        else:
            rows[r] = halo[r - ROWS + 4, at, :]
    return rows


def row_slope_of(rows, r):
    total = None
    for k in range(1, 5):
        term = SLOPE[k - 1] * (rows[r + k] - rows[r - k])
        total = term if total is None else total + term
    return total


def call(body, args, outs, scratch=(), name=None, flops=10_000_000):
    specs, given = [], []
    for arg in args:
        if arg.ndim == 1:
            specs.append(SMEM)
            given.append(arg)
        else:
            specs.append(VMEM)
            given.append(pltpu.with_memory_space_constraint(arg, pltpu.VMEM))
    return pl.pallas_call(
        body,
        out_shape=[
            jax.ShapeDtypeStruct(shape, dtype) if len(shape) == 1 else pltpu.VMEM(shape, dtype)
            for shape, dtype in outs
        ],
        in_specs=specs,
        out_specs=[SMEM if len(shape) == 1 else VMEM for shape, _ in outs],
        scratch_shapes=list(scratch),
        compiler_params=PARAMS,
        cost_estimate=pl.CostEstimate(flops=flops, bytes_accessed=100_000, transcendentals=0),
        name=name,
    )(*given)


SLAB, FACE = (ROWS, COLS, DEPTH), (4, COLS, DEPTH)


def ring_of(ids):
    return ids[1] & 3, ids[1] >> 2


def serves_upper(start, ids):
    ring, upper = ring_of(ids)
    first = start >> 6
    return ((first + ((ring - first) & 3)) >> 2) == upper


def faces_kernel(ids, fwd, bwd, dens, vel, core, cross, own_fwd, own_bwd, dens_out, vel_out):
    parity = ids[0] & 1
    for f, (field, own) in enumerate(((fwd, own_fwd), (bwd, own_bwd))):
        core[f] = field[pl.ds(pl.multiple_of((1 - parity) * 4, 4), 4)]
        own[...] = field[pl.ds(pl.multiple_of(parity * 4, 4), 4)]
        high = own[...].astype(BF16)
        cross[f, :4] = high
        near = parity * 3
        low = (own[near] - own[near].astype(BF16).astype(F32)).astype(BF16)
        cross[f, 4] = low
        own[...] = high.astype(F32)
        own[near] += low.astype(F32)
    dens_out[...] = dens[...]
    vel_out[...] = vel[...]


def select_kernel(base, s1, s2, s3, dens, vel, other_dens, other_vel, *outs):
    *outs, nums = outs
    numbers = [base[i] for i in range(4)] + [s1[0], s2[0], s3[0]]
    for i in range(7):
        nums[i] = numbers[i]
    for i, start in enumerate((numbers[2], numbers[6], numbers[5], numbers[4])):
        mine = serves_upper(start, numbers)

        @pl.when(mine)
        def _():
            outs[i][...] = dens[...]
            outs[4 + i][...] = vel[...]

        @pl.when(jnp.logical_not(mine))
        def _():
            outs[i][...] = other_dens[...]
            outs[4 + i][...] = other_vel[...]


def window_pick(ids):
    ring, _ = ring_of(ids)
    first, offset = ids[2] >> 6, ids[2] & 63
    want = lax.broadcasted_iota(jnp.int32, (COLS, TILE), 0) + offset
    within = lax.broadcasted_iota(jnp.int32, (COLS, TILE), 1)
    picks = [jnp.where(within + ((ring - s - first) & 3) * TILE == want, 1.0, 0.0) for s in range(4)]
    return jnp.concatenate(picks, axis=1).astype(BF16)


def window_dens_kernel(ids, t0, t1, t2, t3, dens_out, cross_out, wide):
    parity = ids[0] & 1
    pick = window_pick(ids)
    for s, tile in enumerate((t0, t1, t2, t3)):
        wide[:, s * TILE : (s + 1) * TILE, :] = tile[...]
    for r in range(ROWS):
        dens_out[r] = jnp.dot(pick, wide[r], preferred_element_type=F32)
    cross_out[...] = dens_out[pl.ds(pl.multiple_of(parity * 4, 4), 4)].astype(BF16)


def coef_kernel(ids, t0, t1, t2, t3, dens, depth_w, cols_w, coef, s1, s2, logs, core_out, wide):
    core_out[...] = dens[pl.ds(pl.multiple_of((1 - (ids[0] & 1)) * 4, 4), 4)].astype(BF16)
    pick = window_pick(ids)
    for s, tile in enumerate((t0, t1, t2, t3)):
        wide[:, s * TILE : (s + 1) * TILE, :] = tile[...]
    for r in range(ROWS):
        speed = jnp.dot(pick, wide[r], preferred_element_type=F32)
        c = speed * speed
        coef[r] = c * LAP_SCALE
        log = jnp.log(dens[r])
        logs[r] = log
        high, low = halves(log)
        cs = c * (SLOPE_SCALE * SLOPE_SCALE)
        s1[r] = cs * (
            jnp.dot(cols_w[COLS:], high, preferred_element_type=F32)
            + jnp.dot(cols_w[COLS:], low, preferred_element_type=F32)
        )
        s2[r] = cs * (
            jnp.dot(high, depth_w[:, DEPTH:], preferred_element_type=F32)
            + jnp.dot(low, depth_w[:, DEPTH:], preferred_element_type=F32)
        )


def row_slope_kernel(ids, logs, core, cross, coef, s0, halo):
    parity, place = ids[0] & 1, ids[0]
    pad = jnp.where((place == 0) | (place == 15), 1.0, 0.0).astype(F32)
    load_halo(halo, parity, jnp.log(core[...].astype(F32)), jnp.log(cross[...].astype(F32) + pad))

    def body(i, carry):
        at = pl.ds(pl.multiple_of(i * 8, 8), 8)
        rows = extended_rows(halo, logs, 0, ROWS, at)
        for r in range(ROWS):
            s0[r, at, :] = (coef[r, at, :] * (SLOPE_SCALE * SLOPE_SCALE / LAP_SCALE)) * row_slope_of(rows, r)
        return carry

    lax.fori_loop(0, COLS // 8, body, 0)


def step_kernel(mode, first, moment, *refs):
    refs = list(refs)
    ids = refs.pop(0)
    amount = refs.pop(0) if mode == "fwd" else None
    prev, now, core, cross = refs[:4]
    refs = refs[4:]
    which = 0 if mode == "fwd" else 1
    if first:
        own = refs.pop(0)
    else:
        qr_now, qr_prev, qs_now, qs_prev = refs[:4]
        refs = refs[4:]
    plane = refs.pop(0) if mode == "bwd" else None
    coef, s0, s1, s2, depth_w, cols_w = refs[:6]
    refs = refs[6:]
    out = refs.pop(0)
    last = len(refs) == 3
    if not last:
        core_out, cross_out, qr_out, qs_out = refs[:4]
        refs = refs[4:]
    halo, zz, cc = refs
    parity = ids[0] & 1
    if first:
        load_halo(halo, parity, core[which], cross[which, :4].astype(F32))
        halo[3 + parity] += cross[which, 4].astype(F32)
    else:
        seen = (2.0 * qr_now[...] - qr_prev[...]) + cross[...].astype(F32)
        load_halo(halo, parity, core[...], seen)
    if not last:
        qr_out[...] = halo[pl.ds(pl.multiple_of(parity * 4, 4), 4)]

    def products(r):
        high, low = halves(now[r])
        zz[r] = jnp.dot(high, depth_w[...], preferred_element_type=F32) + jnp.dot(
            low, depth_w[...], preferred_element_type=F32
        )
        cc[r] = jnp.dot(cols_w[...], high, preferred_element_type=F32) + jnp.dot(
            cols_w[...], low, preferred_element_type=F32
        )

    def update(first_row, i):
        at = pl.ds(i * 8, 8)
        at2 = pl.ds(COLS + i * 8, 8)
        rows = extended_rows(halo, now, first_row, 2, at)
        for r in (first_row, first_row + 1):
            lap = (3.0 * LAP[0]) * rows[r] + (cc[r, at, :] + zz[r, at, :DEPTH])
            for k in range(1, 5):
                lap += LAP[k] * (rows[r + k] + rows[r - k])
            drift = (
                s0[r, at, :] * row_slope_of(rows, r)
                + s1[r, at, :] * cc[r, at2, :]
                + s2[r, at, :] * zz[r, at, DEPTH:]
            )
            new = 2.0 * rows[r] - prev[r, at, :] + (coef[r, at, :] * lap - drift)
            if mode == "bwd":
                out[r, at, :128] = new[:, :128] + plane[moment, r, at, :]
                out[r, at, 128:] = new[:, 128:]
            else:
                out[r, at, :] = new

    for r in range(0, ROWS + 2, 2):
        if r < ROWS:
            products(r)
            products(r + 1)
        if r > 0:
            for i in range(COLS // 8):
                update(r - 2, i)

    if mode == "fwd":

        line = ids[3] >> 8
        row = lax.div(line, COLS) - ids[0] * ROWS

        @pl.when((row >= 0) & (row < ROWS))
        def _():
            col = lax.rem(line, COLS)
            base = pl.multiple_of(col & ~7, 8)
            col_in = lax.broadcasted_iota(jnp.int32, (8, DEPTH), 0)
            depth_in = lax.broadcasted_iota(jnp.int32, (8, DEPTH), 1)
            struck = (col_in == (col & 7)) & (depth_in == (ids[3] & 255))
            out[row, pl.ds(base, 8), :] += jnp.where(struck, amount[moment], 0.0)

    if not last:
        core_out[...] = out[pl.ds(pl.multiple_of((1 - parity) * 4, 4), 4)]
        rows = out[pl.ds(pl.multiple_of(parity * 4, 4), 4)]
        if first:
            base = own[...]
        else:
            base = 2.0 * qs_now[...] - qs_prev[...]
        sent = (rows - base).astype(BF16)
        cross_out[...] = sent
        qs_out[...] = base + sent.astype(F32)


def step(mode, moment, ids, source, prev, now, core, cross, quant, planes, fields, tables):
    first, last = moment == 0, moment == STEPS - 1
    args = [ids]
    if mode == "fwd":
        args.append(source)
    args += [prev, now, core, cross] + list(quant)
    if mode == "bwd":
        args.append(planes)
    args += list(fields) + list(tables)
    outs = [(SLAB, F32)]
    if not last:
        outs += [(FACE, F32), (FACE, BF16), (FACE, F32), (FACE, F32)]
    scratch = [
        pltpu.VMEM((8, COLS, DEPTH), F32),
        pltpu.VMEM((ROWS, COLS, 2 * DEPTH), F32),
        pltpu.VMEM((ROWS, 2 * COLS, DEPTH), F32),
    ]
    return call(functools.partial(step_kernel, mode, first, moment), args, outs, scratch, "step_" + mode, 20_000_000_000)


def blocks_kernel(ids, part, a5, s0, a0, s5, *blocks):
    ring, _ = ring_of(ids)
    first, offset = ids[2] >> 6, ids[2] & 63
    within = lax.broadcasted_iota(jnp.int32, (TILE, COLS), 0)
    column = lax.broadcasted_iota(jnp.int32, (TILE, COLS), 1) + offset
    picks = [jnp.where(within + ((ring + s - first) & 3) * TILE == column, 1.0, 0.0) for s in range(4)]
    pick = jnp.concatenate(picks, axis=0).astype(BF16)
    for r in range(ROWS):
        total = part[r] + a5[r] * s0[r] + a0[r] * s5[r]
        high, low = halves(total)
        placed = jnp.dot(pick, high, preferred_element_type=F32) + jnp.dot(
            pick, low, preferred_element_type=F32
        )
        for s in range(4):
            blocks[s if r < SPLIT else 4 + s][r if r < SPLIT else r - SPLIT] = placed[s * TILE : (s + 1) * TILE]


def combine_kernel(ids, b0, b1, b2, b3, keep, give):
    flags = [jnp.where(serves_upper(ids[i], ids), 1.0, 0.0).astype(F32) for i in (2, 4, 5, 6)]
    for r in range(keep.shape[0]):
        kept = flags[0] * b0[r]
        total = b0[r]
        for flag, block in zip(flags[1:], (b1, b2, b3)):
            kept += flag * block[r]
            total += block[r]
        keep[r] = kept
        gave = (1.0 - flags[0]) * b0[r]
        for flag, block in zip(flags[1:], (b1, b2, b3)):
            gave += (1.0 - flag) * block[r]
        give[r] = gave


def shards(
    forward_prev,
    forward_now,
    adjoint_prev,
    adjoint_now,
    velocity,
    density,
    anchors,
    shot_cell,
    wavelet,
    records,
):
    tables = weight_tables()
    place = lax.axis_index("apert")
    shot = lax.axis_index("shot")
    count = lax.axis_size("apert")
    groups = lax.axis_size("shot")
    half = groups // 2
    ids = jnp.stack([place, shot]).astype(jnp.int32)
    core_pairs = [(i, i ^ 1) for i in range(count)]
    cross_pairs = [(i, i + 1) for i in range(1, count - 1, 2)] + [(i + 1, i) for i in range(1, count - 1, 2)]
    side_pairs = [(i, (i + half) % groups) for i in range(groups)]

    def ring_pairs(shift):
        return [(i, (i // half) * half + (i % half + shift) % half) for i in range(groups)]

    def swap(core, cross):
        return lax.ppermute(core, "apert", core_pairs), lax.ppermute(cross, "apert", cross_pairs)

    both_ways = [
        (i * count + j, ((i // half) * half + (i % half + (1 if j % 2 == 0 else -1)) % half) * count + j)
        for i in range(groups)
        for j in range(count)
    ]

    def ring_send(pieces):
        halfway = lax.ppermute(pieces[2], ("shot", "apert"), both_ways)
        near = lax.ppermute(pieces[1], "shot", ring_pairs(1)), lax.ppermute(pieces[3], "shot", ring_pairs(3))
        return [pieces[0], near[0], lax.ppermute(halfway, ("shot", "apert"), both_ways), near[1]]

    def ring_direct(pieces):
        return [pieces[0]] + [lax.ppermute(pieces[k], "shot", ring_pairs(k)) for k in (1, 2, 3)]

    starts = [lax.ppermute(anchors, "shot", ring_pairs(k)) for k in range(1, half)]
    other_dens = lax.ppermute(density, "shot", side_pairs)
    other_vel = lax.ppermute(velocity, "shot", side_pairs)
    base = jnp.concatenate([ids, anchors, shot_cell])
    tile = ((ROWS, TILE, DEPTH), BF16)
    fwd_prev, fwd_now, bwd_prev, bwd_now = forward_prev[0], forward_now[0], adjoint_prev[0], adjoint_now[0]
    first_core, first_cross, own_fwd, own_bwd, dens, vel = call(
        faces_kernel,
        [base, fwd_now, bwd_now, density, velocity],
        [((2,) + FACE, F32), ((2, 5, COLS, DEPTH), BF16), (FACE, F32), (FACE, F32), tile, tile],
        name="faces",
    )
    *picked, nums = call(
        select_kernel,
        [base, *starts, dens, vel, other_dens, other_vel],
        [tile] * (2 * half) + [((7,), jnp.int32)],
        name="select",
        flops=20_000_000_000,
    )
    first_cross, *picked = lax.optimization_barrier((first_cross, *picked))
    first_cross = lax.ppermute(first_cross, "apert", cross_pairs)
    dens_tiles = ring_direct(picked[:half])
    later = lax.optimization_barrier((dens_tiles[1], dens_tiles[3], *picked[half:]))
    dens_tiles[1], dens_tiles[3] = later[:2]
    vel_tiles = ring_direct(later[2:])
    lane = lax.broadcasted_iota(jnp.int32, (1, 1, 1, 128), 3)
    planes = jnp.where(lane == SURF, records[0][..., None], 0.0)
    first_core = lax.ppermute(first_core, "apert", core_pairs)
    first_core, first_cross, planes, *dens_tiles = lax.optimization_barrier(
        (first_core, first_cross, planes, *dens_tiles)
    )

    wide = [pltpu.VMEM((ROWS, 4 * TILE, DEPTH), BF16)]
    dens, dens_cross = call(
        window_dens_kernel,
        [nums, *dens_tiles],
        [(SLAB, F32), (FACE, BF16)],
        wide,
        "window_dens",
        20_000_000_000,
    )
    dens_cross = lax.ppermute(dens_cross, "apert", cross_pairs)
    coef, slope1, slope2, logs, dens_core = call(
        coef_kernel, [nums, *vel_tiles, dens, *tables], [(SLAB, F32)] * 4 + [(FACE, BF16)], wide, "coef", 20_000_000_000
    )
    dens_core = lax.ppermute(dens_core, "apert", core_pairs)
    (slope0,) = call(
        row_slope_kernel,
        [nums, logs, dens_core, dens_cross, coef],
        [(SLAB, F32)],
        [pltpu.VMEM((8, COLS, DEPTH), F32)],
        "row_slope",
    )
    fields = (coef, slope0, slope1, slope2)
    source = wavelet[0]

    fwd_core = bwd_core = first_core
    fwd_cross = bwd_cross = first_cross
    fwd_quant, bwd_quant = (own_fwd,), (own_bwd,)
    snapshots, states = [], []
    for moment in range(STEPS):
        last = moment == STEPS - 1
        if moment > 0:
            fwd_core, fwd_cross = swap(fwd_core, fwd_cross)
        new, *sent = step(
            "fwd", moment, nums, source, fwd_prev, fwd_now, fwd_core, fwd_cross, fwd_quant, None, fields, tables
        )
        if not last:
            own = own_fwd if moment == 0 else fwd_quant[2]
            fwd_core, fwd_cross, seen, shown = sent
            fwd_quant = (seen, seen if moment == 0 else fwd_quant[0], shown, own)
        snapshots.append(new)
        fwd_prev, fwd_now = fwd_now, new

        if moment > 0:
            bwd_core, bwd_cross = swap(bwd_core, bwd_cross)
        new, *sent = step(
            "bwd", moment, nums, source, bwd_prev, bwd_now, bwd_core, bwd_cross, bwd_quant, planes, fields, tables
        )
        if not last:
            own = own_bwd if moment == 0 else bwd_quant[2]
            bwd_core, bwd_cross, seen, shown = sent
            bwd_quant = (seen, seen if moment == 0 else bwd_quant[0], shown, own)
        states.append(new)
        bwd_prev, bwd_now = bwd_now, new
    part = sum(states[t] * snapshots[STEPS - 1 - t] for t in range(1, STEPS - 1))

    head, rest = ((SPLIT, TILE, DEPTH), F32), ((ROWS - SPLIT, TILE, DEPTH), F32)
    blocks = call(
        blocks_kernel,
        [nums, part, states[STEPS - 1], snapshots[0], states[0], snapshots[STEPS - 1]],
        [head] * half + [rest] * half,
        name="blocks",
    )
    arrived = [ring_send(blocks[:half]), ring_send(blocks[half:])]
    rows = []
    for each, block in zip(arrived, (head, rest)):
        keep, give = call(combine_kernel, [nums, *each], [block] * 2, name="combine")
        rows.append(keep + lax.ppermute(give, "shot", side_pairs))
    image = jnp.concatenate(rows, axis=0)
    return image, states[STEPS - 1][None]


def solution(mesh):
    placed = (
        P("shot", "apert", None, None),
        P("shot", "apert", None, None),
        P("shot", "apert", None, None),
        P("shot", "apert", None, None),
        P("apert", "shot", None),
        P("apert", "shot", None),
        P("shot"),
        P("shot"),
        P("shot", None),
        P("shot", None, "apert", None),
    )
    return jax.shard_map(
        shards,
        mesh=mesh,
        in_specs=placed,
        out_specs=(P("apert", "shot", None), P("shot", "apert", None, None)),
        check_vma=False,
    )
```

```python
import functools

import jax
import jax.numpy as jnp
import ml_dtypes
import numpy as np
from jax import lax
from jax.experimental import pallas as pl
from jax.experimental.pallas import tpu as pltpu
from jax.sharding import PartitionSpec as P

STEPS = 6
SURF = 8
ROWS, COLS, DEPTH = 8, 160, 256
TILE = 64
SPLIT = 4
LAP = (-14350.0, 8064.0, -1008.0, 128.0, -9.0)
SLOPE = (672.0, -168.0, 32.0, -3.0)
LAP_SCALE, SLOPE_SCALE = 1.0 / 5040.0, 1.0 / 840.0
F32, BF16 = jnp.float32, jnp.bfloat16
VMEM = pl.BlockSpec(memory_space=pltpu.VMEM)
SMEM = pl.BlockSpec(memory_space=pltpu.SMEM)
PARAMS = pltpu.CompilerParams(vmem_limit_bytes=16 * 1024 * 1024)


def banded(size):
    lap, slope = np.zeros((size, size)), np.zeros((size, size))
    for k in range(1, 5):
        lap += LAP[k] * (np.eye(size, k=k) + np.eye(size, k=-k))
        slope += SLOPE[k - 1] * (np.eye(size, k=k) - np.eye(size, k=-k))
    return lap, slope


def weight_tables():
    lap, slope = banded(DEPTH)
    depth_table = np.concatenate([lap.T, slope.T], axis=1).astype(ml_dtypes.bfloat16)
    lap, slope = banded(COLS)
    cols_table = np.concatenate([lap, slope], axis=0).astype(ml_dtypes.bfloat16)
    return jnp.asarray(depth_table), jnp.asarray(cols_table)


def halves(x):
    high = x.astype(BF16)
    return high, (x - high.astype(F32)).astype(BF16)


def load_halo(halo, parity, core_rows, cross_rows):
    halo[pl.ds(pl.multiple_of((1 - parity) * 4, 4), 4)] = core_rows
    halo[pl.ds(pl.multiple_of(parity * 4, 4), 4)] = cross_rows


def extended_rows(halo, mid, first, count, at):
    rows = {}
    for r in range(first - 4, first + count + 4):
        if r < 0:
            rows[r] = halo[r + 4, at, :]
        elif r < ROWS:
            rows[r] = mid[r, at, :]
        else:
            rows[r] = halo[r - ROWS + 4, at, :]
    return rows


def row_slope_of(rows, r):
    total = None
    for k in range(1, 5):
        term = SLOPE[k - 1] * (rows[r + k] - rows[r - k])
        total = term if total is None else total + term
    return total


def call(body, args, outs, scratch=(), name=None, flops=10_000_000):
    specs, given = [], []
    for arg in args:
        if arg.ndim == 1:
            specs.append(SMEM)
            given.append(arg)
        else:
            specs.append(VMEM)
            given.append(pltpu.with_memory_space_constraint(arg, pltpu.VMEM))
    return pl.pallas_call(
        body,
        out_shape=[
            jax.ShapeDtypeStruct(shape, dtype) if len(shape) == 1 else pltpu.VMEM(shape, dtype)
            for shape, dtype in outs
        ],
        in_specs=specs,
        out_specs=[SMEM if len(shape) == 1 else VMEM for shape, _ in outs],
        scratch_shapes=list(scratch),
        compiler_params=PARAMS,
        cost_estimate=pl.CostEstimate(flops=flops, bytes_accessed=100_000, transcendentals=0),
        name=name,
    )(*given)


SLAB, FACE = (ROWS, COLS, DEPTH), (4, COLS, DEPTH)


def ring_of(ids):
    return ids[1] & 3, ids[1] >> 2


def serves_upper(start, ids):
    ring, upper = ring_of(ids)
    first = start >> 6
    return ((first + ((ring - first) & 3)) >> 2) == upper


def faces_kernel(ids, fwd, bwd, dens, vel, core, cross, own_fwd, own_bwd, dens_out, vel_out):
    parity = ids[0] & 1
    for f, (field, own) in enumerate(((fwd, own_fwd), (bwd, own_bwd))):
        core[f] = field[pl.ds(pl.multiple_of((1 - parity) * 4, 4), 4)]
        own[...] = field[pl.ds(pl.multiple_of(parity * 4, 4), 4)]
        high = own[...].astype(BF16)
        cross[f, :4] = high
        near = parity * 3
        low = (own[near] - own[near].astype(BF16).astype(F32)).astype(BF16)
        cross[f, 4] = low
        own[...] = high.astype(F32)
        own[near] += low.astype(F32)
    dens_out[...] = dens[...]
    vel_out[...] = vel[...]


def select_kernel(base, s1, s2, s3, dens, vel, other_dens, other_vel, *outs):
    *outs, nums = outs
    numbers = [base[i] for i in range(4)] + [s1[0], s2[0], s3[0]]
    for i in range(7):
        nums[i] = numbers[i]
    for i, start in enumerate((numbers[2], numbers[6], numbers[5], numbers[4])):
        mine = serves_upper(start, numbers)

        @pl.when(mine)
        def _():
            outs[i][...] = dens[...]
            outs[4 + i][...] = vel[...]

        @pl.when(jnp.logical_not(mine))
        def _():
            outs[i][...] = other_dens[...]
            outs[4 + i][...] = other_vel[...]


def window_pick(ids):
    ring, _ = ring_of(ids)
    first, offset = ids[2] >> 6, ids[2] & 63
    want = lax.broadcasted_iota(jnp.int32, (COLS, TILE), 0) + offset
    within = lax.broadcasted_iota(jnp.int32, (COLS, TILE), 1)
    picks = [jnp.where(within + ((ring - s - first) & 3) * TILE == want, 1.0, 0.0) for s in range(4)]
    return jnp.concatenate(picks, axis=1).astype(BF16)


def window_dens_kernel(ids, t0, t1, t2, t3, dens_out, cross_out, wide):
    parity = ids[0] & 1
    pick = window_pick(ids)
    for s, tile in enumerate((t0, t1, t2, t3)):
        wide[:, s * TILE : (s + 1) * TILE, :] = tile[...]
    for r in range(ROWS):
        dens_out[r] = jnp.dot(pick, wide[r], preferred_element_type=F32)
    cross_out[...] = dens_out[pl.ds(pl.multiple_of(parity * 4, 4), 4)].astype(BF16)


def coef_kernel(ids, t0, t1, t2, t3, dens, depth_w, cols_w, coef, s1, s2, logs, core_out, wide):
    core_out[...] = dens[pl.ds(pl.multiple_of((1 - (ids[0] & 1)) * 4, 4), 4)].astype(BF16)
    pick = window_pick(ids)
    for s, tile in enumerate((t0, t1, t2, t3)):
        wide[:, s * TILE : (s + 1) * TILE, :] = tile[...]
    for r in range(ROWS):
        speed = jnp.dot(pick, wide[r], preferred_element_type=F32)
        c = speed * speed
        coef[r] = c * LAP_SCALE
        log = jnp.log(dens[r])
        logs[r] = log
        high, low = halves(log)
        cs = c * (SLOPE_SCALE * SLOPE_SCALE)
        s1[r] = cs * (
            jnp.dot(cols_w[COLS:], high, preferred_element_type=F32)
            + jnp.dot(cols_w[COLS:], low, preferred_element_type=F32)
        )
        s2[r] = cs * (
            jnp.dot(high, depth_w[:, DEPTH:], preferred_element_type=F32)
            + jnp.dot(low, depth_w[:, DEPTH:], preferred_element_type=F32)
        )


def row_slope_kernel(ids, logs, core, cross, coef, s0, halo):
    parity, place = ids[0] & 1, ids[0]
    pad = jnp.where((place == 0) | (place == 15), 1.0, 0.0).astype(F32)
    load_halo(halo, parity, jnp.log(core[...].astype(F32)), jnp.log(cross[...].astype(F32) + pad))

    def body(i, carry):
        at = pl.ds(pl.multiple_of(i * 8, 8), 8)
        rows = extended_rows(halo, logs, 0, ROWS, at)
        for r in range(ROWS):
            s0[r, at, :] = (coef[r, at, :] * (SLOPE_SCALE * SLOPE_SCALE / LAP_SCALE)) * row_slope_of(rows, r)
        return carry

    lax.fori_loop(0, COLS // 8, body, 0)


def step_kernel(mode, first, moment, *refs):
    refs = list(refs)
    ids = refs.pop(0)
    amount = refs.pop(0) if mode == "fwd" else None
    prev, now, core, cross = refs[:4]
    refs = refs[4:]
    which = 0 if mode == "fwd" else 1
    if first:
        own = refs.pop(0)
    else:
        qr_now, qr_prev, qs_now, qs_prev = refs[:4]
        refs = refs[4:]
    plane = refs.pop(0) if mode == "bwd" else None
    coef, s0, s1, s2, depth_w, cols_w = refs[:6]
    refs = refs[6:]
    out = refs.pop(0)
    last = len(refs) == 3
    if not last:
        core_out, cross_out, qr_out, qs_out = refs[:4]
        refs = refs[4:]
    halo, zz, cc = refs
    parity = ids[0] & 1
    if first:
        load_halo(halo, parity, core[which], cross[which, :4].astype(F32))
        halo[3 + parity] += cross[which, 4].astype(F32)
    else:
        seen = (2.0 * qr_now[...] - qr_prev[...]) + cross[...].astype(F32)
        load_halo(halo, parity, core[...], seen)
    if not last:
        qr_out[...] = halo[pl.ds(pl.multiple_of(parity * 4, 4), 4)]

    def products(r):
        high, low = halves(now[r])
        zz[r] = jnp.dot(high, depth_w[...], preferred_element_type=F32) + jnp.dot(
            low, depth_w[...], preferred_element_type=F32
        )
        cc[r] = jnp.dot(cols_w[...], high, preferred_element_type=F32) + jnp.dot(
            cols_w[...], low, preferred_element_type=F32
        )

    def update(first_row, i):
        at = pl.ds(i * 8, 8)
        at2 = pl.ds(COLS + i * 8, 8)
        rows = extended_rows(halo, now, first_row, 2, at)
        for r in (first_row, first_row + 1):
            lap = (3.0 * LAP[0]) * rows[r] + (cc[r, at, :] + zz[r, at, :DEPTH])
            for k in range(1, 5):
                lap += LAP[k] * (rows[r + k] + rows[r - k])
            drift = (
                s0[r, at, :] * row_slope_of(rows, r)
                + s1[r, at, :] * cc[r, at2, :]
                + s2[r, at, :] * zz[r, at, DEPTH:]
            )
            new = 2.0 * rows[r] - prev[r, at, :] + (coef[r, at, :] * lap - drift)
            if mode == "bwd":
                out[r, at, :128] = new[:, :128] + plane[moment, r, at, :]
                out[r, at, 128:] = new[:, 128:]
            else:
                out[r, at, :] = new

    for r in range(0, ROWS + 2, 2):
        if r < ROWS:
            products(r)
            products(r + 1)
        if r > 0:
            for i in range(COLS // 8):
                update(r - 2, i)

    if mode == "fwd":

        line = ids[3] >> 8
        row = lax.div(line, COLS) - ids[0] * ROWS

        @pl.when((row >= 0) & (row < ROWS))
        def _():
            col = lax.rem(line, COLS)
            base = pl.multiple_of(col & ~7, 8)
            col_in = lax.broadcasted_iota(jnp.int32, (8, DEPTH), 0)
            depth_in = lax.broadcasted_iota(jnp.int32, (8, DEPTH), 1)
            struck = (col_in == (col & 7)) & (depth_in == (ids[3] & 255))
            out[row, pl.ds(base, 8), :] += jnp.where(struck, amount[moment], 0.0)

    if not last:
        core_out[...] = out[pl.ds(pl.multiple_of((1 - parity) * 4, 4), 4)]
        rows = out[pl.ds(pl.multiple_of(parity * 4, 4), 4)]
        if first:
            base = own[...]
        else:
            base = 2.0 * qs_now[...] - qs_prev[...]
        sent = (rows - base).astype(BF16)
        cross_out[...] = sent
        qs_out[...] = base + sent.astype(F32)


def step(mode, moment, ids, source, prev, now, core, cross, quant, planes, fields, tables):
    first, last = moment == 0, moment == STEPS - 1
    args = [ids]
    if mode == "fwd":
        args.append(source)
    args += [prev, now, core, cross] + list(quant)
    if mode == "bwd":
        args.append(planes)
    args += list(fields) + list(tables)
    outs = [(SLAB, F32)]
    if not last:
        outs += [(FACE, F32), (FACE, BF16), (FACE, F32), (FACE, F32)]
    scratch = [
        pltpu.VMEM((8, COLS, DEPTH), F32),
        pltpu.VMEM((ROWS, COLS, 2 * DEPTH), F32),
        pltpu.VMEM((ROWS, 2 * COLS, DEPTH), F32),
    ]
    return call(functools.partial(step_kernel, mode, first, moment), args, outs, scratch, "step_" + mode, 20_000_000_000)


def blocks_kernel(ids, part, a5, s0, a0, s5, *blocks):
    ring, _ = ring_of(ids)
    first, offset = ids[2] >> 6, ids[2] & 63
    within = lax.broadcasted_iota(jnp.int32, (TILE, COLS), 0)
    column = lax.broadcasted_iota(jnp.int32, (TILE, COLS), 1) + offset
    picks = [jnp.where(within + ((ring + s - first) & 3) * TILE == column, 1.0, 0.0) for s in range(4)]
    pick = jnp.concatenate(picks, axis=0).astype(BF16)
    for r in range(ROWS):
        total = part[r] + a5[r] * s0[r] + a0[r] * s5[r]
        high, low = halves(total)
        placed = jnp.dot(pick, high, preferred_element_type=F32) + jnp.dot(
            pick, low, preferred_element_type=F32
        )
        for s in range(4):
            blocks[s if r < SPLIT else 4 + s][r if r < SPLIT else r - SPLIT] = placed[s * TILE : (s + 1) * TILE]


def combine_kernel(ids, b0, b1, b2, b3, keep, give):
    flags = [jnp.where(serves_upper(ids[i], ids), 1.0, 0.0).astype(F32) for i in (2, 4, 5, 6)]
    for r in range(keep.shape[0]):
        kept = flags[0] * b0[r]
        total = b0[r]
        for flag, block in zip(flags[1:], (b1, b2, b3)):
            kept += flag * block[r]
            total += block[r]
        keep[r] = kept
        gave = (1.0 - flags[0]) * b0[r]
        for flag, block in zip(flags[1:], (b1, b2, b3)):
            gave += (1.0 - flag) * block[r]
        give[r] = gave


def shards(
    forward_prev,
    forward_now,
    adjoint_prev,
    adjoint_now,
    velocity,
    density,
    anchors,
    shot_cell,
    wavelet,
    records,
):
    tables = weight_tables()
    place = lax.axis_index("apert")
    shot = lax.axis_index("shot")
    count = lax.axis_size("apert")
    groups = lax.axis_size("shot")
    half = groups // 2
    ids = jnp.stack([place, shot]).astype(jnp.int32)
    core_pairs = [(i, i ^ 1) for i in range(count)]
    cross_pairs = [(i, i + 1) for i in range(1, count - 1, 2)] + [(i + 1, i) for i in range(1, count - 1, 2)]
    side_pairs = [(i, (i + half) % groups) for i in range(groups)]

    def ring_pairs(shift):
        return [(i, (i // half) * half + (i % half + shift) % half) for i in range(groups)]

    def swap(core, cross):
        return lax.ppermute(core, "apert", core_pairs), lax.ppermute(cross, "apert", cross_pairs)

    both_ways = [
        (i * count + j, ((i // half) * half + (i % half + (1 if j % 2 == 0 else -1)) % half) * count + j)
        for i in range(groups)
        for j in range(count)
    ]

    def ring_send(pieces):
        halfway = lax.ppermute(pieces[2], ("shot", "apert"), both_ways)
        near = lax.ppermute(pieces[1], "shot", ring_pairs(1)), lax.ppermute(pieces[3], "shot", ring_pairs(3))
        return [pieces[0], near[0], lax.ppermute(halfway, ("shot", "apert"), both_ways), near[1]]

    def ring_direct(pieces):
        return [pieces[0]] + [lax.ppermute(pieces[k], "shot", ring_pairs(k)) for k in (1, 2, 3)]

    starts = [lax.ppermute(anchors, "shot", ring_pairs(k)) for k in range(1, half)]
    other_dens = lax.ppermute(density, "shot", side_pairs)
    other_vel = lax.ppermute(velocity, "shot", side_pairs)
    base = jnp.concatenate([ids, anchors, shot_cell])
    tile = ((ROWS, TILE, DEPTH), BF16)
    fwd_prev, fwd_now, bwd_prev, bwd_now = forward_prev[0], forward_now[0], adjoint_prev[0], adjoint_now[0]
    first_core, first_cross, own_fwd, own_bwd, dens, vel = call(
        faces_kernel,
        [base, fwd_now, bwd_now, density, velocity],
        [((2,) + FACE, F32), ((2, 5, COLS, DEPTH), BF16), (FACE, F32), (FACE, F32), tile, tile],
        name="faces",
    )
    *picked, nums = call(
        select_kernel,
        [base, *starts, dens, vel, other_dens, other_vel],
        [tile] * (2 * half) + [((7,), jnp.int32)],
        name="select",
        flops=20_000_000_000,
    )
    first_cross, *picked = lax.optimization_barrier((first_cross, *picked))
    first_cross = lax.ppermute(first_cross, "apert", cross_pairs)
    dens_tiles = ring_direct(picked[:half])
    later = lax.optimization_barrier((dens_tiles[1], dens_tiles[3], *picked[half:]))
    dens_tiles[1], dens_tiles[3] = later[:2]
    vel_tiles = ring_direct(later[2:])
    lane = lax.broadcasted_iota(jnp.int32, (1, 1, 1, 128), 3)
    planes = jnp.where(lane == SURF, records[0][..., None], 0.0)
    first_core = lax.ppermute(first_core, "apert", core_pairs)
    first_core, first_cross, planes, *dens_tiles = lax.optimization_barrier(
        (first_core, first_cross, planes, *dens_tiles)
    )

    wide = [pltpu.VMEM((ROWS, 4 * TILE, DEPTH), BF16)]
    dens, dens_cross = call(
        window_dens_kernel,
        [nums, *dens_tiles],
        [(SLAB, F32), (FACE, BF16)],
        wide,
        "window_dens",
        20_000_000_000,
    )
    dens_cross = lax.ppermute(dens_cross, "apert", cross_pairs)
    coef, slope1, slope2, logs, dens_core = call(
        coef_kernel, [nums, *vel_tiles, dens, *tables], [(SLAB, F32)] * 4 + [(FACE, BF16)], wide, "coef", 20_000_000_000
    )
    dens_core = lax.ppermute(dens_core, "apert", core_pairs)
    (slope0,) = call(
        row_slope_kernel,
        [nums, logs, dens_core, dens_cross, coef],
        [(SLAB, F32)],
        [pltpu.VMEM((8, COLS, DEPTH), F32)],
        "row_slope",
    )
    fields = (coef, slope0, slope1, slope2)
    source = wavelet[0]

    fwd_core = bwd_core = first_core
    fwd_cross = bwd_cross = first_cross
    fwd_quant, bwd_quant = (own_fwd,), (own_bwd,)
    snapshots, states = [], []
    for moment in range(STEPS):
        last = moment == STEPS - 1
        if moment > 0:
            fwd_core, fwd_cross = swap(fwd_core, fwd_cross)
        new, *sent = step(
            "fwd", moment, nums, source, fwd_prev, fwd_now, fwd_core, fwd_cross, fwd_quant, None, fields, tables
        )
        if not last:
            own = own_fwd if moment == 0 else fwd_quant[2]
            fwd_core, fwd_cross, seen, shown = sent
            fwd_quant = (seen, seen if moment == 0 else fwd_quant[0], shown, own)
        snapshots.append(new)
        fwd_prev, fwd_now = fwd_now, new

        if moment > 0:
            bwd_core, bwd_cross = swap(bwd_core, bwd_cross)
        new, *sent = step(
            "bwd", moment, nums, source, bwd_prev, bwd_now, bwd_core, bwd_cross, bwd_quant, planes, fields, tables
        )
        if not last:
            own = own_bwd if moment == 0 else bwd_quant[2]
            bwd_core, bwd_cross, seen, shown = sent
            bwd_quant = (seen, seen if moment == 0 else bwd_quant[0], shown, own)
        states.append(new)
        bwd_prev, bwd_now = bwd_now, new
    part = sum(states[t] * snapshots[STEPS - 1 - t] for t in range(1, STEPS - 1))

    head, rest = ((SPLIT, TILE, DEPTH), F32), ((ROWS - SPLIT, TILE, DEPTH), F32)
    blocks = call(
        blocks_kernel,
        [nums, part, states[STEPS - 1], snapshots[0], states[0], snapshots[STEPS - 1]],
        [head] * half + [rest] * half,
        name="blocks",
    )
    arrived = [ring_send(blocks[:half]), ring_send(blocks[half:])]
    rows = []
    for each, block in zip(arrived, (head, rest)):
        keep, give = call(combine_kernel, [nums, *each], [block] * 2, name="combine")
        rows.append(keep + lax.ppermute(give, "shot", side_pairs))
    image = jnp.concatenate(rows, axis=0)
    return image, states[STEPS - 1][None]


def solution(mesh):
    placed = (
        P("shot", "apert", None, None),
        P("shot", "apert", None, None),
        P("shot", "apert", None, None),
        P("shot", "apert", None, None),
        P("apert", "shot", None),
        P("apert", "shot", None),
        P("shot"),
        P("shot"),
        P("shot", None),
        P("shot", None, "apert", None),
    )
    return jax.shard_map(
        shards,
        mesh=mesh,
        in_specs=placed,
        out_specs=(P("apert", "shot", None), P("shot", "apert", None, None)),
        check_vma=False,
    )
```

```python
import functools

import jax
import jax.numpy as jnp
import ml_dtypes
import numpy as np
from jax import lax
from jax.experimental import pallas as pl
from jax.experimental.pallas import tpu as pltpu
from jax.sharding import PartitionSpec as P

STEPS = 6
SURF = 8
ROWS, COLS, DEPTH = 8, 160, 256
TILE = 64
SPLIT = 4
LAP = (-14350.0, 8064.0, -1008.0, 128.0, -9.0)
SLOPE = (672.0, -168.0, 32.0, -3.0)
LAP_SCALE, SLOPE_SCALE = 1.0 / 5040.0, 1.0 / 840.0
F32, BF16 = jnp.float32, jnp.bfloat16
VMEM = pl.BlockSpec(memory_space=pltpu.VMEM)
SMEM = pl.BlockSpec(memory_space=pltpu.SMEM)
PARAMS = pltpu.CompilerParams(vmem_limit_bytes=16 * 1024 * 1024)


def banded(size):
    lap, slope = np.zeros((size, size)), np.zeros((size, size))
    for k in range(1, 5):
        lap += LAP[k] * (np.eye(size, k=k) + np.eye(size, k=-k))
        slope += SLOPE[k - 1] * (np.eye(size, k=k) - np.eye(size, k=-k))
    return lap, slope


def weight_tables():
    lap, slope = banded(DEPTH)
    depth_table = np.concatenate([lap.T, slope.T], axis=1).astype(ml_dtypes.bfloat16)
    lap, slope = banded(COLS)
    cols_table = np.concatenate([lap, slope], axis=0).astype(ml_dtypes.bfloat16)
    return jnp.asarray(depth_table), jnp.asarray(cols_table)


def halves(x):
    high = x.astype(BF16)
    return high, (x - high.astype(F32)).astype(BF16)


def load_halo(halo, parity, core_rows, cross_rows):
    halo[pl.ds(pl.multiple_of((1 - parity) * 4, 4), 4)] = core_rows
    halo[pl.ds(pl.multiple_of(parity * 4, 4), 4)] = cross_rows


def extended_rows(halo, mid, first, count, at):
    rows = {}
    for r in range(first - 4, first + count + 4):
        if r < 0:
            rows[r] = halo[r + 4, at, :]
        elif r < ROWS:
            rows[r] = mid[r, at, :]
        else:
            rows[r] = halo[r - ROWS + 4, at, :]
    return rows


def row_slope_of(rows, r):
    total = None
    for k in range(1, 5):
        term = SLOPE[k - 1] * (rows[r + k] - rows[r - k])
        total = term if total is None else total + term
    return total


def call(body, args, outs, scratch=(), name=None, flops=10_000_000):
    specs, given = [], []
    for arg in args:
        if arg.ndim == 1:
            specs.append(SMEM)
            given.append(arg)
        else:
            specs.append(VMEM)
            given.append(pltpu.with_memory_space_constraint(arg, pltpu.VMEM))
    return pl.pallas_call(
        body,
        out_shape=[
            jax.ShapeDtypeStruct(shape, dtype) if len(shape) == 1 else pltpu.VMEM(shape, dtype)
            for shape, dtype in outs
        ],
        in_specs=specs,
        out_specs=[SMEM if len(shape) == 1 else VMEM for shape, _ in outs],
        scratch_shapes=list(scratch),
        compiler_params=PARAMS,
        cost_estimate=pl.CostEstimate(flops=flops, bytes_accessed=100_000, transcendentals=0),
        name=name,
    )(*given)


SLAB, FACE = (ROWS, COLS, DEPTH), (4, COLS, DEPTH)


def ring_of(ids):
    return ids[1] & 3, ids[1] >> 2


def serves_upper(start, ids):
    ring, upper = ring_of(ids)
    first = start >> 6
    return ((first + ((ring - first) & 3)) >> 2) == upper


def faces_kernel(ids, fwd, bwd, dens, vel, core, cross, own_fwd, own_bwd, dens_out, vel_out):
    parity = ids[0] & 1
    for f, (field, own) in enumerate(((fwd, own_fwd), (bwd, own_bwd))):
        core[f] = field[pl.ds(pl.multiple_of((1 - parity) * 4, 4), 4)]
        own[...] = field[pl.ds(pl.multiple_of(parity * 4, 4), 4)]
        high = own[...].astype(BF16)
        cross[f, :4] = high
        near = parity * 3
        low = (own[near] - own[near].astype(BF16).astype(F32)).astype(BF16)
        cross[f, 4] = low
        own[...] = high.astype(F32)
        own[near] += low.astype(F32)
    dens_out[...] = dens[...]
    vel_out[...] = vel[...]


def select_kernel(base, s1, s2, s3, dens, vel, other_dens, other_vel, *outs):
    *outs, nums = outs
    numbers = [base[i] for i in range(4)] + [s1[0], s2[0], s3[0]]
    for i in range(7):
        nums[i] = numbers[i]
    for i, start in enumerate((numbers[2], numbers[6], numbers[5], numbers[4])):
        mine = serves_upper(start, numbers)

        @pl.when(mine)
        def _():
            outs[i][...] = dens[...]
            outs[4 + i][...] = vel[...]

        @pl.when(jnp.logical_not(mine))
        def _():
            outs[i][...] = other_dens[...]
            outs[4 + i][...] = other_vel[...]


def window_pick(ids):
    ring, _ = ring_of(ids)
    first, offset = ids[2] >> 6, ids[2] & 63
    want = lax.broadcasted_iota(jnp.int32, (COLS, TILE), 0) + offset
    within = lax.broadcasted_iota(jnp.int32, (COLS, TILE), 1)
    picks = [jnp.where(within + ((ring - s - first) & 3) * TILE == want, 1.0, 0.0) for s in range(4)]
    return jnp.concatenate(picks, axis=1).astype(BF16)


def window_dens_kernel(ids, t0, t1, t2, t3, dens_out, cross_out, wide):
    parity = ids[0] & 1
    pick = window_pick(ids)
    for s, tile in enumerate((t0, t1, t2, t3)):
        wide[:, s * TILE : (s + 1) * TILE, :] = tile[...]
    for r in range(ROWS):
        dens_out[r] = jnp.dot(pick, wide[r], preferred_element_type=F32)
    cross_out[...] = dens_out[pl.ds(pl.multiple_of(parity * 4, 4), 4)].astype(BF16)


def coef_kernel(ids, t0, t1, t2, t3, dens, depth_w, cols_w, coef, s1, s2, logs, core_out, wide):
    core_out[...] = dens[pl.ds(pl.multiple_of((1 - (ids[0] & 1)) * 4, 4), 4)].astype(BF16)
    pick = window_pick(ids)
    for s, tile in enumerate((t0, t1, t2, t3)):
        wide[:, s * TILE : (s + 1) * TILE, :] = tile[...]
    for r in range(ROWS):
        speed = jnp.dot(pick, wide[r], preferred_element_type=F32)
        c = speed * speed
        coef[r] = c * LAP_SCALE
        log = jnp.log(dens[r])
        logs[r] = log
        high, low = halves(log)
        cs = c * (SLOPE_SCALE * SLOPE_SCALE)
        s1[r] = cs * (
            jnp.dot(cols_w[COLS:], high, preferred_element_type=F32)
            + jnp.dot(cols_w[COLS:], low, preferred_element_type=F32)
        )
        s2[r] = cs * (
            jnp.dot(high, depth_w[:, DEPTH:], preferred_element_type=F32)
            + jnp.dot(low, depth_w[:, DEPTH:], preferred_element_type=F32)
        )


def row_slope_kernel(ids, logs, core, cross, coef, s0, halo):
    parity, place = ids[0] & 1, ids[0]
    pad = jnp.where((place == 0) | (place == 15), 1.0, 0.0).astype(F32)
    load_halo(halo, parity, jnp.log(core[...].astype(F32)), jnp.log(cross[...].astype(F32) + pad))

    def body(i, carry):
        at = pl.ds(pl.multiple_of(i * 8, 8), 8)
        rows = extended_rows(halo, logs, 0, ROWS, at)
        for r in range(ROWS):
            s0[r, at, :] = (coef[r, at, :] * (SLOPE_SCALE * SLOPE_SCALE / LAP_SCALE)) * row_slope_of(rows, r)
        return carry

    lax.fori_loop(0, COLS // 8, body, 0)


def step_kernel(mode, first, moment, *refs):
    refs = list(refs)
    ids = refs.pop(0)
    amount = refs.pop(0) if mode == "fwd" else None
    prev, now, core, cross = refs[:4]
    refs = refs[4:]
    which = 0 if mode == "fwd" else 1
    if first:
        own = refs.pop(0)
    else:
        qr_now, qr_prev, qs_now, qs_prev = refs[:4]
        refs = refs[4:]
    plane = refs.pop(0) if mode == "bwd" else None
    coef, s0, s1, s2, depth_w, cols_w = refs[:6]
    refs = refs[6:]
    out = refs.pop(0)
    last = len(refs) == 3
    if not last:
        core_out, cross_out, qr_out, qs_out = refs[:4]
        refs = refs[4:]
    halo, zz, cc = refs
    parity = ids[0] & 1
    if first:
        load_halo(halo, parity, core[which], cross[which, :4].astype(F32))
        halo[3 + parity] += cross[which, 4].astype(F32)
    else:
        seen = (2.0 * qr_now[...] - qr_prev[...]) + cross[...].astype(F32)
        load_halo(halo, parity, core[...], seen)
    if not last:
        qr_out[...] = halo[pl.ds(pl.multiple_of(parity * 4, 4), 4)]

    def products(r):
        high, low = halves(now[r])
        zz[r] = jnp.dot(high, depth_w[...], preferred_element_type=F32) + jnp.dot(
            low, depth_w[...], preferred_element_type=F32
        )
        cc[r] = jnp.dot(cols_w[...], high, preferred_element_type=F32) + jnp.dot(
            cols_w[...], low, preferred_element_type=F32
        )

    def update(first_row, i):
        at = pl.ds(i * 8, 8)
        at2 = pl.ds(COLS + i * 8, 8)
        rows = extended_rows(halo, now, first_row, 2, at)
        for r in (first_row, first_row + 1):
            lap = (3.0 * LAP[0]) * rows[r] + (cc[r, at, :] + zz[r, at, :DEPTH])
            for k in range(1, 5):
                lap += LAP[k] * (rows[r + k] + rows[r - k])
            drift = (
                s0[r, at, :] * row_slope_of(rows, r)
                + s1[r, at, :] * cc[r, at2, :]
                + s2[r, at, :] * zz[r, at, DEPTH:]
            )
            new = 2.0 * rows[r] - prev[r, at, :] + (coef[r, at, :] * lap - drift)
            if mode == "bwd":
                out[r, at, :128] = new[:, :128] + plane[moment, r, at, :]
                out[r, at, 128:] = new[:, 128:]
            else:
                out[r, at, :] = new

    for r in range(0, ROWS + 2, 2):
        if r < ROWS:
            products(r)
            products(r + 1)
        if r > 0:
            for i in range(COLS // 8):
                update(r - 2, i)

    if mode == "fwd":

        line = ids[3] >> 8
        row = lax.div(line, COLS) - ids[0] * ROWS

        @pl.when((row >= 0) & (row < ROWS))
        def _():
            col = lax.rem(line, COLS)
            base = pl.multiple_of(col & ~7, 8)
            col_in = lax.broadcasted_iota(jnp.int32, (8, DEPTH), 0)
            depth_in = lax.broadcasted_iota(jnp.int32, (8, DEPTH), 1)
            struck = (col_in == (col & 7)) & (depth_in == (ids[3] & 255))
            out[row, pl.ds(base, 8), :] += jnp.where(struck, amount[moment], 0.0)

    if not last:
        core_out[...] = out[pl.ds(pl.multiple_of((1 - parity) * 4, 4), 4)]
        rows = out[pl.ds(pl.multiple_of(parity * 4, 4), 4)]
        if first:
            base = own[...]
        else:
            base = 2.0 * qs_now[...] - qs_prev[...]
        sent = (rows - base).astype(BF16)
        cross_out[...] = sent
        qs_out[...] = base + sent.astype(F32)


def step(mode, moment, ids, source, prev, now, core, cross, quant, planes, fields, tables):
    first, last = moment == 0, moment == STEPS - 1
    args = [ids]
    if mode == "fwd":
        args.append(source)
    args += [prev, now, core, cross] + list(quant)
    if mode == "bwd":
        args.append(planes)
    args += list(fields) + list(tables)
    outs = [(SLAB, F32)]
    if not last:
        outs += [(FACE, F32), (FACE, BF16), (FACE, F32), (FACE, F32)]
    scratch = [
        pltpu.VMEM((8, COLS, DEPTH), F32),
        pltpu.VMEM((ROWS, COLS, 2 * DEPTH), F32),
        pltpu.VMEM((ROWS, 2 * COLS, DEPTH), F32),
    ]
    return call(functools.partial(step_kernel, mode, first, moment), args, outs, scratch, "step_" + mode, 20_000_000_000)


def blocks_kernel(ids, part, a5, s0, a0, s5, *blocks):
    ring, _ = ring_of(ids)
    first, offset = ids[2] >> 6, ids[2] & 63
    within = lax.broadcasted_iota(jnp.int32, (TILE, COLS), 0)
    column = lax.broadcasted_iota(jnp.int32, (TILE, COLS), 1) + offset
    picks = [jnp.where(within + ((ring + s - first) & 3) * TILE == column, 1.0, 0.0) for s in range(4)]
    pick = jnp.concatenate(picks, axis=0).astype(BF16)
    for r in range(ROWS):
        total = part[r] + a5[r] * s0[r] + a0[r] * s5[r]
        high, low = halves(total)
        placed = jnp.dot(pick, high, preferred_element_type=F32) + jnp.dot(
            pick, low, preferred_element_type=F32
        )
        for s in range(4):
            blocks[s if r < SPLIT else 4 + s][r if r < SPLIT else r - SPLIT] = placed[s * TILE : (s + 1) * TILE]


def combine_kernel(ids, b0, b1, b2, b3, keep, give):
    flags = [jnp.where(serves_upper(ids[i], ids), 1.0, 0.0).astype(F32) for i in (2, 4, 5, 6)]
    for r in range(keep.shape[0]):
        kept = flags[0] * b0[r]
        total = b0[r]
        for flag, block in zip(flags[1:], (b1, b2, b3)):
            kept += flag * block[r]
            total += block[r]
        keep[r] = kept
        gave = (1.0 - flags[0]) * b0[r]
        for flag, block in zip(flags[1:], (b1, b2, b3)):
            gave += (1.0 - flag) * block[r]
        give[r] = gave


def shards(
    forward_prev,
    forward_now,
    adjoint_prev,
    adjoint_now,
    velocity,
    density,
    anchors,
    shot_cell,
    wavelet,
    records,
):
    tables = weight_tables()
    place = lax.axis_index("apert")
    shot = lax.axis_index("shot")
    count = lax.axis_size("apert")
    groups = lax.axis_size("shot")
    half = groups // 2
    ids = jnp.stack([place, shot]).astype(jnp.int32)
    core_pairs = [(i, i ^ 1) for i in range(count)]
    cross_pairs = [(i, i + 1) for i in range(1, count - 1, 2)] + [(i + 1, i) for i in range(1, count - 1, 2)]
    side_pairs = [(i, (i + half) % groups) for i in range(groups)]

    def ring_pairs(shift):
        return [(i, (i // half) * half + (i % half + shift) % half) for i in range(groups)]

    def swap(core, cross):
        return lax.ppermute(core, "apert", core_pairs), lax.ppermute(cross, "apert", cross_pairs)

    def ring_direct(pieces):
        return [pieces[0]] + [lax.ppermute(pieces[k], "shot", ring_pairs(k)) for k in (1, 2, 3)]

    starts = [lax.ppermute(anchors, "shot", ring_pairs(k)) for k in range(1, half)]
    other_dens = lax.ppermute(density, "shot", side_pairs)
    other_vel = lax.ppermute(velocity, "shot", side_pairs)
    base = jnp.concatenate([ids, anchors, shot_cell])
    tile = ((ROWS, TILE, DEPTH), BF16)
    fwd_prev, fwd_now, bwd_prev, bwd_now = forward_prev[0], forward_now[0], adjoint_prev[0], adjoint_now[0]
    first_core, first_cross, own_fwd, own_bwd, dens, vel = call(
        faces_kernel,
        [base, fwd_now, bwd_now, density, velocity],
        [((2,) + FACE, F32), ((2, 5, COLS, DEPTH), BF16), (FACE, F32), (FACE, F32), tile, tile],
        name="faces",
    )
    *picked, nums = call(
        select_kernel,
        [base, *starts, dens, vel, other_dens, other_vel],
        [tile] * (2 * half) + [((7,), jnp.int32)],
        name="select",
        flops=20_000_000_000,
    )
    first_cross, *picked = lax.optimization_barrier((first_cross, *picked))
    first_cross = lax.ppermute(first_cross, "apert", cross_pairs)
    dens_tiles = ring_direct(picked[:half])
    later = lax.optimization_barrier((dens_tiles[1], dens_tiles[3], *picked[half:]))
    dens_tiles[1], dens_tiles[3] = later[:2]
    vel_tiles = ring_direct(later[2:])
    lane = lax.broadcasted_iota(jnp.int32, (1, 1, 1, 128), 3)
    planes = jnp.where(lane == SURF, records[0][..., None], 0.0)
    first_core = lax.ppermute(first_core, "apert", core_pairs)
    first_core, first_cross, planes, *dens_tiles = lax.optimization_barrier(
        (first_core, first_cross, planes, *dens_tiles)
    )

    wide = [pltpu.VMEM((ROWS, 4 * TILE, DEPTH), BF16)]
    dens, dens_cross = call(
        window_dens_kernel,
        [nums, *dens_tiles],
        [(SLAB, F32), (FACE, BF16)],
        wide,
        "window_dens",
        20_000_000_000,
    )
    dens_cross = lax.ppermute(dens_cross, "apert", cross_pairs)
    coef, slope1, slope2, logs, dens_core = call(
        coef_kernel, [nums, *vel_tiles, dens, *tables], [(SLAB, F32)] * 4 + [(FACE, BF16)], wide, "coef", 20_000_000_000
    )
    dens_core = lax.ppermute(dens_core, "apert", core_pairs)
    (slope0,) = call(
        row_slope_kernel,
        [nums, logs, dens_core, dens_cross, coef],
        [(SLAB, F32)],
        [pltpu.VMEM((8, COLS, DEPTH), F32)],
        "row_slope",
    )
    fields = (coef, slope0, slope1, slope2)
    source = wavelet[0]

    fwd_core = bwd_core = first_core
    fwd_cross = bwd_cross = first_cross
    fwd_quant, bwd_quant = (own_fwd,), (own_bwd,)
    snapshots, states = [], []
    for moment in range(STEPS):
        last = moment == STEPS - 1
        if moment > 0:
            fwd_core, fwd_cross = swap(fwd_core, fwd_cross)
        new, *sent = step(
            "fwd", moment, nums, source, fwd_prev, fwd_now, fwd_core, fwd_cross, fwd_quant, None, fields, tables
        )
        if not last:
            own = own_fwd if moment == 0 else fwd_quant[2]
            fwd_core, fwd_cross, seen, shown = sent
            fwd_quant = (seen, seen if moment == 0 else fwd_quant[0], shown, own)
        snapshots.append(new)
        fwd_prev, fwd_now = fwd_now, new

        if moment > 0:
            bwd_core, bwd_cross = swap(bwd_core, bwd_cross)
        new, *sent = step(
            "bwd", moment, nums, source, bwd_prev, bwd_now, bwd_core, bwd_cross, bwd_quant, planes, fields, tables
        )
        if not last:
            own = own_bwd if moment == 0 else bwd_quant[2]
            bwd_core, bwd_cross, seen, shown = sent
            bwd_quant = (seen, seen if moment == 0 else bwd_quant[0], shown, own)
        states.append(new)
        bwd_prev, bwd_now = bwd_now, new
    part = sum(states[t] * snapshots[STEPS - 1 - t] for t in range(1, STEPS - 1))

    head, rest = ((SPLIT, TILE, DEPTH), F32), ((ROWS - SPLIT, TILE, DEPTH), F32)
    blocks = call(
        blocks_kernel,
        [nums, part, states[STEPS - 1], snapshots[0], states[0], snapshots[STEPS - 1]],
        [head] * half + [rest] * half,
        name="blocks",
    )
    arrived = [ring_direct(blocks[:half]), ring_direct(blocks[half:])]
    rows = []
    for each, block in zip(arrived, (head, rest)):
        keep, give = call(combine_kernel, [nums, *each], [block] * 2, name="combine")
        rows.append(keep + lax.ppermute(give, "shot", side_pairs))
    image = jnp.concatenate(rows, axis=0)
    return image, states[STEPS - 1][None]


def solution(mesh):
    placed = (
        P("shot", "apert", None, None),
        P("shot", "apert", None, None),
        P("shot", "apert", None, None),
        P("shot", "apert", None, None),
        P("apert", "shot", None),
        P("apert", "shot", None),
        P("shot"),
        P("shot"),
        P("shot", None),
        P("shot", None, "apert", None),
    )
    return jax.shard_map(
        shards,
        mesh=mesh,
        in_specs=placed,
        out_specs=(P("apert", "shot", None), P("shot", "apert", None, None)),
        check_vma=False,
    )
```
